32 devices in a mesh: bucket: 8 (over y, x, core), span: 4 (over z).
Axes of the slice: x: 2, y: 2, z: 4, core: 2. Of those that a mesh axis runs over, the one named last changes fastest.
Arguments:
- source_table: float32 [8192, 400], P('bucket'), may hold values from -6 to 6
- target_table: float32 [8192, 400], P('bucket'), may hold values from -6 to 6
- source_state: float32 [8192], P('bucket'), may hold values from 0.001 to 0.03
- target_state: float32 [8192], P('bucket'), may hold values from 0.001 to 0.03
- relation: float32 [16, 400], replicated, may hold values from -3 to 3
- relation_state: float32 [16], replicated, may hold values from 10 to 1000
- plan: int32 [8], replicated, may hold values from 0 to 7, each once
- source_index: int32 [8, 10240], P('bucket', 'span'), may hold values from 0 to 1023
- target_index: int32 [8, 10240], P('bucket', 'span'), may hold values from 0 to 1023
- relation_index: int32 [8, 10240], P('bucket', 'span'), may hold values from 0 to 15
- edge_counts: int32 [8], P('bucket'), may hold values from 1280 to 10240, as said below
Outputs:
- new_source: float32 [8192, 400], P('bucket')
- new_target: float32 [8192, 400], P('bucket')
- new_relation: float32 [16, 400], replicated
The draws below stay inside these ranges and needn't reach their ends.
Inputs may be any that keep to these rules, and one draw needn't show every extreme that they name: `plan`: each partition index appears once. `edge_counts`: one bucket has exactly 10240 live slots and another exactly 1280.
All inputs are finite; a program needn't handle non-finite values.
Results may differ from the reference program's by a relative error of at most 0.0028.
The reference program's roundings to bfloat16 on the way count: a program that leaves them out, or rounds other values in their place, can miss the bound.
Values may be sent and summed in bfloat16 or wider, within the bound.
No kernel may reach another device: no remote copies, remote signals or barrier semaphores. Data moves between devices by JAX's collectives and lax.ppermute only.
A program may use at most 64 MiB of HBM per device.

```python
import math
import jax
import jax.numpy as jnp
import numpy as np
from jax import lax

D = 400
ROWS = 1024
E_CH = 640
REL = 16
BUCKETS = 8
EDGES_B = 10240
TABLE = 8192


def scaled_field(key, table_rows, feature_width):
    key_col, key_row, key_base = jax.random.split(key, 3)
    column_scale = jnp.exp(jax.random.uniform(key_col, (1, feature_width), jnp.float32, -1.15, 1.15))
    row_scale = jnp.exp(jax.random.uniform(key_row, (table_rows, 1), jnp.float32, -1.15, 1.15))
    base_values = jnp.clip(jax.random.normal(key_base, (table_rows, feature_width), jnp.float32), -4.0, 4.0)
    return 0.14 * base_values * row_scale * column_scale


def draw_source_table(key, part):
    return scaled_field(jax.random.fold_in(key, 11), BUCKETS * ROWS, D)


def draw_target_table(key, part):
    return scaled_field(jax.random.fold_in(key, 12), BUCKETS * ROWS, D)


def draw_edge_counts(key, part):
    key_counts, key_first, key_second = jax.random.split(jax.random.fold_in(key, 13), 3)
    counts = jax.random.randint(key_counts, (BUCKETS,), EDGES_B // 8, EDGES_B + 1)
    first_bucket = jax.random.randint(key_first, (), 0, BUCKETS)
    second_bucket = (first_bucket + jax.random.randint(key_second, (), 1, BUCKETS)) % BUCKETS
    counts = counts.at[first_bucket].set(EDGES_B).at[second_bucket].set(EDGES_B // 8)
    return counts.astype(jnp.int32)


def with_ends(array, stream_key, least, high):
    longest = array.shape.index(max(array.shape))
    spots = []
    for shift in (0, 1):
        where = [jax.random.randint(jax.random.fold_in(stream_key, axis), (), 0, length) for axis, length in enumerate(array.shape)]
        where[longest] = (where[longest] + shift) % array.shape[longest]
        spots.append(tuple(where))
    return array.at[spots[0]].set(least).at[spots[1]].set(high)


def levels(stream_key, shape, cuts, smallest, high):
    def one(position, blocks):
        draws = jax.random.uniform(jax.random.fold_in(jax.random.fold_in(stream_key, 6), position), (blocks,), jnp.float32, smallest / len(cuts), high / len(cuts))
        return jnp.repeat(jnp.exp(draws), shape[position] // blocks).reshape((-1,) + (1,) * (len(shape) - position - 1))

    level = one(*cuts[0])
    for cut in cuts[1:]:
        level = level * one(*cut)
    return level


def rank_table(amount, slope):
    loads = [(1 << 20) // math.isqrt(standing ** slope) + 1 for standing in range(1, amount + 1)]
    deviation = 1 + sum(loads) // (1 << 30)
    return np.cumsum(np.array([max(1, weight // deviation) for weight in loads]))


def ranked(stream_key, shape, amount, slope):
    listing = rank_table(amount, slope)
    ticket = jax.random.randint(jax.random.fold_in(stream_key, 1), shape, 0, int(listing[amount - 1]))
    rank = jnp.searchsorted(jnp.asarray(listing, jnp.int32), ticket, side="right")
    return jax.random.permutation(jax.random.fold_in(stream_key, 2), amount)[rank].astype(jnp.int32)


def normal_values(stream_key, extent, spread, most, held_as=jnp.bfloat16):
    return jnp.clip(spread * jax.random.normal(stream_key, extent, jnp.float32), -most, most).astype(held_as)


def setup_inputs(seed: int = 0) -> dict:
    keys = jax.random.split(jax.random.key(seed), 12)
    return {
        "source_table": draw_source_table(jax.random.fold_in(keys[11], 71), 0),
        "target_table": draw_target_table(jax.random.fold_in(keys[11], 71), 0),
        "source_state": jnp.clip(jnp.exp(math.log(0.03) - 3.4011973 * jax.random.uniform(keys[2], (TABLE,), jnp.float32) ** levels(keys[2], (TABLE,), ((0, 8),), -0.2, 0.2)), 0.001, 0.03),
        "target_state": jnp.clip(jnp.exp(math.log(0.03) - 3.4011973 * jax.random.uniform(keys[3], (TABLE,), jnp.float32) ** levels(keys[3], (TABLE,), ((0, 8),), -0.2, 0.2)), 0.001, 0.03),
        "relation": normal_values(keys[4], (REL, D), 0.5, 3.0, jnp.float32),
        "relation_state": jnp.clip(jnp.exp(jax.random.uniform(keys[5], (REL,), jnp.float32, math.log(10.0), math.log(1000.0))), 10.0, 1000.0),
        "plan": jax.random.permutation(keys[6], BUCKETS).astype(jnp.int32),
        "source_index": with_ends(ranked(keys[7], (BUCKETS, EDGES_B), ROWS, 1), jax.random.fold_in(keys[7], 3), 0, ROWS - 1).astype(jnp.int32),
        "target_index": with_ends(ranked(keys[8], (BUCKETS, EDGES_B), ROWS, 1), jax.random.fold_in(keys[8], 3), 0, ROWS - 1).astype(jnp.int32),
        "relation_index": with_ends(ranked(keys[9], (BUCKETS, EDGES_B), REL, 2), jax.random.fold_in(keys[9], 3), 0, REL - 1).astype(jnp.int32),
        "edge_counts": draw_edge_counts(jax.random.fold_in(keys[11], 71), 0),
    }


LEARN_RATE = 0.25
NEG_WEIGHT = 0.03125

def span_terms(head_rows, relation_rows, tail_rows, live_mask):
    half_width = head_rows.shape[1] // 2
    head_float = head_rows.astype(jnp.float32)
    head_real = head_float[:, :half_width]
    head_imag = head_float[:, half_width:]
    rel_real = relation_rows[:, :half_width]
    rel_imag = relation_rows[:, half_width:]
    query_rows = jnp.concatenate([head_real * rel_real - head_imag * rel_imag, head_real * rel_imag + head_imag * rel_real], axis=1).astype(jnp.bfloat16)
    scores = lax.dot_general(query_rows, tail_rows, (((1,), (1,)), ((), ())), preferred_element_type=jnp.float32)
    diagonal = lax.broadcasted_iota(jnp.int32, scores.shape, 0) == lax.broadcasted_iota(jnp.int32, scores.shape, 1)
    weights = jnp.where(diagonal, -jax.nn.sigmoid(-scores), NEG_WEIGHT * jax.nn.sigmoid(scores))
    coefficients = (weights * live_mask[:, None] * live_mask[None, :]).astype(jnp.bfloat16)
    grad_query = jnp.dot(coefficients, tail_rows, preferred_element_type=jnp.float32)
    grad_tail = lax.dot_general(coefficients, query_rows, (((0,), (0,)), ((), ())), preferred_element_type=jnp.float32)
    query_real = grad_query[:, :half_width]
    query_imag = grad_query[:, half_width:]
    grad_head = jnp.concatenate([query_real * rel_real + query_imag * rel_imag, query_imag * rel_real - query_real * rel_imag], axis=1)
    grad_relation = jnp.concatenate([query_real * head_real + query_imag * head_imag, query_imag * head_real - query_real * head_imag], axis=1)
    return (grad_head, grad_relation, grad_tail)

def row_adagrad(weights, accumulated, gradient):
    summed = accumulated + lax.optimization_barrier(jnp.mean(gradient * gradient, axis=1))
    return weights - LEARN_RATE * gradient / jnp.sqrt(summed)[:, None]

def reference(source_table, target_table, source_state, target_state, relation, relation_state, plan, source_index, target_index, relation_index, edge_counts):
    source_low = source_table.astype(jnp.bfloat16)
    target_low = target_table.astype(jnp.bfloat16)
    span_total = EDGES_B // E_CH
    relation_iota = jnp.arange(REL, dtype=jnp.int32)

    def one_bucket(relation_grad, bucket):
        source_block = lax.dynamic_slice_in_dim(source_low, (bucket * ROWS).astype(jnp.int32), ROWS, 0)
        partner = plan[bucket]
        target_block = lax.dynamic_slice_in_dim(target_low, (partner * ROWS).astype(jnp.int32), ROWS, 0)
        live_limit = edge_counts[bucket]
        head_table = source_index[bucket].reshape(span_total, E_CH)
        tail_table = target_index[bucket].reshape(span_total, E_CH)
        kind_table = relation_index[bucket].reshape(span_total, E_CH)

        def one_span(carried, span_slot):

            def compute(values):
                source_grad, target_grad, rel_grad = values
                slots = span_slot * E_CH + jnp.arange(E_CH, dtype=jnp.int32)
                live_mask = (slots < live_limit).astype(jnp.float32)
                head_ids = lax.dynamic_index_in_dim(head_table, span_slot, 0, keepdims=False)
                tail_ids = lax.dynamic_index_in_dim(tail_table, span_slot, 0, keepdims=False)
                kind_ids = lax.dynamic_index_in_dim(kind_table, span_slot, 0, keepdims=False)
                one_hot = (kind_ids[:, None] == relation_iota[None, :]).astype(jnp.float32)
                relation_rows = jnp.dot(one_hot, relation, precision=lax.Precision.HIGHEST)
                head_rows = jnp.take(source_block, head_ids, axis=0)
                tail_rows = jnp.take(target_block, tail_ids, axis=0)
                grad_head, grad_relation, grad_tail = span_terms(head_rows, relation_rows, tail_rows, live_mask)
                rel_add = lax.dot_general(one_hot, grad_relation, (((0,), (0,)), ((), ())), precision=lax.Precision.HIGHEST)
                return (source_grad.at[head_ids].add(grad_head), target_grad.at[tail_ids].add(grad_tail), rel_grad + rel_add)

            def keep_values(values):
                return values
            result = lax.cond(span_slot * E_CH < live_limit, compute, keep_values, carried)
            return (result, None)
        start_values = (jnp.zeros((ROWS, D), jnp.float32), jnp.zeros((ROWS, D), jnp.float32), relation_grad)
        final_values, unused = lax.scan(one_span, start_values, jnp.arange(span_total, dtype=jnp.int32))
        return (final_values[2], (final_values[0], final_values[1]))
    relation_grad, grads = lax.scan(one_bucket, jnp.zeros((REL, D), jnp.float32), jnp.arange(BUCKETS, dtype=jnp.int32))
    source_grad = grads[0].reshape(BUCKETS * ROWS, D)
    inverse = jnp.zeros((BUCKETS,), jnp.int32).at[plan].set(jnp.arange(BUCKETS, dtype=jnp.int32))
    target_grad = jnp.take(grads[1], inverse, axis=0).reshape(BUCKETS * ROWS, D)
    new_source = row_adagrad(source_table, source_state, source_grad)
    new_target = row_adagrad(target_table, target_state, target_grad)
    new_relation = row_adagrad(relation, relation_state, relation_grad)
    return (new_source, new_target, new_relation)
```

```python
import functools

import jax
import jax.numpy as jnp
from jax import lax
from jax.experimental import pallas as pl
from jax.experimental.pallas import tpu as pltpu
from jax.sharding import PartitionSpec as P

E_CH = 640
LEARN_RATE = 0.25
NEG_WEIGHT = 0.03125

F32 = jnp.float32
BF16 = jnp.bfloat16
VMEM_BYTES = 56 * 1024 * 1024
SMEM_SPEC = pl.BlockSpec(memory_space=pltpu.SMEM)


def params():
    return pltpu.CompilerParams(vmem_limit_bytes=VMEM_BYTES)


def dot_nn(a, b):
    return lax.dot_general(a, b, (((1,), (0,)), ((), ())), preferred_element_type=F32)


def dot_nt(a, b):
    return lax.dot_general(a, b, (((1,), (1,)), ((), ())), preferred_element_type=F32)


def dot_tn(a, b):
    return lax.dot_general(a, b, (((0,), (0,)), ((), ())), preferred_element_type=F32)


def live_ids(ids, meta_ref, step, steps):
    width = ids.shape[1]
    start = (meta_ref[1] * steps + step) * width
    slots = start + lax.broadcasted_iota(jnp.int32, ids.shape, 1)
    return jnp.where(slots < meta_ref[0], ids, -1)


def is_live(meta_ref, step, steps, width):
    return (meta_ref[1] * steps + step) * width < meta_ref[0]


def one_hot(ids, rows):
    match = lax.broadcasted_iota(jnp.int32, (rows, ids.shape[1]), 0) == ids
    return jnp.where(match, 1.0, 0.0).astype(BF16)


def relation_columns(rel_ref, kind):
    rel = rel_ref[...]
    high = rel.astype(BF16)
    rest = rel - high.astype(F32)
    middle = rest.astype(BF16)
    low = (rest - middle.astype(F32)).astype(BF16)
    parts = jnp.concatenate([high.astype(F32), middle.astype(F32), low.astype(F32)], axis=0)
    hot = jnp.concatenate([kind, kind, kind], axis=0)
    return dot_tn(parts.astype(BF16), hot.astype(BF16))


def kind_hot(ids, count):
    match = lax.broadcasted_iota(jnp.int32, (count, ids.shape[1]), 0) == ids
    return jnp.where(match, 1.0, 0.0)


def prep_kernel(steps, meta_ref, hid_ref, rid_ref, src_ref, rel_ref, q_ref, head_ref, low_ref):
    step = pl.program_id(0)

    @pl.when(step == 0)
    def _():
        low_ref[...] = src_ref[...].astype(BF16)

    @pl.when(is_live(meta_ref, step, steps, hid_ref.shape[2]))
    def _():
        ids = live_ids(hid_ref[0], meta_ref, step, steps)
        kinds = live_ids(rid_ref[0], meta_ref, step, steps)
        head = dot_nn(low_ref[...], one_hot(ids, low_ref.shape[1]))
        rel = relation_columns(rel_ref, kind_hot(kinds, rel_ref.shape[0]))
        half = head.shape[0] // 2
        h_re, h_im, r_re, r_im = head[:half], head[half:], rel[:half], rel[half:]
        query = jnp.concatenate([h_re * r_re - h_im * r_im, h_re * r_im + h_im * r_re], axis=0)
        q_ref[0] = query.astype(BF16)
        head_ref[0] = head.astype(BF16)


def assemble(lane, parts, out_ref):
    total = len(parts)
    pieces, block, width = parts[0].shape
    for at in range(total):

        @pl.when(lane == at)
        def _():
            for k in range(total):
                row = ((at - k) % total) * block
                for b in range(pieces):
                    out_ref[row : row + block, b * width : (b + 1) * width] = parts[k][b].astype(F32)


def emit(lane, acc_ref, outs):
    total = len(outs)
    pieces, block, width = outs[0].shape
    for at in range(total):

        @pl.when(lane == at)
        def _():
            for k in range(total):
                row = ((at + k) % total) * block
                for b in range(pieces):
                    outs[k][b] = acc_ref[row : row + block, b * width : (b + 1) * width].astype(
                        outs[k].dtype
                    )


def target_kernel(steps, lanes, meta_ref, tid_ref, q_ref, *refs):
    parts = refs[:lanes]
    tail_ref, coef_ref = refs[lanes : lanes + 2]
    outs = refs[lanes + 2 : 2 * lanes + 2]
    wide_ref, table_ref, acc_ref, hot_ref = refs[2 * lanes + 2 :]
    step = pl.program_id(0)

    @pl.when(step == 0)
    def _():
        assemble(meta_ref[1], parts, wide_ref)
        table_ref[...] = wide_ref[...].astype(BF16)
        acc_ref[...] = jnp.zeros_like(acc_ref)

    @pl.when(is_live(meta_ref, step, steps, tid_ref.shape[2]))
    def _():
        ids = live_ids(tid_ref[0], meta_ref, step, steps)
        hot_ref[...] = one_hot(ids, table_ref.shape[1])
        tail = dot_nn(table_ref[...], hot_ref[...]).astype(BF16)
        tail_ref[0] = tail
        scores = dot_tn(q_ref[0], tail)
        sig = 0.5 * jnp.tanh(0.5 * scores) + 0.5
        diagonal = lax.broadcasted_iota(jnp.int32, scores.shape, 0) == lax.broadcasted_iota(
            jnp.int32, scores.shape, 1
        )
        coef_ref[0] = jnp.where(diagonal, sig - 1.0, NEG_WEIGHT * sig).astype(BF16)
        grad_tail = dot_nn(q_ref[0], coef_ref[0])
        acc_ref[...] += dot_nt(grad_tail.astype(BF16), hot_ref[...])

    @pl.when(step == steps - 1)
    def _():
        emit(meta_ref[1], acc_ref, outs)


def source_kernel(steps, lanes, meta_ref, hid_ref, rid_ref, rel_ref, head_ref, tail_ref, coef_ref, *refs):
    outs = refs[:lanes]
    rel_out_ref, acc_ref = refs[lanes:]
    step = pl.program_id(0)

    @pl.when(step == 0)
    def _():
        acc_ref[...] = jnp.zeros_like(acc_ref)
        rel_out_ref[...] = jnp.zeros_like(rel_out_ref)

    @pl.when(is_live(meta_ref, step, steps, hid_ref.shape[2]))
    def _():
        ids = live_ids(hid_ref[0], meta_ref, step, steps)
        kinds = live_ids(rid_ref[0], meta_ref, step, steps)
        kind = kind_hot(kinds, rel_ref.shape[0])
        rel = relation_columns(rel_ref, kind)
        head = head_ref[0].astype(F32)
        half = head.shape[0] // 2
        h_re, h_im, r_re, r_im = head[:half], head[half:], rel[:half], rel[half:]
        grad_query = dot_nt(tail_ref[0], coef_ref[0])
        g_re, g_im = grad_query[:half], grad_query[half:]
        grad_head = jnp.concatenate([g_re * r_re + g_im * r_im, g_im * r_re - g_re * r_im], axis=0)
        acc_ref[...] += dot_nt(grad_head.astype(BF16), one_hot(ids, acc_ref.shape[1]))
        grad_rel = jnp.concatenate([g_re * h_re + g_im * h_im, g_im * h_re - g_re * h_im], axis=0)
        high = grad_rel.astype(BF16)
        low = (grad_rel - high.astype(F32)).astype(BF16)
        kind = kind.astype(BF16)
        rel_out_ref[...] += dot_nt(kind, high) + dot_nt(kind, low)

    @pl.when(step == steps - 1)
    def _():
        emit(meta_ref[1], acc_ref, outs)


def sum_kernel(*refs):
    total = refs[0][...]
    for ref in refs[1:-1]:
        total = total + ref[...].astype(F32)
    refs[-1][...] = total.astype(BF16)


def pick_kernel(plan_ref, in_ref, out_ref):
    for b in range(in_ref.shape[0]):
        out_ref[b] = in_ref[plan_ref[b]]


def place_kernel(plan_ref, in_ref, out_ref):
    for b in range(in_ref.shape[0]):
        out_ref[plan_ref[b]] = in_ref[b]


def update_kernel(lanes, meta_ref, table_ref, state_ref, *refs):
    parts = refs[:lanes]
    out_ref, grad_ref = refs[lanes:]
    assemble(meta_ref[1], parts, grad_ref)
    grad = grad_ref[...]
    mean = jnp.sum(grad * grad, axis=0, keepdims=True) / grad.shape[0]
    scale = LEARN_RATE / jnp.sqrt(state_ref[...] + mean)
    out_ref[...] = table_ref[...] - grad * scale


def whole(shape):
    zeros = (0,) * len(shape)
    return pl.BlockSpec(tuple(shape), lambda i: zeros)


def per_span(shape):
    rest = (0,) * (len(shape) - 1)
    return pl.BlockSpec((1,) + tuple(shape[1:]), lambda i: (i,) + rest)


def shift_span(x, by):
    count = lax.axis_size("span")
    return lax.ppermute(x, "span", [(i, (i + by) % count) for i in range(count)])


def plain(kernel, out, *operands, smem=1):
    vmem = pl.BlockSpec(memory_space=pltpu.VMEM)
    return pl.pallas_call(
        kernel,
        out_shape=out,
        in_specs=[SMEM_SPEC] * smem + [vmem] * (len(operands) - smem),
        out_specs=vmem,
        compiler_params=params(),
    )(*operands)


def swap_buckets(x):
    return lax.all_to_all(x, "bucket", split_axis=0, concat_axis=0, tiled=True)


def update(meta, table, state, parts):
    lanes = len(parts)
    vmem = pl.BlockSpec(memory_space=pltpu.VMEM)
    return pl.pallas_call(
        functools.partial(update_kernel, lanes),
        out_shape=jax.ShapeDtypeStruct(table.shape, F32),
        in_specs=[SMEM_SPEC] + [vmem] * (lanes + 2),
        out_specs=vmem,
        scratch_shapes=[pltpu.VMEM(table.shape, F32)],
        compiler_params=params(),
    )(meta, table, state, *parts)


def sum_all(x):
    for axis in ("span", "bucket"):
        count = lax.axis_size(axis)
        if count & (count - 1):
            x = lax.psum(x, axis)
            continue
        bit = 1
        while bit < count:
            x = x + lax.ppermute(x, axis, [(i, i ^ bit) for i in range(count)])
            bit *= 2
    return x


def per_device(
    source_table,
    target_table,
    source_state,
    target_state,
    relation,
    relation_state,
    plan,
    source_index,
    target_index,
    relation_index,
    edge_counts,
):
    buckets = lax.axis_size("bucket")
    lanes = lax.axis_size("span")
    lane = lax.axis_index("span").astype(jnp.int32)
    rows, features = source_table.shape
    steps = source_index.shape[1] // E_CH
    kinds = relation.shape[0]
    block = features // lanes
    width = rows // buckets
    meta = jnp.stack([edge_counts[0], lane])
    hid = source_index.reshape(steps, 1, E_CH)
    tid = target_index.reshape(steps, 1, E_CH)
    rid = relation_index.reshape(steps, 1, E_CH)
    source_cols, target_cols = source_table.T, target_table.T

    own = lax.dynamic_slice_in_dim(target_cols, lane * block, block, 0).astype(BF16)
    pieces = own.reshape(block, buckets, width).transpose(1, 0, 2)
    piece_shape = jax.ShapeDtypeStruct(pieces.shape, BF16)
    spread = swap_buckets(pieces)
    chosen = plain(pick_kernel, piece_shape, plan, spread)
    fetched = swap_buckets(chosen)
    target_parts = [fetched] + [shift_span(fetched, k) for k in range(1, lanes)]

    edge_shape = (steps, features, E_CH)
    query, head = pl.pallas_call(
        functools.partial(prep_kernel, steps),
        grid=(steps,),
        out_shape=[jax.ShapeDtypeStruct(edge_shape, BF16)] * 2,
        in_specs=[
            SMEM_SPEC,
            per_span(hid.shape),
            per_span(rid.shape),
            whole(source_cols.shape),
            whole(relation.shape),
        ],
        out_specs=[per_span(edge_shape)] * 2,
        scratch_shapes=[pltpu.VMEM((features, rows), BF16)],
        compiler_params=params(),
    )(meta, hid, rid, source_cols, relation)

    out_pieces = [jax.ShapeDtypeStruct(pieces.shape, F32)] + [piece_shape] * (lanes - 1)
    coef_shape = (steps, E_CH, E_CH)
    tail, coef, *target_out = pl.pallas_call(
        functools.partial(target_kernel, steps, lanes),
        grid=(steps,),
        out_shape=[jax.ShapeDtypeStruct(edge_shape, BF16), jax.ShapeDtypeStruct(coef_shape, BF16)]
        + out_pieces,
        in_specs=[SMEM_SPEC, per_span(tid.shape), per_span(edge_shape)]
        + [whole(pieces.shape)] * lanes,
        out_specs=[per_span(edge_shape), per_span(coef_shape)] + [whole(pieces.shape)] * lanes,
        scratch_shapes=[
            pltpu.VMEM((features, rows), F32),
            pltpu.VMEM((features, rows), BF16),
            pltpu.VMEM((features, rows), F32),
            pltpu.VMEM((rows, E_CH), BF16),
        ],
        compiler_params=params(),
    )(meta, tid, query, *target_parts)

    target_in = [shift_span(target_out[k], k) for k in range(1, lanes)]
    *source_out, rel_part = pl.pallas_call(
        functools.partial(source_kernel, steps, lanes),
        grid=(steps,),
        out_shape=out_pieces + [jax.ShapeDtypeStruct(relation.shape, F32)],
        in_specs=[
            SMEM_SPEC,
            per_span(hid.shape),
            per_span(rid.shape),
            whole(relation.shape),
            per_span(edge_shape),
            per_span(edge_shape),
            per_span(coef_shape),
        ],
        out_specs=[whole(pieces.shape)] * lanes + [whole(relation.shape)],
        scratch_shapes=[pltpu.VMEM((features, rows), F32)],
        compiler_params=params(),
    )(meta, hid, rid, relation, head, tail, coef)

    target_sum = plain(sum_kernel, piece_shape, target_out[0], *target_in, smem=0)
    returned = swap_buckets(target_sum)
    sorted_out = plain(place_kernel, piece_shape, plan, returned)
    target_home = swap_buckets(sorted_out)
    source_in = [shift_span(source_out[k], k) for k in range(1, lanes)]
    source_sum = plain(sum_kernel, piece_shape, source_out[0], *source_in, smem=0)
    source_parts = [source_sum] + [shift_span(source_sum, k) for k in range(1, lanes)]
    home_parts = [target_home] + [shift_span(target_home, k) for k in range(1, lanes)]
    new_source = update(meta, source_cols, source_state.reshape(1, rows), source_parts)
    new_target = update(meta, target_cols, target_state.reshape(1, rows), home_parts)

    rel_total = sum_all(rel_part)
    rel_scale = LEARN_RATE / jnp.sqrt(relation_state + jnp.mean(rel_total * rel_total, axis=1))
    new_relation = relation - rel_total * rel_scale[:, None]
    return (new_source.T, new_target.T, new_relation)


def solution(mesh):
    placed = (
        P("bucket", None),
        P("bucket", None),
        P("bucket"),
        P("bucket"),
        P(),
        P(),
        P(),
        P("bucket", "span"),
        P("bucket", "span"),
        P("bucket", "span"),
        P("bucket"),
    )
    return jax.shard_map(
        per_device,
        mesh=mesh,
        in_specs=placed,
        out_specs=(P("bucket", None), P("bucket", None), P()),
        check_vma=False,
    )
```

```python
import functools

import jax
import jax.numpy as jnp
from jax import lax
from jax.experimental import pallas as pl
from jax.experimental.pallas import tpu as pltpu
from jax.sharding import PartitionSpec as P

E_CH = 640
LEARN_RATE = 0.25
NEG_WEIGHT = 0.03125

F32 = jnp.float32
BF16 = jnp.bfloat16
VMEM_BYTES = 56 * 1024 * 1024
SMEM_SPEC = pl.BlockSpec(memory_space=pltpu.SMEM)


def params():
    return pltpu.CompilerParams(vmem_limit_bytes=VMEM_BYTES)


def cost(flops, nbytes):
    return pl.CostEstimate(flops=int(flops), bytes_accessed=int(nbytes), transcendentals=0)


def dot_nn(a, b):
    return lax.dot_general(a, b, (((1,), (0,)), ((), ())), preferred_element_type=F32)


def dot_nt(a, b):
    return lax.dot_general(a, b, (((1,), (1,)), ((), ())), preferred_element_type=F32)


def dot_tn(a, b):
    return lax.dot_general(a, b, (((0,), (0,)), ((), ())), preferred_element_type=F32)


def live_ids(ids, meta_ref, step, steps):
    width = ids.shape[1]
    start = (meta_ref[1] * steps + step) * width
    slots = start + lax.broadcasted_iota(jnp.int32, ids.shape, 1)
    return jnp.where(slots < meta_ref[0], ids, -1)


def is_live(meta_ref, step, steps, width):
    return (meta_ref[1] * steps + step) * width < meta_ref[0]


def one_hot(ids, rows):
    match = lax.broadcasted_iota(jnp.int32, (rows, ids.shape[1]), 0) == ids
    return jnp.where(match, 1.0, 0.0).astype(BF16)


def relation_columns(rel_ref, kind):
    rel = rel_ref[...]
    high = rel.astype(BF16)
    rest = rel - high.astype(F32)
    middle = rest.astype(BF16)
    low = (rest - middle.astype(F32)).astype(BF16)
    parts = jnp.concatenate([high.astype(F32), middle.astype(F32), low.astype(F32)], axis=0)
    hot = jnp.concatenate([kind, kind, kind], axis=0)
    return dot_tn(parts.astype(BF16), hot.astype(BF16))


def kind_hot(ids, count):
    match = lax.broadcasted_iota(jnp.int32, (count, ids.shape[1]), 0) == ids
    return jnp.where(match, 1.0, 0.0)


def prep_kernel(steps, meta_ref, hid_ref, rid_ref, src_ref, rel_ref, q_ref, head_ref, low_ref):
    step = pl.program_id(0)

    @pl.when(step == 0)
    def _():
        low_ref[...] = src_ref[...].astype(BF16)

    @pl.when(is_live(meta_ref, step, steps, hid_ref.shape[2]))
    def _():
        ids = live_ids(hid_ref[0], meta_ref, step, steps)
        kinds = live_ids(rid_ref[0], meta_ref, step, steps)
        head = dot_nn(low_ref[...], one_hot(ids, low_ref.shape[1]))
        rel = relation_columns(rel_ref, kind_hot(kinds, rel_ref.shape[0]))
        half = head.shape[0] // 2
        h_re, h_im, r_re, r_im = head[:half], head[half:], rel[:half], rel[half:]
        query = jnp.concatenate([h_re * r_re - h_im * r_im, h_re * r_im + h_im * r_re], axis=0)
        q_ref[0] = query.astype(BF16)
        head_ref[0] = head.astype(BF16)


def ring_plan(lanes, pieces):
    plan = [(0, 0, pieces)]
    for k in range(1, (lanes + 1) // 2):
        plan += [(k, 0, pieces), (-k, 0, pieces)]
    if lanes % 2 == 0:
        half = pieces // 2
        plan += [(lanes // 2, 0, half), (-(lanes // 2), half, pieces - half)]
    return plan


def add_pieces(total, part, first):
    last, part = first + part.shape[0], part.astype(F32)
    if part.shape == total.shape:
        return total + part
    return jnp.concatenate([total[:first], total[first:last] + part, total[last:]], axis=0)


def ring_sum(parts, waits):
    lanes = lax.axis_size("span")
    if lanes == 1:
        return parts[0].astype(BF16)
    plan = ring_plan(lanes, parts[0].shape[0])
    blocks = {away: part for part, (away, _, _) in zip(parts, plan)}
    reach, first = lanes // 2, plan[-1][1]
    ahead, behind = blocks[reach].astype(BF16), blocks[-reach].astype(BF16)
    for away in range(reach, 0, -1):
        ahead, behind = shift_span(ahead, 1), shift_span(behind, -1)
        for wait in waits[reach - away : reach - away + 1]:
            ahead, behind = after((ahead, behind), wait)
        if away > 1:
            ahead = add_pieces(blocks[away - 1], ahead, 0).astype(BF16)
            behind = add_pieces(blocks[1 - away], behind, first).astype(BF16)
    return add_pieces(add_pieces(parts[0], ahead, 0), behind, first).astype(BF16)


def ring_shapes(shape, lanes):
    return [
        jax.ShapeDtypeStruct((count,) + tuple(shape[1:]), F32 if abs(away) < (lanes + 1) // 2 else BF16)
        for away, first, count in ring_plan(lanes, shape[0])
    ]


def gather_span(x):
    lanes = lax.axis_size("span")
    parts, ahead, behind = [x], x, x
    for _ in range(1, (lanes + 1) // 2):
        ahead, behind = shift_span(ahead, 1), shift_span(behind, -1)
        parts += [ahead, behind]
    if lanes % 2 == 0:
        half = x.shape[0] // 2
        parts += [shift_span(ahead[:half], 1), shift_span(behind[half:], -1)]
    return parts


def assemble(lanes, lane, parts, out_ref):
    width = parts[0].shape[2]
    block = out_ref.shape[0] // lanes
    plan = ring_plan(lanes, parts[0].shape[0])
    for at in range(lanes):

        @pl.when(lane == at)
        def _():
            for part, (behind, first, count) in zip(parts, plan):
                row = ((at - behind) % lanes) * block
                for b in range(count):
                    col = (first + b) * width
                    out_ref[row : row + block, col : col + width] = part[b, :block].astype(F32)


def emit(lanes, lane, acc_ref, outs):
    width = outs[0].shape[2]
    block = acc_ref.shape[0] // lanes
    plan = ring_plan(lanes, outs[0].shape[0])
    for at in range(lanes):

        @pl.when(lane == at)
        def _():
            for out, (away, first, count) in zip(outs, plan):
                row = ((at + away) % lanes) * block
                for b in range(count):
                    col = (first + b) * width
                    out[b, :block] = acc_ref[row : row + block, col : col + width].astype(out.dtype)


def main_kernel(
    steps, lanes, packed, meta_ref, tid_ref, rid_ref, rel_ref, q_ref, head_ref, parts_ref, *refs
):
    grad_ref, rel_out_ref = refs[:2]
    outs = refs[2:-4]
    table_ref, acc_ref, hot_ref, coef_ref = refs[-4:]
    step = pl.program_id(0)

    @pl.when(step == 0)
    def _():
        width = parts_ref.shape[2]
        for b in range(parts_ref.shape[0]):
            table_ref[:, b * width : (b + 1) * width] = parts_ref[b]
        acc_ref[...] = jnp.zeros_like(acc_ref)
        rel_out_ref[...] = jnp.zeros_like(rel_out_ref)

    @pl.when(is_live(meta_ref, step, steps, tid_ref.shape[2]))
    def _():
        ids = live_ids(tid_ref[0], meta_ref, step, steps)
        hot_ref[...] = one_hot(ids, table_ref.shape[1])
        tail = dot_nn(table_ref[...], hot_ref[...]).astype(BF16)
        scores = dot_tn(q_ref[0], tail)
        sig = 0.5 * jnp.tanh(0.5 * scores) + 0.5
        diagonal = lax.broadcasted_iota(jnp.int32, scores.shape, 0) == lax.broadcasted_iota(
            jnp.int32, scores.shape, 1
        )
        coef_ref[...] = jnp.where(diagonal, sig - 1.0, NEG_WEIGHT * sig).astype(BF16)
        grad_tail = dot_nn(q_ref[0], coef_ref[...])
        acc_ref[...] += dot_nt(grad_tail.astype(BF16), hot_ref[...])

        kinds = live_ids(rid_ref[0], meta_ref, step, steps)
        kind = kind_hot(kinds, rel_ref.shape[0])
        rel = relation_columns(rel_ref, kind)
        head = head_ref[0].astype(F32)
        half = head.shape[0] // 2
        h_re, h_im, r_re, r_im = head[:half], head[half:], rel[:half], rel[half:]
        grad_query = dot_nt(tail, coef_ref[...])
        g_re, g_im = grad_query[:half], grad_query[half:]
        grad_head = jnp.concatenate([g_re * r_re + g_im * r_im, g_im * r_re - g_re * r_im], axis=0)
        grad_ref[0] = grad_head.astype(BF16)
        grad_rel = jnp.concatenate([g_re * h_re + g_im * h_im, g_im * h_re - g_re * h_im], axis=0)
        rel_out_ref[...] += dot_nt(grad_rel.astype(BF16), kind.astype(BF16))

    @pl.when(step == steps - 1)
    def _():
        emit(lanes, meta_ref[1], acc_ref, outs)
        if packed:
            rel_rows = rel_out_ref[...].T
            block = rel_rows.shape[1] // lanes
            each = rel_rows.shape[0] // outs[0].shape[0]
            plan = ring_plan(lanes, outs[0].shape[0])
            for at in range(lanes):

                @pl.when(meta_ref[1] == at)
                def _():
                    for out, (away, first, count) in zip(outs, plan):
                        col = ((at + away) % lanes) * block
                        for b in range(count):
                            row = (first + b) * each
                            out[b, block:, :block] = rel_rows[
                                row : row + each, col : col + block
                            ].astype(out.dtype)


def source_kernel(steps, lanes, meta_ref, hid_ref, grad_ref, *refs):
    outs, acc_ref = refs[:-1], refs[-1]
    step = pl.program_id(0)

    @pl.when(step == 0)
    def _():
        acc_ref[...] = jnp.zeros_like(acc_ref)

    @pl.when(is_live(meta_ref, step, steps, hid_ref.shape[2]))
    def _():
        ids = live_ids(hid_ref[0], meta_ref, step, steps)
        acc_ref[...] += dot_nt(grad_ref[0], one_hot(ids, acc_ref.shape[1]))

    @pl.when(step == steps - 1)
    def _():
        emit(lanes, meta_ref[1], acc_ref, outs)


def pick_kernel(plan_ref, in_ref, out_ref):
    for b in range(in_ref.shape[0]):
        out_ref[b] = in_ref[plan_ref[b]]


def place_kernel(block, plan_ref, in_ref, out_ref):
    for b in range(in_ref.shape[0]):
        out_ref[plan_ref[b]] = in_ref[b]
    if in_ref.shape[1] > block:
        total = jnp.sum(in_ref[:, block:].astype(F32), axis=0).astype(BF16)
        for b in range(in_ref.shape[0]):
            out_ref[b, block:] = total


def adagrad(table, state, grad, axis):
    mean = jnp.sum(grad * grad, axis=axis, keepdims=True) / grad.shape[axis]
    return table - grad * (LEARN_RATE / jnp.sqrt(state + mean))


def update_kernel(lanes, meta_ref, table_ref, state_ref, *refs):
    parts, out_ref, grad_ref = refs[:-2], refs[-2], refs[-1]
    assemble(lanes, meta_ref[1], parts, grad_ref)
    out_ref[...] = adagrad(table_ref[...], state_ref[...], grad_ref[...], 0)


def update_both_kernel(lanes, meta_ref, table_ref, state_ref, rel_ref, rel_state_ref, *refs):
    parts = refs[:-4]
    out_ref, rel_out_ref, grad_ref, rel_grad_ref = refs[-4:]
    assemble(lanes, meta_ref[1], parts, grad_ref)
    out_ref[...] = adagrad(table_ref[...], state_ref[...], grad_ref[...], 0)
    block = rel_ref.shape[1] // lanes
    each = parts[0].shape[1] - block
    plan = ring_plan(lanes, parts[0].shape[0])
    for at in range(lanes):

        @pl.when(meta_ref[1] == at)
        def _():
            for part, (behind, first, count) in zip(parts, plan):
                col = ((at - behind) % lanes) * block
                for b in range(count):
                    row = (first + b) * each
                    rel_grad_ref[row : row + each, col : col + block] = part[
                        b, block:, :block
                    ].astype(F32)

    rel_out_ref[...] = adagrad(rel_ref[...], rel_state_ref[...], rel_grad_ref[...], 1)


def whole(shape):
    zeros = (0,) * len(shape)
    return pl.BlockSpec(tuple(shape), lambda i: zeros)


def per_span(shape):
    rest = (0,) * (len(shape) - 1)
    return pl.BlockSpec((1,) + tuple(shape[1:]), lambda i: (i,) + rest)


def shift_span(x, by):
    count = lax.axis_size("span")
    return lax.ppermute(x, "span", [(i, (i + by) % count) for i in range(count)])


def plain(kernel, out, *operands, smem=1):
    vmem = pl.BlockSpec(memory_space=pltpu.VMEM)
    return pl.pallas_call(
        kernel,
        out_shape=out,
        in_specs=[SMEM_SPEC] * smem + [vmem] * (len(operands) - smem),
        out_specs=vmem,
        compiler_params=params(),
    )(*operands)


def swap_buckets(x):
    return lax.all_to_all(x, "bucket", split_axis=0, concat_axis=0, tiled=True)


def after(x, y):
    return lax.optimization_barrier((x, y))[0]


def update(kernel, lanes, meta, weights, parts):
    vmem = pl.BlockSpec(memory_space=pltpu.VMEM)
    tables = weights[::2]
    return pl.pallas_call(
        functools.partial(kernel, lanes),
        out_shape=[jax.ShapeDtypeStruct(t.shape, F32) for t in tables],
        in_specs=[SMEM_SPEC] + [vmem] * (len(weights) + len(parts)),
        out_specs=[vmem] * len(tables),
        scratch_shapes=[pltpu.VMEM(t.shape, F32) for t in tables],
        compiler_params=params(),
    )(meta, *weights, *parts)


def sum_all(x):
    for axis in ("span", "bucket"):
        count = lax.axis_size(axis)
        if count & (count - 1):
            x = lax.psum(x, axis)
            continue
        bit = 1
        while bit < count:
            x = x + lax.ppermute(x, axis, [(i, i ^ bit) for i in range(count)])
            bit *= 2
    return x


def per_device(
    source_table,
    target_table,
    source_state,
    target_state,
    relation,
    relation_state,
    plan,
    source_index,
    target_index,
    relation_index,
    edge_counts,
):
    buckets = lax.axis_size("bucket")
    lanes = lax.axis_size("span")
    lane = lax.axis_index("span").astype(jnp.int32)
    rows, features = source_table.shape
    steps = source_index.shape[1] // E_CH
    kinds = relation.shape[0]
    block = features // lanes
    width = rows // buckets
    meta = jnp.stack([edge_counts[0], lane])
    hid = source_index.reshape(steps, 1, E_CH)
    tid = target_index.reshape(steps, 1, E_CH)
    rid = relation_index.reshape(steps, 1, E_CH)
    source_cols, target_cols = source_table.T, target_table.T

    owned = target_cols.astype(BF16).reshape(features, buckets, width).transpose(1, 0, 2)
    spread = swap_buckets(owned)
    chosen = plain(pick_kernel, jax.ShapeDtypeStruct(owned.shape, BF16), plan, spread)
    fetched = swap_buckets(chosen)
    packed = kinds % buckets == 0 and width >= block
    pieces = (buckets, block, width)
    piece_shape = jax.ShapeDtypeStruct(pieces, BF16)
    bundles = (buckets, block + kinds // buckets, width) if packed else pieces
    bundle_shape = jax.ShapeDtypeStruct(bundles, BF16)

    edge_shape = (steps, features, E_CH)
    query, head = pl.pallas_call(
        functools.partial(prep_kernel, steps),
        grid=(steps,),
        out_shape=[jax.ShapeDtypeStruct(edge_shape, BF16)] * 2,
        in_specs=[
            SMEM_SPEC,
            per_span(hid.shape),
            per_span(rid.shape),
            whole(source_cols.shape),
            whole(relation.shape),
        ],
        out_specs=[per_span(edge_shape)] * 2,
        scratch_shapes=[pltpu.VMEM((features, rows), BF16)],
        compiler_params=params(),
        cost_estimate=cost(4 * steps * features * rows * E_CH, 8 * features * steps * E_CH),
    )(meta, hid, rid, source_cols, relation)

    bundle_outs, piece_outs = ring_shapes(bundles, lanes), ring_shapes(pieces, lanes)
    grad_head, rel_part, *target_out = pl.pallas_call(
        functools.partial(main_kernel, steps, lanes, packed),
        grid=(steps,),
        out_shape=[
            jax.ShapeDtypeStruct(edge_shape, BF16),
            jax.ShapeDtypeStruct((features, kinds), F32),
        ]
        + bundle_outs,
        in_specs=[
            SMEM_SPEC,
            per_span(tid.shape),
            per_span(rid.shape),
            whole(relation.shape),
            per_span(edge_shape),
            per_span(edge_shape),
            whole(owned.shape),
        ],
        out_specs=[per_span(edge_shape), whole((features, kinds))]
        + [whole(out.shape) for out in bundle_outs],
        scratch_shapes=[
            pltpu.VMEM((features, rows), BF16),
            pltpu.VMEM((features, rows), F32),
            pltpu.VMEM((rows, E_CH), BF16),
            pltpu.VMEM((E_CH, E_CH), BF16),
        ],
        compiler_params=params(),
        cost_estimate=cost(12 * steps * features * rows * E_CH, 8 * features * steps * E_CH),
    )(meta, tid, rid, relation, query, head, fetched)

    source_out = pl.pallas_call(
        functools.partial(source_kernel, steps, lanes),
        grid=(steps,),
        out_shape=piece_outs,
        in_specs=[SMEM_SPEC, per_span(hid.shape), per_span(edge_shape)],
        out_specs=[whole(out.shape) for out in piece_outs],
        scratch_shapes=[pltpu.VMEM((features, rows), F32)],
        compiler_params=params(),
        cost_estimate=cost(4 * steps * features * rows * E_CH, 8 * features * steps * E_CH),
    )(meta, hid, grad_head)

    target_sum = ring_sum(target_out, [source_out])
    returned = swap_buckets(target_sum)
    placing = functools.partial(place_kernel, block)
    sorted_out = plain(placing, bundle_shape, plan, returned)
    target_home = swap_buckets(sorted_out)
    source_sum = ring_sum(source_out, [sorted_out])
    source_parts = gather_span(source_sum)
    home_parts = gather_span(target_home)
    source_weights = (source_cols, source_state.reshape(1, rows))
    target_weights = (target_cols, target_state.reshape(1, rows))
    (new_source,) = update(update_kernel, lanes, meta, source_weights, source_parts)
    if packed:
        weights = target_weights + (relation, relation_state.reshape(kinds, 1))
        new_target, new_relation = update(update_both_kernel, lanes, meta, weights, home_parts)
    else:
        (new_target,) = update(update_kernel, lanes, meta, target_weights, home_parts)
        rel_total = sum_all(rel_part).T
        mean = jnp.mean(rel_total * rel_total, axis=1)
        new_relation = relation - LEARN_RATE * rel_total / jnp.sqrt(relation_state + mean)[:, None]
    return (new_source.T, new_target.T, new_relation)


def solution(mesh):
    placed = (
        P("bucket", None),
        P("bucket", None),
        P("bucket"),
        P("bucket"),
        P(),
        P(),
        P(),
        P("bucket", "span"),
        P("bucket", "span"),
        P("bucket", "span"),
        P("bucket"),
    )
    return jax.shard_map(
        per_device,
        mesh=mesh,
        in_specs=placed,
        out_specs=(P("bucket", None), P("bucket", None), P()),
        check_vma=False,
    )
```

```python
import functools

import jax
import jax.numpy as jnp
from jax import lax
from jax.experimental import pallas as pl
from jax.experimental.pallas import tpu as pltpu
from jax.sharding import PartitionSpec as P

E_CH = 640
LEARN_RATE = 0.25
NEG_WEIGHT = 0.03125

F32 = jnp.float32
BF16 = jnp.bfloat16
MIB = 1024 * 1024
SMEM_SPEC = pl.BlockSpec(memory_space=pltpu.SMEM)


ANY_SPEC = pl.BlockSpec(memory_space=pl.ANY)


def params(mib):
    return pltpu.CompilerParams(vmem_limit_bytes=mib * MIB)


def cost(flops, nbytes):
    return pl.CostEstimate(flops=int(flops), bytes_accessed=int(nbytes), transcendentals=0)


def dot_nn(a, b):
    return lax.dot_general(a, b, (((1,), (0,)), ((), ())), preferred_element_type=F32)


def dot_nt(a, b):
    return lax.dot_general(a, b, (((1,), (1,)), ((), ())), preferred_element_type=F32)


def dot_tn(a, b):
    return lax.dot_general(a, b, (((0,), (0,)), ((), ())), preferred_element_type=F32)


def live_ids(ids, meta_ref, step, steps):
    width = ids.shape[1]
    start = (meta_ref[1] * steps + step) * width
    slots = start + lax.broadcasted_iota(jnp.int32, ids.shape, 1)
    return jnp.where(slots < meta_ref[0], ids, -1)


def is_live(meta_ref, step, steps, width):
    return (meta_ref[1] * steps + step) * width < meta_ref[0]


def one_hot(ids, rows):
    match = lax.broadcasted_iota(jnp.int32, (rows, ids.shape[1]), 0) == ids
    return jnp.where(match, 1.0, 0.0).astype(BF16)


def relation_columns(rel_ref, kind):
    rel = rel_ref[...]
    high = rel.astype(BF16)
    rest = rel - high.astype(F32)
    middle = rest.astype(BF16)
    low = (rest - middle.astype(F32)).astype(BF16)
    parts = jnp.concatenate([high.astype(F32), middle.astype(F32), low.astype(F32)], axis=0)
    hot = jnp.concatenate([kind, kind, kind], axis=0)
    return dot_tn(parts.astype(BF16), hot.astype(BF16))


def kind_hot(ids, count):
    match = lax.broadcasted_iota(jnp.int32, (count, ids.shape[1]), 0) == ids
    return jnp.where(match, 1.0, 0.0)


def prep_kernel(steps, meta_ref, hid_ref, rid_ref, src_ref, rel_ref, out_ref, low_ref):
    step = pl.program_id(0)

    @pl.when(step == 0)
    def _():
        low_ref[...] = src_ref[...].astype(BF16)

    @pl.when(is_live(meta_ref, step, steps, hid_ref.shape[2]))
    def _():
        ids = live_ids(hid_ref[0], meta_ref, step, steps)
        kinds = live_ids(rid_ref[0], meta_ref, step, steps)
        head = dot_nn(low_ref[...], one_hot(ids, low_ref.shape[1]))
        rel = relation_columns(rel_ref, kind_hot(kinds, rel_ref.shape[0]))
        half = head.shape[0] // 2
        h_re, h_im, r_re, r_im = head[:half], head[half:], rel[:half], rel[half:]
        query = jnp.concatenate([h_re * r_re - h_im * r_im, h_re * r_im + h_im * r_re], axis=0)
        out_ref[0, 0] = query.astype(BF16)
        out_ref[0, 1] = head.astype(BF16)


def ring_plan(lanes, pieces):
    plan = [(0, 0, pieces)]
    for k in range(1, (lanes + 1) // 2):
        plan += [(k, 0, pieces), (-k, 0, pieces)]
    if lanes % 2 == 0:
        half = pieces // 2
        plan += [(lanes // 2, 0, half), (-(lanes // 2), half, pieces - half)]
    return plan


def add_pieces(total, part, first):
    last, part = first + part.shape[0], part.astype(F32)
    if part.shape == total.shape:
        return total + part
    return jnp.concatenate([total[:first], total[first:last] + part, total[last:]], axis=0)


def ring_payload(parts, away, ahead=None, behind=None):
    plan = ring_plan(lax.axis_size("span"), parts[0].shape[0])
    blocks = {far: part for part, (far, _, _) in zip(parts, plan)}
    if ahead is None:
        return blocks[away].astype(BF16), blocks[-away].astype(BF16)
    ahead = add_pieces(blocks[away], ahead, 0)
    return ahead.astype(BF16), add_pieces(blocks[-away], behind, plan[-1][1]).astype(BF16)


def ring_total(parts, ahead, behind):
    plan = ring_plan(lax.axis_size("span"), parts[0].shape[0])
    return add_pieces(add_pieces(parts[0], ahead, 0), behind, plan[-1][1]).astype(BF16)


def shift_two(x, y, by):
    both = shift_span(jnp.concatenate([x, y], axis=0), by)
    return both[: x.shape[0]], both[x.shape[0] :]


def ring_shapes(shape, lanes):
    return [
        jax.ShapeDtypeStruct((count,) + tuple(shape[1:]), F32 if abs(away) < (lanes + 1) // 2 else BF16)
        for away, first, count in ring_plan(lanes, shape[0])
    ]


def gather_span(x):
    lanes = lax.axis_size("span")
    parts, ahead, behind = [x], x, x
    for _ in range(1, (lanes + 1) // 2):
        ahead, behind = shift_span(ahead, 1), shift_span(behind, -1)
        parts += [ahead, behind]
    if lanes % 2 == 0:
        half = x.shape[0] // 2
        parts += [shift_span(ahead[:half], 1), shift_span(behind[half:], -1)]
    return parts


def assemble(lanes, lane, parts, out_ref):
    width = parts[0].shape[2]
    block = out_ref.shape[0] // lanes
    plan = ring_plan(lanes, parts[0].shape[0])
    for at in range(lanes):

        @pl.when(lane == at)
        def _():
            for part, (behind, first, count) in zip(parts, plan):
                row = ((at - behind) % lanes) * block
                for b in range(count):
                    col = (first + b) * width
                    out_ref[row : row + block, col : col + width] = part[b, :block].astype(F32)


def emit(lanes, lane, acc_ref, outs):
    width = outs[0].shape[2]
    block = acc_ref.shape[0] // lanes
    plan = ring_plan(lanes, outs[0].shape[0])
    for at in range(lanes):

        @pl.when(lane == at)
        def _():
            for out, (away, first, count) in zip(outs, plan):
                row = ((at + away) % lanes) * block
                for b in range(count):
                    col = (first + b) * width
                    out[b, :block] = acc_ref[row : row + block, col : col + width].astype(out.dtype)


def main_kernel(
    steps, lanes, packed, meta_ref, tid_ref, rid_ref, rel_ref, edge_ref, parts_ref, *refs
):
    grad_ref, rel_out_ref = refs[:2]
    outs = refs[2:-6]
    table_ref, acc_ref, hot_ref, coef_ref, stage_ref, sems = refs[-6:]
    step = pl.program_id(0)

    @pl.when(step == 0)
    def _():
        pieces, _, width = parts_ref.shape
        copies = [
            pltpu.make_async_copy(parts_ref.at[b], there, sems.at[b])
            for b, there in enumerate(
                table_ref.at[:, pl.ds(b * width, width)] if width % 128 == 0 else stage_ref.at[b]
                for b in range(pieces)
            )
        ]
        for copy in copies:
            copy.start()
        acc_ref[...] = jnp.zeros_like(acc_ref)
        rel_out_ref[...] = jnp.zeros_like(rel_out_ref)
        for copy in copies:
            copy.wait()
        if width % 128:
            for b in range(pieces):
                table_ref[:, b * width : (b + 1) * width] = stage_ref[b]

    @pl.when(is_live(meta_ref, step, steps, tid_ref.shape[2]))
    def _():
        ids = live_ids(tid_ref[0], meta_ref, step, steps)
        hot_ref[...] = one_hot(ids, table_ref.shape[1])
        tail = dot_nn(table_ref[...], hot_ref[...]).astype(BF16)
        scores = dot_tn(edge_ref[0, 0], tail)
        sig = 0.5 * jnp.tanh(0.5 * scores) + 0.5
        diagonal = lax.broadcasted_iota(jnp.int32, scores.shape, 0) == lax.broadcasted_iota(
            jnp.int32, scores.shape, 1
        )
        coef_ref[...] = jnp.where(diagonal, sig - 1.0, NEG_WEIGHT * sig).astype(BF16)
        grad_tail = dot_nn(edge_ref[0, 0], coef_ref[...])
        acc_ref[...] += dot_nt(grad_tail.astype(BF16), hot_ref[...])

        kinds = live_ids(rid_ref[0], meta_ref, step, steps)
        kind = kind_hot(kinds, rel_ref.shape[0])
        rel = relation_columns(rel_ref, kind)
        head = edge_ref[0, 1].astype(F32)
        half = head.shape[0] // 2
        h_re, h_im, r_re, r_im = head[:half], head[half:], rel[:half], rel[half:]
        grad_query = dot_nt(tail, coef_ref[...])
        g_re, g_im = grad_query[:half], grad_query[half:]
        grad_head = jnp.concatenate([g_re * r_re + g_im * r_im, g_im * r_re - g_re * r_im], axis=0)
        grad_ref[0] = grad_head.astype(BF16)
        grad_rel = jnp.concatenate([g_re * h_re + g_im * h_im, g_im * h_re - g_re * h_im], axis=0)
        rel_out_ref[...] += dot_nt(grad_rel.astype(BF16), kind.astype(BF16))

    @pl.when(step == steps - 1)
    def _():
        emit(lanes, meta_ref[1], acc_ref, outs)
        if packed:
            rel_rows = rel_out_ref[...].T
            block = rel_rows.shape[1] // lanes
            each = rel_rows.shape[0] // outs[0].shape[0]
            plan = ring_plan(lanes, outs[0].shape[0])
            for at in range(lanes):

                @pl.when(meta_ref[1] == at)
                def _():
                    for out, (away, first, count) in zip(outs, plan):
                        col = ((at + away) % lanes) * block
                        for b in range(count):
                            row = (first + b) * each
                            out[b, block:, :block] = rel_rows[
                                row : row + each, col : col + block
                            ].astype(out.dtype)


def source_kernel(steps, lanes, meta_ref, hid_ref, grad_ref, *refs):
    outs, acc_ref = refs[:-1], refs[-1]
    step = pl.program_id(0)

    @pl.when(step == 0)
    def _():
        acc_ref[...] = jnp.zeros_like(acc_ref)

    @pl.when(is_live(meta_ref, step, steps, hid_ref.shape[2]))
    def _():
        ids = live_ids(hid_ref[0], meta_ref, step, steps)
        acc_ref[...] += dot_nt(grad_ref[0], one_hot(ids, acc_ref.shape[1]))

    @pl.when(step == steps - 1)
    def _():
        emit(lanes, meta_ref[1], acc_ref, outs)
        block = acc_ref.shape[0] // lanes
        for out in outs:
            if out.shape[1] > block:
                out[:, block:] = jnp.zeros((out.shape[0], out.shape[1] - block, out.shape[2]), out.dtype)


def pick_kernel(plan_ref, in_ref, out_ref, sems):
    copies = [
        pltpu.make_async_copy(in_ref.at[plan_ref[b]], out_ref.at[b], sems.at[b])
        for b in range(in_ref.shape[0])
    ]
    for copy in copies:
        copy.start()
    for copy in copies:
        copy.wait()


def place_kernel(block, plan_ref, in_ref, out_ref, held_ref, load_sem, sems):
    load = pltpu.make_async_copy(in_ref, held_ref, load_sem)
    load.start()
    load.wait()
    if in_ref.shape[1] > block:
        total = jnp.sum(held_ref[:, block:].astype(F32), axis=0).astype(BF16)
        for b in range(in_ref.shape[0]):
            held_ref[b, block:] = total
    copies = [
        pltpu.make_async_copy(held_ref.at[b], out_ref.at[plan_ref[b]], sems.at[b])
        for b in range(in_ref.shape[0])
    ]
    for copy in copies:
        copy.start()
    for copy in copies:
        copy.wait()


def adagrad(table, state, grad, axis):
    mean = jnp.sum(grad * grad, axis=axis, keepdims=True) / grad.shape[axis]
    return table - grad * (LEARN_RATE / jnp.sqrt(state + mean))


def update_kernel(lanes, joined, meta_ref, *refs):
    count = len(ring_plan(lanes, 2))
    if joined:
        table_any, state_ref, rel_ref, rel_state_ref = refs[:4]
        parts_any, refs = refs[4 : 4 + count], refs[4 + count :]
        out_any, rel_out_ref, rel_grad_ref = refs[:3]
        refs = refs[3:]
    else:
        table_any, state_ref = refs[:2]
        parts_any, out_any, refs = refs[2 : 2 + count], refs[2 + count], refs[3 + count :]
    table_ref, grad_ref, parts, (part_sems, load_sems, store_sems) = refs[0], refs[1], refs[2:-3], refs[-3:]
    features, rows = table_ref.shape
    chunk = 256 if rows % 256 == 0 else rows
    spots = [pl.ds(first, chunk) for first in range(0, rows, chunk)]
    fetches = [
        pltpu.make_async_copy(far, near, part_sems.at[k])
        for k, (far, near) in enumerate(zip(parts_any, parts))
    ]
    loads = [
        pltpu.make_async_copy(table_any.at[:, spot], table_ref.at[:, spot], load_sems.at[k])
        for k, spot in enumerate(spots)
    ]
    stores = [
        pltpu.make_async_copy(table_ref.at[:, spot], out_any.at[:, spot], store_sems.at[k])
        for k, spot in enumerate(spots)
    ]
    for copy in fetches + loads:
        copy.start()
    for copy in fetches:
        copy.wait()
    assemble(lanes, meta_ref[1], parts, grad_ref)
    for spot, load, store in zip(spots, loads, stores):
        load.wait()
        table_ref[:, spot] = adagrad(table_ref[:, spot], state_ref[:, spot], grad_ref[:, spot], 0)
        store.start()
    if joined:
        block = features // lanes
        each = parts[0].shape[1] - block
        plan = ring_plan(lanes, parts[0].shape[0])
        for at in range(lanes):

            @pl.when(meta_ref[1] == at)
            def _():
                for part, (behind, first, pieces) in zip(parts, plan):
                    col = ((at - behind) % lanes) * block
                    for b in range(pieces):
                        row = (first + b) * each
                        piece = part[b, block:, :block].astype(F32)
                        rel_grad_ref[row : row + each, col : col + block] = piece

        rel_out_ref[...] = adagrad(rel_ref[...], rel_state_ref[...], rel_grad_ref[...], 1)
    for store in stores:
        store.wait()


def whole(shape):
    zeros = (0,) * len(shape)
    return pl.BlockSpec(tuple(shape), lambda i: zeros)


def per_span(shape):
    rest = (0,) * (len(shape) - 1)
    return pl.BlockSpec((1,) + tuple(shape[1:]), lambda i: (i,) + rest)


def shift_span(x, by):
    count = lax.axis_size("span")
    return lax.ppermute(x, "span", [(i, (i + by) % count) for i in range(count)])


def swap_buckets(x):
    return lax.all_to_all(x, "bucket", split_axis=0, concat_axis=0, tiled=True)


def after(x, y):
    return lax.optimization_barrier((x, y))[0]


def update(lanes, meta, table, state, parts, relation=None, relation_state=None):
    joined = relation is not None
    vmem = pl.BlockSpec(memory_space=pltpu.VMEM)
    dma = pltpu.SemaphoreType.DMA
    extra = (relation, relation_state) if joined else ()
    chunks = max(1, table.shape[1] // 256)
    return pl.pallas_call(
        functools.partial(update_kernel, lanes, joined),
        out_shape=[jax.ShapeDtypeStruct(t.shape, F32) for t in (table,) + extra[:1]],
        in_specs=[SMEM_SPEC, ANY_SPEC, vmem] + [vmem] * len(extra) + [ANY_SPEC] * len(parts),
        out_specs=[ANY_SPEC] + [vmem] * joined,
        scratch_shapes=[pltpu.VMEM(t.shape, F32) for t in extra[:1]]
        + [pltpu.VMEM(table.shape, F32)] * 2
        + [pltpu.VMEM(part.shape, BF16) for part in parts]
        + [dma((len(parts),)), dma((chunks,)), dma((chunks,))],
        compiler_params=params(24),
    )(meta, table, state, *extra, *parts)


def sum_all(x):
    for axis in ("span", "bucket"):
        count = lax.axis_size(axis)
        if count & (count - 1):
            x = lax.psum(x, axis)
            continue
        bit = 1
        while bit < count:
            x = x + lax.ppermute(x, axis, [(i, i ^ bit) for i in range(count)])
            bit *= 2
    return x


def per_device(
    source_table,
    target_table,
    source_state,
    target_state,
    relation,
    relation_state,
    plan,
    source_index,
    target_index,
    relation_index,
    edge_counts,
):
    buckets = lax.axis_size("bucket")
    lanes = lax.axis_size("span")
    lane = lax.axis_index("span").astype(jnp.int32)
    rows, features = source_table.shape
    steps = source_index.shape[1] // E_CH
    kinds = relation.shape[0]
    block = features // lanes
    width = rows // buckets
    meta = jnp.stack([edge_counts[0], lane])
    hid = source_index.reshape(steps, 1, E_CH)
    tid = target_index.reshape(steps, 1, E_CH)
    rid = relation_index.reshape(steps, 1, E_CH)
    source_cols, target_cols = source_table.T, target_table.T

    owned = target_cols.astype(BF16).reshape(features, buckets, width).transpose(1, 0, 2)
    spread = swap_buckets(owned)
    dma = pltpu.SemaphoreType.DMA
    chosen = pl.pallas_call(
        pick_kernel,
        out_shape=jax.ShapeDtypeStruct(owned.shape, BF16),
        in_specs=[SMEM_SPEC, ANY_SPEC],
        out_specs=ANY_SPEC,
        scratch_shapes=[dma((buckets,))],
        compiler_params=params(8),
    )(plan, spread)
    fetched = swap_buckets(chosen)
    packed = kinds % buckets == 0 and width >= block
    pieces = (buckets, block, width)
    bundles = (buckets, block + kinds // buckets, width) if packed else pieces
    bundle_shape = jax.ShapeDtypeStruct(bundles, BF16)

    edge_shape = (steps, features, E_CH)
    both_shape = (steps, 2) + edge_shape[1:]
    edges = pl.pallas_call(
        functools.partial(prep_kernel, steps),
        grid=(steps,),
        out_shape=jax.ShapeDtypeStruct(both_shape, BF16),
        in_specs=[
            SMEM_SPEC,
            per_span(hid.shape),
            per_span(rid.shape),
            whole(source_cols.shape),
            whole(relation.shape),
        ],
        out_specs=per_span(both_shape),
        scratch_shapes=[pltpu.VMEM((features, rows), BF16)],
        compiler_params=params(56),
        cost_estimate=cost(4 * steps * features * rows * E_CH, 8 * features * steps * E_CH),
    )(meta, hid, rid, source_cols, relation)

    bundle_outs = ring_shapes(bundles, lanes)
    grad_head, rel_part, *target_out = pl.pallas_call(
        functools.partial(main_kernel, steps, lanes, packed),
        grid=(steps,),
        out_shape=[
            jax.ShapeDtypeStruct(edge_shape, BF16),
            jax.ShapeDtypeStruct((features, kinds), F32),
        ]
        + bundle_outs,
        in_specs=[
            SMEM_SPEC,
            per_span(tid.shape),
            per_span(rid.shape),
            whole(relation.shape),
            per_span(both_shape),
            ANY_SPEC,
        ],
        out_specs=[per_span(edge_shape), whole((features, kinds))]
        + [whole(out.shape) for out in bundle_outs],
        scratch_shapes=[
            pltpu.VMEM((features, rows), BF16),
            pltpu.VMEM((features, rows), F32),
            pltpu.VMEM((rows, E_CH), BF16),
            pltpu.VMEM((E_CH, E_CH), BF16),
            pltpu.VMEM(owned.shape if width % 128 else (16, 128), BF16),
            dma((buckets,)),
        ],
        compiler_params=params(48),
        cost_estimate=cost(12 * steps * features * rows * E_CH, 8 * features * steps * E_CH),
    )(meta, tid, rid, relation, edges, fetched)

    source_out = pl.pallas_call(
        functools.partial(source_kernel, steps, lanes),
        grid=(steps,),
        out_shape=bundle_outs,
        in_specs=[SMEM_SPEC, per_span(hid.shape), per_span(edge_shape)],
        out_specs=[whole(out.shape) for out in bundle_outs],
        scratch_shapes=[pltpu.VMEM((features, rows), F32)],
        compiler_params=params(24),
        cost_estimate=cost(4 * steps * features * rows * E_CH, 8 * features * steps * E_CH),
    )(meta, hid, grad_head)

    reach = lanes // 2
    ahead, behind = ring_payload(target_out, reach)
    for away in range(reach - 1, 0, -1):
        ahead, behind = shift_span(ahead, 1), shift_span(behind, -1)
        ahead, behind = after((ahead, behind), source_out)
        ahead, behind = ring_payload(target_out, away, ahead, behind)
    source_ahead, source_behind = ring_payload(source_out, reach)
    ahead, source_ahead = shift_two(ahead, source_ahead, 1)
    behind, source_behind = shift_two(behind, source_behind, -1)
    target_sum = ring_total(target_out, ahead, behind)
    returned = swap_buckets(target_sum)
    sorted_out = pl.pallas_call(
        functools.partial(place_kernel, block),
        out_shape=bundle_shape,
        in_specs=[SMEM_SPEC, ANY_SPEC],
        out_specs=ANY_SPEC,
        scratch_shapes=[pltpu.VMEM(bundles, BF16), dma, dma((buckets,))],
        compiler_params=params(16),
    )(plan, returned)
    target_home = swap_buckets(sorted_out)
    for away in range(reach - 1, 0, -1):
        source_ahead, source_behind = after((source_ahead, source_behind), target_sum)
        source_ahead, source_behind = ring_payload(source_out, away, source_ahead, source_behind)
        source_ahead, source_behind = shift_span(source_ahead, 1), shift_span(source_behind, -1)
    source_ahead, source_behind = after((source_ahead, source_behind), returned)
    source_sum = ring_total(source_out, source_ahead, source_behind)
    source_parts = gather_span(source_sum)
    home_parts = gather_span(target_home)
    (new_source,) = update(lanes, meta, source_cols, source_state.reshape(1, rows), source_parts)
    target_update = (lanes, meta, target_cols, target_state.reshape(1, rows), home_parts)
    if packed:
        relation_update = (relation, relation_state.reshape(kinds, 1))
        new_target, new_relation = update(*target_update, *relation_update)
    else:
        (new_target,) = update(*target_update)
        rel_total = sum_all(rel_part).T
        mean = jnp.mean(rel_total * rel_total, axis=1)
        new_relation = relation - LEARN_RATE * rel_total / jnp.sqrt(relation_state + mean)[:, None]
    return (new_source.T, new_target.T, new_relation)


def solution(mesh):
    placed = (
        P("bucket", None),
        P("bucket", None),
        P("bucket"),
        P("bucket"),
        P(),
        P(),
        P(),
        P("bucket", "span"),
        P("bucket", "span"),
        P("bucket", "span"),
        P("bucket"),
    )
    return jax.shard_map(
        per_device,
        mesh=mesh,
        in_specs=placed,
        out_specs=(P("bucket", None), P("bucket", None), P()),
        check_vma=False,
    )
```

```python
import functools

import jax
import jax.numpy as jnp
from jax import lax
from jax.experimental import pallas as pl
from jax.experimental.pallas import tpu as pltpu
from jax.sharding import PartitionSpec as P

E_CH = 640
LEARN_RATE = 0.25
NEG_WEIGHT = 0.03125

F32 = jnp.float32
BF16 = jnp.bfloat16
MIB = 1024 * 1024
SMEM_SPEC = pl.BlockSpec(memory_space=pltpu.SMEM)


ANY_SPEC = pl.BlockSpec(memory_space=pl.ANY)


def params(mib):
    return pltpu.CompilerParams(vmem_limit_bytes=mib * MIB)


def cost(flops, nbytes):
    return pl.CostEstimate(flops=int(flops), bytes_accessed=int(nbytes), transcendentals=0)


def dot_nn(a, b):
    return lax.dot_general(a, b, (((1,), (0,)), ((), ())), preferred_element_type=F32)


def dot_nt(a, b):
    return lax.dot_general(a, b, (((1,), (1,)), ((), ())), preferred_element_type=F32)


def dot_tn(a, b):
    return lax.dot_general(a, b, (((0,), (0,)), ((), ())), preferred_element_type=F32)


def live_ids(ids, meta_ref, step, steps):
    width = ids.shape[1]
    start = (meta_ref[1] * steps + step) * width
    slots = start + lax.broadcasted_iota(jnp.int32, ids.shape, 1)
    return jnp.where(slots < meta_ref[0], ids, -1)


def is_live(meta_ref, step, steps, width):
    return (meta_ref[1] * steps + step) * width < meta_ref[0]


def one_hot(ids, rows):
    match = lax.broadcasted_iota(jnp.int32, (rows, ids.shape[1]), 0) == ids
    return jnp.where(match, 1.0, 0.0).astype(BF16)


def relation_columns(rel_ref, kind):
    rel = rel_ref[...]
    high = rel.astype(BF16)
    rest = rel - high.astype(F32)
    middle = rest.astype(BF16)
    low = (rest - middle.astype(F32)).astype(BF16)
    parts = jnp.concatenate([high.astype(F32), middle.astype(F32), low.astype(F32)], axis=0)
    hot = jnp.concatenate([kind, kind, kind], axis=0)
    return dot_tn(parts.astype(BF16), hot.astype(BF16))


def kind_hot(ids, count):
    match = lax.broadcasted_iota(jnp.int32, (count, ids.shape[1]), 0) == ids
    return jnp.where(match, 1.0, 0.0)


def prep_kernel(steps, meta_ref, hid_ref, rid_ref, src_ref, rel_ref, out_ref, low_ref):
    step = pl.program_id(0)

    @pl.when(step == 0)
    def _():
        low_ref[...] = src_ref[...].astype(BF16)

    @pl.when(is_live(meta_ref, step, steps, hid_ref.shape[2]))
    def _():
        ids = live_ids(hid_ref[0], meta_ref, step, steps)
        kinds = live_ids(rid_ref[0], meta_ref, step, steps)
        head = dot_nn(low_ref[...], one_hot(ids, low_ref.shape[1]))
        rel = relation_columns(rel_ref, kind_hot(kinds, rel_ref.shape[0]))
        half = head.shape[0] // 2
        h_re, h_im, r_re, r_im = head[:half], head[half:], rel[:half], rel[half:]
        query = jnp.concatenate([h_re * r_re - h_im * r_im, h_re * r_im + h_im * r_re], axis=0)
        out_ref[0, 0] = query.astype(BF16)
        out_ref[0, 1] = head.astype(BF16)


def ring_plan(lanes, pieces):
    plan = [(0, 0, pieces)]
    for k in range(1, (lanes + 1) // 2):
        plan += [(k, 0, pieces), (-k, 0, pieces)]
    if lanes % 2 == 0:
        half = pieces // 2
        plan += [(lanes // 2, 0, half), (-(lanes // 2), half, pieces - half)]
    return plan


def add_pieces(total, part, first):
    last, part = first + part.shape[0], part.astype(F32)
    if part.shape == total.shape:
        return total + part
    return jnp.concatenate([total[:first], total[first:last] + part, total[last:]], axis=0)


def ring_payload(parts, away, ahead=None, behind=None):
    plan = ring_plan(lax.axis_size("span"), parts[0].shape[0])
    blocks = {far: part for part, (far, _, _) in zip(parts, plan)}
    if ahead is None:
        return blocks[away].astype(BF16), blocks[-away].astype(BF16)
    ahead = add_pieces(blocks[away], ahead, 0)
    return ahead.astype(BF16), add_pieces(blocks[-away], behind, plan[-1][1]).astype(BF16)


def ring_total(parts, ahead, behind):
    plan = ring_plan(lax.axis_size("span"), parts[0].shape[0])
    return add_pieces(add_pieces(parts[0], ahead, 0), behind, plan[-1][1]).astype(BF16)


def shift_two(x, y, by):
    both = shift_span(jnp.concatenate([x, y], axis=0), by)
    return both[: x.shape[0]], both[x.shape[0] :]


def ring_shapes(shape, lanes):
    return [
        jax.ShapeDtypeStruct((count,) + tuple(shape[1:]), F32 if abs(away) < (lanes + 1) // 2 else BF16)
        for away, first, count in ring_plan(lanes, shape[0])
    ]


def gather_span(x):
    lanes = lax.axis_size("span")
    parts, ahead, behind = [x], x, x
    for _ in range(1, (lanes + 1) // 2):
        ahead, behind = shift_span(ahead, 1), shift_span(behind, -1)
        parts += [ahead, behind]
    if lanes % 2 == 0:
        half = x.shape[0] // 2
        parts += [shift_span(ahead[:half], 1), shift_span(behind[half:], -1)]
    return parts


def assemble(lanes, lane, parts, out_ref):
    width = parts[0].shape[2]
    block = out_ref.shape[0] // lanes
    plan = ring_plan(lanes, parts[0].shape[0])
    for at in range(lanes):

        @pl.when(lane == at)
        def _():
            for part, (behind, first, count) in zip(parts, plan):
                row = ((at - behind) % lanes) * block
                for b in range(count):
                    col = (first + b) * width
                    out_ref[row : row + block, col : col + width] = part[b, :block].astype(F32)


def emit(lanes, lane, acc_ref, outs):
    width = outs[0].shape[2]
    block = acc_ref.shape[0] // lanes
    plan = ring_plan(lanes, outs[0].shape[0])
    for at in range(lanes):

        @pl.when(lane == at)
        def _():
            for out, (away, first, count) in zip(outs, plan):
                row = ((at + away) % lanes) * block
                for b in range(count):
                    col = (first + b) * width
                    out[b, :block] = acc_ref[row : row + block, col : col + width].astype(out.dtype)


def main_kernel(
    steps, lanes, packed, meta_ref, tid_ref, rid_ref, rel_ref, edge_ref, parts_ref, *refs
):
    grad_ref, rel_out_ref = refs[:2]
    outs = refs[2:-6]
    table_ref, acc_ref, hot_ref, coef_ref, stage_ref, sems = refs[-6:]
    step = pl.program_id(0)

    @pl.when(step == 0)
    def _():
        pieces, _, width = parts_ref.shape
        copies = [
            pltpu.make_async_copy(parts_ref.at[b], there, sems.at[b])
            for b, there in enumerate(
                table_ref.at[:, pl.ds(b * width, width)] if width % 128 == 0 else stage_ref.at[b]
                for b in range(pieces)
            )
        ]
        for copy in copies:
            copy.start()
        acc_ref[...] = jnp.zeros_like(acc_ref)
        rel_out_ref[...] = jnp.zeros_like(rel_out_ref)
        for copy in copies:
            copy.wait()
        if width % 128:
            for b in range(pieces):
                table_ref[:, b * width : (b + 1) * width] = stage_ref[b]

    @pl.when(is_live(meta_ref, step, steps, tid_ref.shape[2]))
    def _():
        ids = live_ids(tid_ref[0], meta_ref, step, steps)
        hot_ref[...] = one_hot(ids, table_ref.shape[1])
        tail = dot_nn(table_ref[...], hot_ref[...]).astype(BF16)
        scores = dot_tn(edge_ref[0, 0], tail)
        sig = 0.5 * jnp.tanh(0.5 * scores) + 0.5
        diagonal = lax.broadcasted_iota(jnp.int32, scores.shape, 0) == lax.broadcasted_iota(
            jnp.int32, scores.shape, 1
        )
        coef_ref[...] = jnp.where(diagonal, sig - 1.0, NEG_WEIGHT * sig).astype(BF16)
        grad_tail = dot_nn(edge_ref[0, 0], coef_ref[...])
        acc_ref[...] += dot_nt(grad_tail.astype(BF16), hot_ref[...])

        kinds = live_ids(rid_ref[0], meta_ref, step, steps)
        kind = kind_hot(kinds, rel_ref.shape[0])
        rel = relation_columns(rel_ref, kind)
        head = edge_ref[0, 1].astype(F32)
        half = head.shape[0] // 2
        h_re, h_im, r_re, r_im = head[:half], head[half:], rel[:half], rel[half:]
        grad_query = dot_nt(tail, coef_ref[...])
        g_re, g_im = grad_query[:half], grad_query[half:]
        grad_head = jnp.concatenate([g_re * r_re + g_im * r_im, g_im * r_re - g_re * r_im], axis=0)
        grad_ref[0] = grad_head.astype(BF16)
        grad_rel = jnp.concatenate([g_re * h_re + g_im * h_im, g_im * h_re - g_re * h_im], axis=0)
        rel_out_ref[...] += dot_nt(grad_rel.astype(BF16), kind.astype(BF16))

    @pl.when(step == steps - 1)
    def _():
        emit(lanes, meta_ref[1], acc_ref, outs)
        if packed:
            rel_rows = rel_out_ref[...].T
            block = rel_rows.shape[1] // lanes
            each = rel_rows.shape[0] // outs[0].shape[0]
            plan = ring_plan(lanes, outs[0].shape[0])
            for at in range(lanes):

                @pl.when(meta_ref[1] == at)
                def _():
                    for out, (away, first, count) in zip(outs, plan):
                        col = ((at + away) % lanes) * block
                        for b in range(count):
                            row = (first + b) * each
                            out[b, block:, :block] = rel_rows[
                                row : row + each, col : col + block
                            ].astype(out.dtype)


def source_kernel(steps, lanes, meta_ref, hid_ref, grad_ref, *refs):
    outs, acc_ref = refs[:-1], refs[-1]
    step = pl.program_id(0)

    @pl.when(step == 0)
    def _():
        acc_ref[...] = jnp.zeros_like(acc_ref)

    @pl.when(is_live(meta_ref, step, steps, hid_ref.shape[2]))
    def _():
        ids = live_ids(hid_ref[0], meta_ref, step, steps)
        acc_ref[...] += dot_nt(grad_ref[0], one_hot(ids, acc_ref.shape[1]))

    @pl.when(step == steps - 1)
    def _():
        emit(lanes, meta_ref[1], acc_ref, outs)
        block = acc_ref.shape[0] // lanes
        for out in outs:
            if out.shape[1] > block:
                out[:, block:] = jnp.zeros((out.shape[0], out.shape[1] - block, out.shape[2]), out.dtype)


def pick_kernel(plan_ref, in_ref, out_ref, sems):
    copies = [
        pltpu.make_async_copy(in_ref.at[plan_ref[b]], out_ref.at[b], sems.at[b])
        for b in range(in_ref.shape[0])
    ]
    for copy in copies:
        copy.start()
    for copy in copies:
        copy.wait()


def place_kernel(block, plan_ref, in_ref, out_ref, held_ref, load_sem, sems):
    load = pltpu.make_async_copy(in_ref, held_ref, load_sem)
    load.start()
    load.wait()
    if in_ref.shape[1] > block:
        total = jnp.sum(held_ref[:, block:].astype(F32), axis=0).astype(BF16)
        for b in range(in_ref.shape[0]):
            held_ref[b, block:] = total
    copies = [
        pltpu.make_async_copy(held_ref.at[b], out_ref.at[plan_ref[b]], sems.at[b])
        for b in range(in_ref.shape[0])
    ]
    for copy in copies:
        copy.start()
    for copy in copies:
        copy.wait()


def adagrad(table, state, grad, axis):
    mean = jnp.sum(grad * grad, axis=axis, keepdims=True) / grad.shape[axis]
    return table - grad * (LEARN_RATE / jnp.sqrt(state + mean))


def update_kernel(lanes, joined, meta_ref, *refs):
    count = len(ring_plan(lanes, 2))
    if joined:
        table_any, state_ref, rel_ref, rel_state_ref = refs[:4]
        parts_any, refs = refs[4 : 4 + count], refs[4 + count :]
        out_any, rel_out_ref, rel_grad_ref = refs[:3]
        refs = refs[3:]
    else:
        table_any, state_ref = refs[:2]
        parts_any, out_any, refs = refs[2 : 2 + count], refs[2 + count], refs[3 + count :]
    table_ref, grad_ref, parts, (part_sems, load_sems, store_sems) = refs[0], refs[1], refs[2:-3], refs[-3:]
    features, rows = table_ref.shape
    chunk = 256 if rows % 256 == 0 else rows
    spots = [pl.ds(first, chunk) for first in range(0, rows, chunk)]
    fetches = [
        pltpu.make_async_copy(far, near, part_sems.at[k])
        for k, (far, near) in enumerate(zip(parts_any, parts))
    ]
    loads = [
        pltpu.make_async_copy(table_any.at[:, spot], table_ref.at[:, spot], load_sems.at[k])
        for k, spot in enumerate(spots)
    ]
    stores = [
        pltpu.make_async_copy(table_ref.at[:, spot], out_any.at[:, spot], store_sems.at[k])
        for k, spot in enumerate(spots)
    ]
    for copy in fetches + loads:
        copy.start()
    for copy in fetches:
        copy.wait()
    assemble(lanes, meta_ref[1], parts, grad_ref)
    for spot, load, store in zip(spots, loads, stores):
        load.wait()
        table_ref[:, spot] = adagrad(table_ref[:, spot], state_ref[:, spot], grad_ref[:, spot], 0)
        store.start()
    if joined:
        block = features // lanes
        each = parts[0].shape[1] - block
        plan = ring_plan(lanes, parts[0].shape[0])
        for at in range(lanes):

            @pl.when(meta_ref[1] == at)
            def _():
                for part, (behind, first, pieces) in zip(parts, plan):
                    col = ((at - behind) % lanes) * block
                    for b in range(pieces):
                        row = (first + b) * each
                        piece = part[b, block:, :block].astype(F32)
                        rel_grad_ref[row : row + each, col : col + block] = piece

        rel_out_ref[...] = adagrad(rel_ref[...], rel_state_ref[...], rel_grad_ref[...], 1)
    for store in stores:
        store.wait()


def whole(shape):
    zeros = (0,) * len(shape)
    return pl.BlockSpec(tuple(shape), lambda i: zeros)


def per_span(shape):
    rest = (0,) * (len(shape) - 1)
    return pl.BlockSpec((1,) + tuple(shape[1:]), lambda i: (i,) + rest)


def shift_span(x, by):
    count = lax.axis_size("span")
    return lax.ppermute(x, "span", [(i, (i + by) % count) for i in range(count)])


def swap_buckets(x):
    return lax.all_to_all(x, "bucket", split_axis=0, concat_axis=0, tiled=True)


def after(x, y):
    return lax.optimization_barrier((x, y))[0]


def update(lanes, meta, table, state, parts, relation=None, relation_state=None):
    joined = relation is not None
    vmem = pl.BlockSpec(memory_space=pltpu.VMEM)
    dma = pltpu.SemaphoreType.DMA
    extra = (relation, relation_state) if joined else ()
    chunks = max(1, table.shape[1] // 256)
    return pl.pallas_call(
        functools.partial(update_kernel, lanes, joined),
        out_shape=[jax.ShapeDtypeStruct(t.shape, F32) for t in (table,) + extra[:1]],
        in_specs=[SMEM_SPEC, ANY_SPEC, vmem] + [vmem] * len(extra) + [ANY_SPEC] * len(parts),
        out_specs=[ANY_SPEC] + [vmem] * joined,
        scratch_shapes=[pltpu.VMEM(t.shape, F32) for t in extra[:1]]
        + [pltpu.VMEM(table.shape, F32)] * 2
        + [pltpu.VMEM(part.shape, BF16) for part in parts]
        + [dma((len(parts),)), dma((chunks,)), dma((chunks,))],
        compiler_params=params(24),
    )(meta, table, state, *extra, *parts)


def sum_all(x):
    for axis in ("span", "bucket"):
        count = lax.axis_size(axis)
        if count & (count - 1):
            x = lax.psum(x, axis)
            continue
        bit = 1
        while bit < count:
            x = x + lax.ppermute(x, axis, [(i, i ^ bit) for i in range(count)])
            bit *= 2
    return x


def per_device(
    source_table,
    target_table,
    source_state,
    target_state,
    relation,
    relation_state,
    plan,
    source_index,
    target_index,
    relation_index,
    edge_counts,
):
    buckets = lax.axis_size("bucket")
    lanes = lax.axis_size("span")
    lane = lax.axis_index("span").astype(jnp.int32)
    rows, features = source_table.shape
    steps = source_index.shape[1] // E_CH
    kinds = relation.shape[0]
    block = features // lanes
    width = rows // buckets
    meta = jnp.stack([edge_counts[0], lane])
    hid = source_index.reshape(steps, 1, E_CH)
    tid = target_index.reshape(steps, 1, E_CH)
    rid = relation_index.reshape(steps, 1, E_CH)
    source_cols, target_cols = source_table.T, target_table.T

    owned = target_cols.astype(BF16).reshape(features, buckets, width).transpose(1, 0, 2)
    spread = swap_buckets(owned)
    dma = pltpu.SemaphoreType.DMA
    chosen = pl.pallas_call(
        pick_kernel,
        out_shape=jax.ShapeDtypeStruct(owned.shape, BF16),
        in_specs=[SMEM_SPEC, ANY_SPEC],
        out_specs=ANY_SPEC,
        scratch_shapes=[dma((buckets,))],
        compiler_params=params(8),
    )(plan, spread)
    fetched = swap_buckets(chosen)
    packed = kinds % buckets == 0 and width >= block
    pieces = (buckets, block, width)
    bundles = (buckets, block + kinds // buckets, width) if packed else pieces
    bundle_shape = jax.ShapeDtypeStruct(bundles, BF16)

    edge_shape = (steps, features, E_CH)
    both_shape = (steps, 2) + edge_shape[1:]
    edges = pl.pallas_call(
        functools.partial(prep_kernel, steps),
        grid=(steps,),
        out_shape=jax.ShapeDtypeStruct(both_shape, BF16),
        in_specs=[
            SMEM_SPEC,
            per_span(hid.shape),
            per_span(rid.shape),
            whole(source_cols.shape),
            whole(relation.shape),
        ],
        out_specs=per_span(both_shape),
        scratch_shapes=[pltpu.VMEM((features, rows), BF16)],
        compiler_params=params(56),
        cost_estimate=cost(4 * steps * features * rows * E_CH, 8 * features * steps * E_CH),
    )(meta, hid, rid, source_cols, relation)

    bundle_outs = ring_shapes(bundles, lanes)
    grad_head, rel_part, *target_out = pl.pallas_call(
        functools.partial(main_kernel, steps, lanes, packed),
        grid=(steps,),
        out_shape=[
            jax.ShapeDtypeStruct(edge_shape, BF16),
            jax.ShapeDtypeStruct((features, kinds), F32),
        ]
        + bundle_outs,
        in_specs=[
            SMEM_SPEC,
            per_span(tid.shape),
            per_span(rid.shape),
            whole(relation.shape),
            per_span(both_shape),
            ANY_SPEC,
        ],
        out_specs=[per_span(edge_shape), whole((features, kinds))]
        + [whole(out.shape) for out in bundle_outs],
        scratch_shapes=[
            pltpu.VMEM((features, rows), BF16),
            pltpu.VMEM((features, rows), F32),
            pltpu.VMEM((rows, E_CH), BF16),
            pltpu.VMEM((E_CH, E_CH), BF16),
            pltpu.VMEM(owned.shape if width % 128 else (16, 128), BF16),
            dma((buckets,)),
        ],
        compiler_params=params(48),
        cost_estimate=cost(12 * steps * features * rows * E_CH, 8 * features * steps * E_CH),
    )(meta, tid, rid, relation, edges, fetched)

    source_out = pl.pallas_call(
        functools.partial(source_kernel, steps, lanes),
        grid=(steps,),
        out_shape=bundle_outs,
        in_specs=[SMEM_SPEC, per_span(hid.shape), per_span(edge_shape)],
        out_specs=[whole(out.shape) for out in bundle_outs],
        scratch_shapes=[pltpu.VMEM((features, rows), F32)],
        compiler_params=params(24),
        cost_estimate=cost(4 * steps * features * rows * E_CH, 8 * features * steps * E_CH),
    )(meta, hid, grad_head)

    reach = lanes // 2
    ahead, behind = ring_payload(target_out, reach)
    for away in range(reach - 1, 0, -1):
        ahead, behind = shift_span(ahead, 1), shift_span(behind, -1)
        ahead, behind = after((ahead, behind), source_out)
        ahead, behind = ring_payload(target_out, away, ahead, behind)
    ahead, behind = shift_span(ahead, 1), shift_span(behind, -1)
    target_sum = ring_total(target_out, ahead, behind)
    returned = swap_buckets(target_sum)
    ahead, behind = ring_payload(source_out, reach)
    for away in range(reach - 1, 0, -1):
        ahead, behind = shift_span(ahead, 1), shift_span(behind, -1)
        ahead, behind = ring_payload(source_out, away, ahead, behind)
    ahead, behind = shift_span(ahead, 1), shift_span(behind, -1)
    source_sum = ring_total(source_out, ahead, behind)
    returned = after(returned, source_sum)
    sorted_out = pl.pallas_call(
        functools.partial(place_kernel, block),
        out_shape=bundle_shape,
        in_specs=[SMEM_SPEC, ANY_SPEC],
        out_specs=ANY_SPEC,
        scratch_shapes=[pltpu.VMEM(bundles, BF16), dma, dma((buckets,))],
        compiler_params=params(16),
    )(plan, returned)
    target_home = swap_buckets(sorted_out)
    source_parts = gather_span(source_sum)
    target_home = after(target_home, source_parts)
    home_parts = gather_span(target_home)
    (new_source,) = update(lanes, meta, source_cols, source_state.reshape(1, rows), source_parts)
    target_update = (lanes, meta, target_cols, target_state.reshape(1, rows), home_parts)
    if packed:
        relation_update = (relation, relation_state.reshape(kinds, 1))
        new_target, new_relation = update(*target_update, *relation_update)
    else:
        (new_target,) = update(*target_update)
        rel_total = sum_all(rel_part).T
        mean = jnp.mean(rel_total * rel_total, axis=1)
        new_relation = relation - LEARN_RATE * rel_total / jnp.sqrt(relation_state + mean)[:, None]
    return (new_source.T, new_target.T, new_relation)


def solution(mesh):
    placed = (
        P("bucket", None),
        P("bucket", None),
        P("bucket"),
        P("bucket"),
        P(),
        P(),
        P(),
        P("bucket", "span"),
        P("bucket", "span"),
        P("bucket", "span"),
        P("bucket"),
    )
    return jax.shard_map(
        per_device,
        mesh=mesh,
        in_specs=placed,
        out_specs=(P("bucket", None), P("bucket", None), P()),
        check_vma=False,
    )
```

```python
import functools

import jax
import jax.numpy as jnp
from jax import lax
from jax.experimental import pallas as pl
from jax.experimental.pallas import tpu as pltpu
from jax.sharding import PartitionSpec as P

E_CH = 640
LEARN_RATE = 0.25
NEG_WEIGHT = 0.03125

F32 = jnp.float32
BF16 = jnp.bfloat16
MIB = 1024 * 1024
SMEM_SPEC = pl.BlockSpec(memory_space=pltpu.SMEM)


ANY_SPEC = pl.BlockSpec(memory_space=pl.ANY)
VMEM_SPEC = pl.BlockSpec(memory_space=pltpu.VMEM)


def params(mib):
    return pltpu.CompilerParams(vmem_limit_bytes=mib * MIB)


def cost(flops, nbytes):
    return pl.CostEstimate(flops=int(flops), bytes_accessed=int(nbytes), transcendentals=0)


def dot_nn(a, b):
    return lax.dot_general(a, b, (((1,), (0,)), ((), ())), preferred_element_type=F32)


def dot_nt(a, b):
    return lax.dot_general(a, b, (((1,), (1,)), ((), ())), preferred_element_type=F32)


def dot_tn(a, b):
    return lax.dot_general(a, b, (((0,), (0,)), ((), ())), preferred_element_type=F32)


def live_ids(ids, meta_ref, step, steps):
    width = ids.shape[1]
    start = (meta_ref[1] * steps + step) * width
    slots = start + lax.broadcasted_iota(jnp.int32, ids.shape, 1)
    return jnp.where(slots < meta_ref[0], ids, -1)


def is_live(meta_ref, step, steps, width):
    return (meta_ref[1] * steps + step) * width < meta_ref[0]


def one_hot(ids, rows):
    match = lax.broadcasted_iota(jnp.int32, (rows, ids.shape[1]), 0) == ids
    return jnp.where(match, 1.0, 0.0).astype(BF16)


def relation_columns(rel_ref, kind):
    rel = rel_ref[...]
    high = rel.astype(BF16)
    rest = rel - high.astype(F32)
    middle = rest.astype(BF16)
    low = (rest - middle.astype(F32)).astype(BF16)
    parts = jnp.concatenate([high.astype(F32), middle.astype(F32), low.astype(F32)], axis=0)
    hot = jnp.concatenate([kind, kind, kind], axis=0)
    return dot_tn(parts.astype(BF16), hot.astype(BF16))


def kind_hot(ids, count):
    match = lax.broadcasted_iota(jnp.int32, (count, ids.shape[1]), 0) == ids
    return jnp.where(match, 1.0, 0.0)


def prep_kernel(steps, meta_ref, hid_ref, rid_ref, src_ref, rel_ref, out_ref, low_ref):
    step = pl.program_id(0)

    @pl.when(step == 0)
    def _():
        low_ref[...] = src_ref[...].astype(BF16)

    @pl.when(is_live(meta_ref, step, steps, hid_ref.shape[2]))
    def _():
        ids = live_ids(hid_ref[0], meta_ref, step, steps)
        kinds = live_ids(rid_ref[0], meta_ref, step, steps)
        head = dot_nn(low_ref[...], one_hot(ids, low_ref.shape[1]))
        rel = relation_columns(rel_ref, kind_hot(kinds, rel_ref.shape[0]))
        half = head.shape[0] // 2
        h_re, h_im, r_re, r_im = head[:half], head[half:], rel[:half], rel[half:]
        query = jnp.concatenate([h_re * r_re - h_im * r_im, h_re * r_im + h_im * r_re], axis=0)
        out_ref[0, 0] = query.astype(BF16)
        out_ref[0, 1] = head.astype(BF16)


def ring_plan(lanes, pieces):
    plan = [(0, 0, pieces)]
    for k in range(1, (lanes + 1) // 2):
        plan += [(k, 0, pieces), (-k, 0, pieces)]
    if lanes % 2 == 0:
        half = pieces // 2
        plan += [(lanes // 2, 0, half), (-(lanes // 2), half, pieces - half)]
    return plan


def add_pieces(total, part, first):
    last, part = first + part.shape[0], part.astype(F32)
    if part.shape == total.shape:
        return total + part
    return jnp.concatenate([total[:first], total[first:last] + part, total[last:]], axis=0)


def ring_payload(parts, away, ahead=None, behind=None):
    plan = ring_plan(lax.axis_size("span"), parts[0].shape[0])
    blocks = {far: part for part, (far, _, _) in zip(parts, plan)}
    if ahead is None:
        return blocks[away].astype(BF16), blocks[-away].astype(BF16)
    ahead = add_pieces(blocks[away], ahead, 0)
    return ahead.astype(BF16), add_pieces(blocks[-away], behind, plan[-1][1]).astype(BF16)


def ring_total(parts, ahead, behind):
    plan = ring_plan(lax.axis_size("span"), parts[0].shape[0])
    return add_pieces(add_pieces(parts[0], ahead, 0), behind, plan[-1][1]).astype(BF16)


def shift_two(x, y, by):
    both = shift_span(jnp.concatenate([x, y], axis=0), by)
    return both[: x.shape[0]], both[x.shape[0] :]


def ring_shapes(shape, lanes):
    return [
        jax.ShapeDtypeStruct((count,) + tuple(shape[1:]), F32 if abs(away) < (lanes + 1) // 2 else BF16)
        for away, first, count in ring_plan(lanes, shape[0])
    ]


def gather_span(x):
    lanes = lax.axis_size("span")
    parts, ahead, behind = [x], x, x
    for _ in range(1, (lanes + 1) // 2):
        ahead, behind = shift_span(ahead, 1), shift_span(behind, -1)
        parts += [ahead, behind]
    if lanes % 2 == 0:
        half = x.shape[0] // 2
        parts += [shift_span(ahead[:half], 1), shift_span(behind[half:], -1)]
    return parts


def assemble(lanes, lane, parts, out_ref):
    width = parts[0].shape[2]
    block = out_ref.shape[0] // lanes
    plan = ring_plan(lanes, parts[0].shape[0])
    for at in range(lanes):

        @pl.when(lane == at)
        def _():
            for part, (behind, first, count) in zip(parts, plan):
                row = ((at - behind) % lanes) * block
                for b in range(count):
                    col = (first + b) * width
                    out_ref[row : row + block, col : col + width] = part[b, :block].astype(F32)


def emit(lanes, lane, acc_ref, outs):
    width = outs[0].shape[2]
    block = acc_ref.shape[0] // lanes
    plan = ring_plan(lanes, outs[0].shape[0])
    for at in range(lanes):

        @pl.when(lane == at)
        def _():
            for out, (away, first, count) in zip(outs, plan):
                row = ((at + away) % lanes) * block
                for b in range(count):
                    col = (first + b) * width
                    out[b, :block] = acc_ref[row : row + block, col : col + width].astype(out.dtype)


def main_kernel(
    steps, lanes, packed, meta_ref, tid_ref, rid_ref, rel_ref, edge_ref, parts_ref, *refs
):
    grad_ref, rel_out_ref = refs[:2]
    outs = refs[2:-4]
    table_ref, acc_ref, hot_ref, coef_ref = refs[-4:]
    step = pl.program_id(0)

    @pl.when(step == 0)
    def _():
        pieces, _, width = parts_ref.shape
        for b in range(pieces):
            table_ref[:, b * width : (b + 1) * width] = parts_ref[b]
        acc_ref[...] = jnp.zeros_like(acc_ref)
        rel_out_ref[...] = jnp.zeros_like(rel_out_ref)

    @pl.when(is_live(meta_ref, step, steps, tid_ref.shape[2]))
    def _():
        ids = live_ids(tid_ref[0], meta_ref, step, steps)
        hot_ref[...] = one_hot(ids, table_ref.shape[1])
        tail = dot_nn(table_ref[...], hot_ref[...]).astype(BF16)
        scores = dot_tn(edge_ref[0, 0], tail)
        sig = 0.5 * jnp.tanh(0.5 * scores) + 0.5
        diagonal = lax.broadcasted_iota(jnp.int32, scores.shape, 0) == lax.broadcasted_iota(
            jnp.int32, scores.shape, 1
        )
        coef_ref[...] = jnp.where(diagonal, sig - 1.0, NEG_WEIGHT * sig).astype(BF16)
        grad_tail = dot_nn(edge_ref[0, 0], coef_ref[...])
        acc_ref[...] += dot_nt(grad_tail.astype(BF16), hot_ref[...])

        kinds = live_ids(rid_ref[0], meta_ref, step, steps)
        kind = kind_hot(kinds, rel_ref.shape[0])
        rel = relation_columns(rel_ref, kind)
        head = edge_ref[0, 1].astype(F32)
        half = head.shape[0] // 2
        h_re, h_im, r_re, r_im = head[:half], head[half:], rel[:half], rel[half:]
        grad_query = dot_nt(tail, coef_ref[...])
        g_re, g_im = grad_query[:half], grad_query[half:]
        grad_head = jnp.concatenate([g_re * r_re + g_im * r_im, g_im * r_re - g_re * r_im], axis=0)
        grad_ref[0] = grad_head.astype(BF16)
        grad_rel = jnp.concatenate([g_re * h_re + g_im * h_im, g_im * h_re - g_re * h_im], axis=0)
        rel_out_ref[...] += dot_nt(grad_rel.astype(BF16), kind.astype(BF16))

    @pl.when(step == steps - 1)
    def _():
        emit(lanes, meta_ref[1], acc_ref, outs)
        if packed:
            rel_rows = rel_out_ref[...].T
            block = rel_rows.shape[1] // lanes
            each = rel_rows.shape[0] // outs[0].shape[0]
            plan = ring_plan(lanes, outs[0].shape[0])
            for at in range(lanes):

                @pl.when(meta_ref[1] == at)
                def _():
                    for out, (away, first, count) in zip(outs, plan):
                        col = ((at + away) % lanes) * block
                        for b in range(count):
                            row = (first + b) * each
                            out[b, block:, :block] = rel_rows[
                                row : row + each, col : col + block
                            ].astype(out.dtype)


def source_kernel(steps, lanes, meta_ref, hid_ref, grad_ref, *refs):
    outs, acc_ref = refs[:-1], refs[-1]
    step = pl.program_id(0)

    @pl.when(step == 0)
    def _():
        acc_ref[...] = jnp.zeros_like(acc_ref)

    @pl.when(is_live(meta_ref, step, steps, hid_ref.shape[2]))
    def _():
        ids = live_ids(hid_ref[0], meta_ref, step, steps)
        acc_ref[...] += dot_nt(grad_ref[0], one_hot(ids, acc_ref.shape[1]))

    @pl.when(step == steps - 1)
    def _():
        emit(lanes, meta_ref[1], acc_ref, outs)
        block = acc_ref.shape[0] // lanes
        for out in outs:
            if out.shape[1] > block:
                out[:, block:] = jnp.zeros((out.shape[0], out.shape[1] - block, out.shape[2]), out.dtype)


def pick_kernel(plan_ref, in_ref, out_ref):
    for b in range(in_ref.shape[0]):
        out_ref[b] = in_ref[plan_ref[b]]


def place_kernel(block, plan_ref, in_ref, out_ref):
    for b in range(in_ref.shape[0]):
        out_ref[plan_ref[b]] = in_ref[b]
    if in_ref.shape[1] > block:
        total = jnp.sum(in_ref[:, block:].astype(F32), axis=0).astype(BF16)
        for b in range(in_ref.shape[0]):
            out_ref[b, block:] = total


def adagrad(table, state, grad, axis):
    mean = jnp.sum(grad * grad, axis=axis, keepdims=True) / grad.shape[axis]
    return table - grad * (LEARN_RATE / jnp.sqrt(state + mean))


def update_kernel(lanes, joined, meta_ref, *refs):
    count = len(ring_plan(lanes, 2))
    if joined:
        table_ref, state_ref, rel_ref, rel_state_ref = refs[:4]
        parts, refs = refs[4 : 4 + count], refs[4 + count :]
        out_any, rel_out_ref, rel_grad_ref = refs[:3]
        refs = refs[3:]
    else:
        table_ref, state_ref = refs[:2]
        parts, out_any, refs = refs[2 : 2 + count], refs[2 + count], refs[3 + count :]
    new_ref, grad_ref, store_sems = refs
    features, rows = table_ref.shape
    chunk = 256 if rows % 256 == 0 else rows
    spots = [pl.ds(first, chunk) for first in range(0, rows, chunk)]
    stores = [
        pltpu.make_async_copy(new_ref.at[:, spot], out_any.at[:, spot], store_sems.at[k])
        for k, spot in enumerate(spots)
    ]
    assemble(lanes, meta_ref[1], parts, grad_ref)
    for spot, store in zip(spots, stores):
        new_ref[:, spot] = adagrad(table_ref[:, spot], state_ref[:, spot], grad_ref[:, spot], 0)
        store.start()
    if joined:
        block = features // lanes
        each = parts[0].shape[1] - block
        plan = ring_plan(lanes, parts[0].shape[0])
        for at in range(lanes):

            @pl.when(meta_ref[1] == at)
            def _():
                for part, (behind, first, pieces) in zip(parts, plan):
                    col = ((at - behind) % lanes) * block
                    for b in range(pieces):
                        row = (first + b) * each
                        piece = part[b, block:, :block].astype(F32)
                        rel_grad_ref[row : row + each, col : col + block] = piece

        rel_out_ref[...] = adagrad(rel_ref[...], rel_state_ref[...], rel_grad_ref[...], 1)
    for store in stores:
        store.wait()


def whole(shape):
    zeros = (0,) * len(shape)
    return pl.BlockSpec(tuple(shape), lambda i: zeros)


def per_span(shape):
    rest = (0,) * (len(shape) - 1)
    return pl.BlockSpec((1,) + tuple(shape[1:]), lambda i: (i,) + rest)


def shift_span(x, by):
    count = lax.axis_size("span")
    return lax.ppermute(x, "span", [(i, (i + by) % count) for i in range(count)])


def swap_buckets(x):
    return lax.all_to_all(x, "bucket", split_axis=0, concat_axis=0, tiled=True)


def after(x, y):
    return lax.optimization_barrier((x, y))[0]


def update(lanes, meta, table, state, parts, relation=None, relation_state=None):
    joined = relation is not None
    vmem = pl.BlockSpec(memory_space=pltpu.VMEM)
    dma = pltpu.SemaphoreType.DMA
    extra = (relation, relation_state) if joined else ()
    chunks = max(1, table.shape[1] // 256)
    return pl.pallas_call(
        functools.partial(update_kernel, lanes, joined),
        out_shape=[jax.ShapeDtypeStruct(t.shape, F32) for t in (table,) + extra[:1]],
        in_specs=[SMEM_SPEC] + [vmem] * (2 + len(extra) + len(parts)),
        out_specs=[ANY_SPEC] + [vmem] * joined,
        scratch_shapes=[pltpu.VMEM(t.shape, F32) for t in extra[:1]]
        + [pltpu.VMEM(table.shape, F32)] * 2
        + [dma((chunks,))],
        compiler_params=params(24),
    )(meta, table, state, *extra, *parts)


def sum_all(x):
    for axis in ("span", "bucket"):
        count = lax.axis_size(axis)
        if count & (count - 1):
            x = lax.psum(x, axis)
            continue
        bit = 1
        while bit < count:
            x = x + lax.ppermute(x, axis, [(i, i ^ bit) for i in range(count)])
            bit *= 2
    return x


def per_device(
    source_table,
    target_table,
    source_state,
    target_state,
    relation,
    relation_state,
    plan,
    source_index,
    target_index,
    relation_index,
    edge_counts,
):
    buckets = lax.axis_size("bucket")
    lanes = lax.axis_size("span")
    lane = lax.axis_index("span").astype(jnp.int32)
    rows, features = source_table.shape
    steps = source_index.shape[1] // E_CH
    kinds = relation.shape[0]
    block = features // lanes
    width = rows // buckets
    meta = jnp.stack([edge_counts[0], lane])
    hid = source_index.reshape(steps, 1, E_CH)
    tid = target_index.reshape(steps, 1, E_CH)
    rid = relation_index.reshape(steps, 1, E_CH)
    source_cols, target_cols = source_table.T, target_table.T

    owned = target_cols.astype(BF16).reshape(features, buckets, width).transpose(1, 0, 2)
    spread = swap_buckets(owned)
    dma = pltpu.SemaphoreType.DMA
    chosen = pl.pallas_call(
        pick_kernel,
        out_shape=jax.ShapeDtypeStruct(owned.shape, BF16),
        in_specs=[SMEM_SPEC, VMEM_SPEC],
        out_specs=VMEM_SPEC,
        compiler_params=params(8),
    )(plan, spread)
    fetched = swap_buckets(chosen)
    packed = kinds % buckets == 0 and width >= block
    pieces = (buckets, block, width)
    bundles = (buckets, block + kinds // buckets, width) if packed else pieces
    bundle_shape = jax.ShapeDtypeStruct(bundles, BF16)

    edge_shape = (steps, features, E_CH)
    both_shape = (steps, 2) + edge_shape[1:]
    edges = pl.pallas_call(
        functools.partial(prep_kernel, steps),
        grid=(steps,),
        out_shape=jax.ShapeDtypeStruct(both_shape, BF16),
        in_specs=[
            SMEM_SPEC,
            per_span(hid.shape),
            per_span(rid.shape),
            whole(source_cols.shape),
            whole(relation.shape),
        ],
        out_specs=per_span(both_shape),
        scratch_shapes=[pltpu.VMEM((features, rows), BF16)],
        compiler_params=params(56),
        cost_estimate=cost(4 * steps * features * rows * E_CH, 8 * features * steps * E_CH),
    )(meta, hid, rid, source_cols, relation)

    bundle_outs = ring_shapes(bundles, lanes)
    grad_head, rel_part, *target_out = pl.pallas_call(
        functools.partial(main_kernel, steps, lanes, packed),
        grid=(steps,),
        out_shape=[
            jax.ShapeDtypeStruct(edge_shape, BF16),
            jax.ShapeDtypeStruct((features, kinds), F32),
        ]
        + bundle_outs,
        in_specs=[
            SMEM_SPEC,
            per_span(tid.shape),
            per_span(rid.shape),
            whole(relation.shape),
            per_span(both_shape),
            VMEM_SPEC,
        ],
        out_specs=[per_span(edge_shape), whole((features, kinds))]
        + [whole(out.shape) for out in bundle_outs],
        scratch_shapes=[
            pltpu.VMEM((features, rows), BF16),
            pltpu.VMEM((features, rows), F32),
            pltpu.VMEM((rows, E_CH), BF16),
            pltpu.VMEM((E_CH, E_CH), BF16),
        ],
        compiler_params=params(48),
        cost_estimate=cost(12 * steps * features * rows * E_CH, 8 * features * steps * E_CH),
    )(meta, tid, rid, relation, edges, fetched)

    source_out = pl.pallas_call(
        functools.partial(source_kernel, steps, lanes),
        grid=(steps,),
        out_shape=bundle_outs,
        in_specs=[SMEM_SPEC, per_span(hid.shape), per_span(edge_shape)],
        out_specs=[whole(out.shape) for out in bundle_outs],
        scratch_shapes=[pltpu.VMEM((features, rows), F32)],
        compiler_params=params(24),
        cost_estimate=cost(4 * steps * features * rows * E_CH, 8 * features * steps * E_CH),
    )(meta, hid, grad_head)

    reach = lanes // 2
    ahead, behind = ring_payload(target_out, reach)
    for away in range(reach - 1, 0, -1):
        ahead, behind = shift_span(ahead, 1), shift_span(behind, -1)
        ahead, behind = after((ahead, behind), source_out)
        ahead, behind = ring_payload(target_out, away, ahead, behind)
    ahead, behind = shift_span(ahead, 1), shift_span(behind, -1)
    target_sum = ring_total(target_out, ahead, behind)
    returned = swap_buckets(target_sum)
    ahead, behind = ring_payload(source_out, reach)
    for away in range(reach - 1, 0, -1):
        ahead, behind = shift_span(ahead, 1), shift_span(behind, -1)
        ahead, behind = ring_payload(source_out, away, ahead, behind)
    ahead, behind = shift_span(ahead, 1), shift_span(behind, -1)
    source_sum = ring_total(source_out, ahead, behind)
    returned = after(returned, source_sum)
    sorted_out = pl.pallas_call(
        functools.partial(place_kernel, block),
        out_shape=bundle_shape,
        in_specs=[SMEM_SPEC, VMEM_SPEC],
        out_specs=VMEM_SPEC,
        compiler_params=params(8),
    )(plan, returned)
    target_home = swap_buckets(sorted_out)
    source_parts = gather_span(source_sum)
    target_home = after(target_home, source_parts)
    home_parts = gather_span(target_home)
    (new_source,) = update(lanes, meta, source_cols, source_state.reshape(1, rows), source_parts)
    target_update = (lanes, meta, target_cols, target_state.reshape(1, rows), home_parts)
    if packed:
        relation_update = (relation, relation_state.reshape(kinds, 1))
        new_target, new_relation = update(*target_update, *relation_update)
    else:
        (new_target,) = update(*target_update)
        rel_total = sum_all(rel_part).T
        mean = jnp.mean(rel_total * rel_total, axis=1)
        new_relation = relation - LEARN_RATE * rel_total / jnp.sqrt(relation_state + mean)[:, None]
    return (new_source.T, new_target.T, new_relation)


def solution(mesh):
    placed = (
        P("bucket", None),
        P("bucket", None),
        P("bucket"),
        P("bucket"),
        P(),
        P(),
        P(),
        P("bucket", "span"),
        P("bucket", "span"),
        P("bucket", "span"),
        P("bucket"),
    )
    return jax.shard_map(
        per_device,
        mesh=mesh,
        in_specs=placed,
        out_specs=(P("bucket", None), P("bucket", None), P()),
        check_vma=False,
    )
```

```python
import functools

import jax
import jax.numpy as jnp
from jax import lax
from jax.experimental import pallas as pl
from jax.experimental.pallas import tpu as pltpu
from jax.sharding import PartitionSpec as P

E_CH = 640
LEARN_RATE = 0.25
NEG_WEIGHT = 0.03125

F32 = jnp.float32
BF16 = jnp.bfloat16
MIB = 1024 * 1024
SMEM_SPEC = pl.BlockSpec(memory_space=pltpu.SMEM)


ANY_SPEC = pl.BlockSpec(memory_space=pl.ANY)
VMEM_SPEC = pl.BlockSpec(memory_space=pltpu.VMEM)


def params(mib):
    return pltpu.CompilerParams(vmem_limit_bytes=mib * MIB)


def cost(flops, nbytes):
    return pl.CostEstimate(flops=int(flops), bytes_accessed=int(nbytes), transcendentals=0)


def dot_nn(a, b):
    return lax.dot_general(a, b, (((1,), (0,)), ((), ())), preferred_element_type=F32)


def dot_nt(a, b):
    return lax.dot_general(a, b, (((1,), (1,)), ((), ())), preferred_element_type=F32)


def dot_tn(a, b):
    return lax.dot_general(a, b, (((0,), (0,)), ((), ())), preferred_element_type=F32)


def live_ids(ids, meta_ref, step, steps):
    width = ids.shape[1]
    start = (meta_ref[1] * steps + step) * width
    slots = start + lax.broadcasted_iota(jnp.int32, ids.shape, 1)
    return jnp.where(slots < meta_ref[0], ids, -1)


def is_live(meta_ref, step, steps, width):
    return (meta_ref[1] * steps + step) * width < meta_ref[0]


def one_hot(ids, rows):
    match = lax.broadcasted_iota(jnp.int32, (rows, ids.shape[1]), 0) == ids
    return jnp.where(match, 1.0, 0.0).astype(BF16)


def relation_columns(rel_ref, kind):
    rel = rel_ref[...]
    high = rel.astype(BF16)
    rest = rel - high.astype(F32)
    middle = rest.astype(BF16)
    low = (rest - middle.astype(F32)).astype(BF16)
    parts = jnp.concatenate([high.astype(F32), middle.astype(F32), low.astype(F32)], axis=0)
    hot = jnp.concatenate([kind, kind, kind], axis=0)
    return dot_tn(parts.astype(BF16), hot.astype(BF16))


def kind_hot(ids, count):
    match = lax.broadcasted_iota(jnp.int32, (count, ids.shape[1]), 0) == ids
    return jnp.where(match, 1.0, 0.0)


def prep_kernel(steps, meta_ref, hid_ref, rid_ref, src_ref, rel_ref, out_ref, low_ref):
    step = pl.program_id(0)

    @pl.when(step == 0)
    def _():
        low_ref[...] = src_ref[...].astype(BF16)

    @pl.when(is_live(meta_ref, step, steps, hid_ref.shape[2]))
    def _():
        ids = live_ids(hid_ref[0], meta_ref, step, steps)
        kinds = live_ids(rid_ref[0], meta_ref, step, steps)
        head = dot_nn(low_ref[...], one_hot(ids, low_ref.shape[1]))
        rel = relation_columns(rel_ref, kind_hot(kinds, rel_ref.shape[0]))
        half = head.shape[0] // 2
        h_re, h_im, r_re, r_im = head[:half], head[half:], rel[:half], rel[half:]
        query = jnp.concatenate([h_re * r_re - h_im * r_im, h_re * r_im + h_im * r_re], axis=0)
        out_ref[0, 0] = query.astype(BF16)
        out_ref[0, 1] = head.astype(BF16)


def ring_plan(lanes, pieces):
    plan = [(0, 0, pieces)]
    for k in range(1, (lanes + 1) // 2):
        plan += [(k, 0, pieces), (-k, 0, pieces)]
    if lanes % 2 == 0:
        half = pieces // 2
        plan += [(lanes // 2, 0, half), (-(lanes // 2), half, pieces - half)]
    return plan


def add_pieces(total, part, first):
    last, part = first + part.shape[0], part.astype(F32)
    if part.shape == total.shape:
        return total + part
    return jnp.concatenate([total[:first], total[first:last] + part, total[last:]], axis=0)


def ring_payload(parts, away, ahead=None, behind=None):
    plan = ring_plan(lax.axis_size("span"), parts[0].shape[0])
    blocks = {far: part for part, (far, _, _) in zip(parts, plan)}
    if ahead is None:
        return blocks[away].astype(BF16), blocks[-away].astype(BF16)
    ahead = add_pieces(blocks[away], ahead, 0)
    return ahead.astype(BF16), add_pieces(blocks[-away], behind, plan[-1][1]).astype(BF16)


def ring_total(parts, ahead, behind):
    plan = ring_plan(lax.axis_size("span"), parts[0].shape[0])
    return add_pieces(add_pieces(parts[0], ahead, 0), behind, plan[-1][1]).astype(BF16)


def shift_two(x, y, by):
    both = shift_span(jnp.concatenate([x, y], axis=0), by)
    return both[: x.shape[0]], both[x.shape[0] :]


def ring_shapes(shape, lanes):
    return [
        jax.ShapeDtypeStruct((count,) + tuple(shape[1:]), F32 if abs(away) < (lanes + 1) // 2 else BF16)
        for away, first, count in ring_plan(lanes, shape[0])
    ]


def gather_span(x):
    lanes = lax.axis_size("span")
    parts, ahead, behind = [x], x, x
    for _ in range(1, (lanes + 1) // 2):
        ahead, behind = shift_span(ahead, 1), shift_span(behind, -1)
        parts += [ahead, behind]
    if lanes % 2 == 0:
        half = x.shape[0] // 2
        parts += [shift_span(ahead[:half], 1), shift_span(behind[half:], -1)]
    return parts


def assemble(lanes, lane, parts, out_ref):
    width = parts[0].shape[2]
    block = out_ref.shape[0] // lanes
    plan = ring_plan(lanes, parts[0].shape[0])
    for at in range(lanes):

        @pl.when(lane == at)
        def _():
            for part, (behind, first, count) in zip(parts, plan):
                row = ((at - behind) % lanes) * block
                for b in range(count):
                    col = (first + b) * width
                    out_ref[row : row + block, col : col + width] = part[b, :block].astype(F32)


def emit(lanes, lane, acc_ref, outs):
    width = outs[0].shape[2]
    block = acc_ref.shape[0] // lanes
    plan = ring_plan(lanes, outs[0].shape[0])
    for at in range(lanes):

        @pl.when(lane == at)
        def _():
            for out, (away, first, count) in zip(outs, plan):
                row = ((at + away) % lanes) * block
                for b in range(count):
                    col = (first + b) * width
                    out[b, :block] = acc_ref[row : row + block, col : col + width].astype(out.dtype)


def main_kernel(
    steps, lanes, packed, meta_ref, tid_ref, rid_ref, rel_ref, edge_ref, parts_ref, *refs
):
    grad_ref, rel_out_ref = refs[:2]
    outs = refs[2:-4]
    table_ref, acc_ref, hot_ref, coef_ref = refs[-4:]
    step = pl.program_id(0)

    @pl.when(step == 0)
    def _():
        pieces, _, width = parts_ref.shape
        for b in range(pieces):
            table_ref[:, b * width : (b + 1) * width] = parts_ref[b]
        acc_ref[...] = jnp.zeros_like(acc_ref)
        rel_out_ref[...] = jnp.zeros_like(rel_out_ref)

    live = is_live(meta_ref, step, steps, tid_ref.shape[2])

    @pl.when(jnp.logical_not(live))
    def _():
        grad_ref[...] = jnp.zeros_like(grad_ref)

    @pl.when(live)
    def _():
        ids = live_ids(tid_ref[0], meta_ref, step, steps)
        hot_ref[...] = one_hot(ids, table_ref.shape[1])
        tail = dot_nn(table_ref[...], hot_ref[...]).astype(BF16)
        scores = dot_tn(edge_ref[0, 0], tail)
        sig = 0.5 * jnp.tanh(0.5 * scores) + 0.5
        diagonal = lax.broadcasted_iota(jnp.int32, scores.shape, 0) == lax.broadcasted_iota(
            jnp.int32, scores.shape, 1
        )
        coef_ref[...] = jnp.where(diagonal, sig - 1.0, NEG_WEIGHT * sig).astype(BF16)
        grad_tail = dot_nn(edge_ref[0, 0], coef_ref[...])
        acc_ref[...] += dot_nt(grad_tail.astype(BF16), hot_ref[...])

        kinds = live_ids(rid_ref[0], meta_ref, step, steps)
        kind = kind_hot(kinds, rel_ref.shape[0])
        rel = relation_columns(rel_ref, kind)
        head = edge_ref[0, 1].astype(F32)
        half = head.shape[0] // 2
        h_re, h_im, r_re, r_im = head[:half], head[half:], rel[:half], rel[half:]
        grad_query = dot_nt(tail, coef_ref[...])
        g_re, g_im = grad_query[:half], grad_query[half:]
        grad_head = jnp.concatenate([g_re * r_re + g_im * r_im, g_im * r_re - g_re * r_im], axis=0)
        grad_ref[0] = grad_head.astype(BF16)
        grad_rel = jnp.concatenate([g_re * h_re + g_im * h_im, g_im * h_re - g_re * h_im], axis=0)
        rel_out_ref[...] += dot_nt(grad_rel.astype(BF16), kind.astype(BF16))

    @pl.when(step == steps - 1)
    def _():
        emit(lanes, meta_ref[1], acc_ref, outs)
        if packed:
            rel_rows = rel_out_ref[...].T
            block = rel_rows.shape[1] // lanes
            each = rel_rows.shape[0] // outs[0].shape[0]
            plan = ring_plan(lanes, outs[0].shape[0])
            for at in range(lanes):

                @pl.when(meta_ref[1] == at)
                def _():
                    for out, (away, first, count) in zip(outs, plan):
                        col = ((at + away) % lanes) * block
                        for b in range(count):
                            row = (first + b) * each
                            out[b, block:, :block] = rel_rows[
                                row : row + each, col : col + block
                            ].astype(out.dtype)


def source_kernel(lanes, meta_ref, hid_ref, grad_ref, *refs):
    outs, acc_ref = refs[:-1], refs[-1]
    steps, rows = grad_ref.shape[0], acc_ref.shape[1]
    part = 256 if rows % 256 == 0 else rows
    ids = [live_ids(hid_ref[step], meta_ref, step, steps) for step in range(steps)]
    for first in range(0, rows, part):
        total = 0.0
        for step in range(steps):
            total += dot_nt(grad_ref[step], one_hot(ids[step] - first, part))
        acc_ref[:, first : first + part] = total
    emit(lanes, meta_ref[1], acc_ref, outs)
    block = acc_ref.shape[0] // lanes
    for out in outs:
        if out.shape[1] > block:
            out[:, block:] = jnp.zeros((out.shape[0], out.shape[1] - block, out.shape[2]), out.dtype)


def pick_kernel(plan_ref, in_ref, out_ref):
    for b in range(in_ref.shape[0]):
        out_ref[b] = in_ref[plan_ref[b]]


def place_kernel(block, plan_ref, in_ref, out_ref):
    for b in range(in_ref.shape[0]):
        out_ref[plan_ref[b]] = in_ref[b]
    if in_ref.shape[1] > block:
        total = jnp.sum(in_ref[:, block:].astype(F32), axis=0).astype(BF16)
        for b in range(in_ref.shape[0]):
            out_ref[b, block:] = total


def adagrad(table, state, grad, axis):
    mean = jnp.sum(grad * grad, axis=axis, keepdims=True) / grad.shape[axis]
    return table - grad * (LEARN_RATE / jnp.sqrt(state + mean))


def update_kernel(lanes, joined, meta_ref, *refs):
    count = len(ring_plan(lanes, 2))
    if joined:
        table_ref, state_ref, rel_ref, rel_state_ref = refs[:4]
        parts, refs = refs[4 : 4 + count], refs[4 + count :]
        out_any, rel_out_ref, rel_grad_ref = refs[:3]
        refs = refs[3:]
    else:
        table_ref, state_ref = refs[:2]
        parts, out_any, refs = refs[2 : 2 + count], refs[2 + count], refs[3 + count :]
    new_ref, grad_ref, store_sems = refs
    features, rows = table_ref.shape
    chunk = 256 if rows % 256 == 0 else rows
    spots = [pl.ds(first, chunk) for first in range(0, rows, chunk)]
    stores = [
        pltpu.make_async_copy(new_ref.at[:, spot], out_any.at[:, spot], store_sems.at[k])
        for k, spot in enumerate(spots)
    ]
    assemble(lanes, meta_ref[1], parts, grad_ref)
    for spot, store in zip(spots, stores):
        new_ref[:, spot] = adagrad(table_ref[:, spot], state_ref[:, spot], grad_ref[:, spot], 0)
        store.start()
    if joined:
        block = features // lanes
        each = parts[0].shape[1] - block
        plan = ring_plan(lanes, parts[0].shape[0])
        for at in range(lanes):

            @pl.when(meta_ref[1] == at)
            def _():
                for part, (behind, first, pieces) in zip(parts, plan):
                    col = ((at - behind) % lanes) * block
                    for b in range(pieces):
                        row = (first + b) * each
                        piece = part[b, block:, :block].astype(F32)
                        rel_grad_ref[row : row + each, col : col + block] = piece

        rel_out_ref[...] = adagrad(rel_ref[...], rel_state_ref[...], rel_grad_ref[...], 1)
    for store in stores:
        store.wait()


def whole(shape):
    zeros = (0,) * len(shape)
    return pl.BlockSpec(tuple(shape), lambda i: zeros)


def per_span(shape):
    rest = (0,) * (len(shape) - 1)
    return pl.BlockSpec((1,) + tuple(shape[1:]), lambda i: (i,) + rest)


def shift_span(x, by):
    count = lax.axis_size("span")
    return lax.ppermute(x, "span", [(i, (i + by) % count) for i in range(count)])


def swap_buckets(x):
    return lax.all_to_all(x, "bucket", split_axis=0, concat_axis=0, tiled=True)


def after(x, y):
    return lax.optimization_barrier((x, y))[0]


def update(lanes, meta, table, state, parts, relation=None, relation_state=None):
    joined = relation is not None
    vmem = pl.BlockSpec(memory_space=pltpu.VMEM)
    dma = pltpu.SemaphoreType.DMA
    extra = (relation, relation_state) if joined else ()
    chunks = max(1, table.shape[1] // 256)
    return pl.pallas_call(
        functools.partial(update_kernel, lanes, joined),
        out_shape=[jax.ShapeDtypeStruct(t.shape, F32) for t in (table,) + extra[:1]],
        in_specs=[SMEM_SPEC] + [vmem] * (2 + len(extra) + len(parts)),
        out_specs=[ANY_SPEC] + [vmem] * joined,
        scratch_shapes=[pltpu.VMEM(t.shape, F32) for t in extra[:1]]
        + [pltpu.VMEM(table.shape, F32)] * 2
        + [dma((chunks,))],
        compiler_params=params(24),
    )(meta, table, state, *extra, *parts)


def sum_all(x):
    for axis in ("span", "bucket"):
        count = lax.axis_size(axis)
        if count & (count - 1):
            x = lax.psum(x, axis)
            continue
        bit = 1
        while bit < count:
            x = x + lax.ppermute(x, axis, [(i, i ^ bit) for i in range(count)])
            bit *= 2
    return x


def per_device(
    source_table,
    target_table,
    source_state,
    target_state,
    relation,
    relation_state,
    plan,
    source_index,
    target_index,
    relation_index,
    edge_counts,
):
    buckets = lax.axis_size("bucket")
    lanes = lax.axis_size("span")
    lane = lax.axis_index("span").astype(jnp.int32)
    rows, features = source_table.shape
    steps = source_index.shape[1] // E_CH
    kinds = relation.shape[0]
    block = features // lanes
    width = rows // buckets
    meta = jnp.stack([edge_counts[0], lane])
    hid = source_index.reshape(steps, 1, E_CH)
    tid = target_index.reshape(steps, 1, E_CH)
    rid = relation_index.reshape(steps, 1, E_CH)
    source_cols, target_cols = source_table.T, target_table.T

    owned = target_cols.astype(BF16).reshape(features, buckets, width).transpose(1, 0, 2)
    spread = swap_buckets(owned)
    dma = pltpu.SemaphoreType.DMA
    chosen = pl.pallas_call(
        pick_kernel,
        out_shape=jax.ShapeDtypeStruct(owned.shape, BF16),
        in_specs=[SMEM_SPEC, VMEM_SPEC],
        out_specs=VMEM_SPEC,
        compiler_params=params(8),
    )(plan, spread)
    fetched = swap_buckets(chosen)
    packed = kinds % buckets == 0 and width >= block
    pieces = (buckets, block, width)
    bundles = (buckets, block + kinds // buckets, width) if packed else pieces
    bundle_shape = jax.ShapeDtypeStruct(bundles, BF16)

    edge_shape = (steps, features, E_CH)
    both_shape = (steps, 2) + edge_shape[1:]
    edges = pl.pallas_call(
        functools.partial(prep_kernel, steps),
        grid=(steps,),
        out_shape=jax.ShapeDtypeStruct(both_shape, BF16),
        in_specs=[
            SMEM_SPEC,
            per_span(hid.shape),
            per_span(rid.shape),
            whole(source_cols.shape),
            whole(relation.shape),
        ],
        out_specs=per_span(both_shape),
        scratch_shapes=[pltpu.VMEM((features, rows), BF16)],
        compiler_params=params(56),
        cost_estimate=cost(4 * steps * features * rows * E_CH, 8 * features * steps * E_CH),
    )(meta, hid, rid, source_cols, relation)

    bundle_outs = ring_shapes(bundles, lanes)
    grad_head, rel_part, *target_out = pl.pallas_call(
        functools.partial(main_kernel, steps, lanes, packed),
        grid=(steps,),
        out_shape=[
            jax.ShapeDtypeStruct(edge_shape, BF16),
            jax.ShapeDtypeStruct((features, kinds), F32),
        ]
        + bundle_outs,
        in_specs=[
            SMEM_SPEC,
            per_span(tid.shape),
            per_span(rid.shape),
            whole(relation.shape),
            per_span(both_shape),
            VMEM_SPEC,
        ],
        out_specs=[per_span(edge_shape), whole((features, kinds))]
        + [whole(out.shape) for out in bundle_outs],
        scratch_shapes=[
            pltpu.VMEM((features, rows), BF16),
            pltpu.VMEM((features, rows), F32),
            pltpu.VMEM((rows, E_CH), BF16),
            pltpu.VMEM((E_CH, E_CH), BF16),
        ],
        compiler_params=params(48),
        cost_estimate=cost(12 * steps * features * rows * E_CH, 8 * features * steps * E_CH),
    )(meta, tid, rid, relation, edges, fetched)

    source_out = pl.pallas_call(
        functools.partial(source_kernel, lanes),
        out_shape=bundle_outs,
        in_specs=[SMEM_SPEC, VMEM_SPEC, VMEM_SPEC],
        out_specs=[VMEM_SPEC] * len(bundle_outs),
        scratch_shapes=[pltpu.VMEM((features, rows), F32)],
        compiler_params=params(24),
        cost_estimate=cost(4 * steps * features * rows * E_CH, 8 * features * steps * E_CH),
    )(meta, hid, grad_head)

    reach = lanes // 2
    ahead, behind = ring_payload(target_out, reach)
    for away in range(reach - 1, 0, -1):
        ahead, behind = shift_span(ahead, 1), shift_span(behind, -1)
        ahead, behind = after((ahead, behind), source_out)
        ahead, behind = ring_payload(target_out, away, ahead, behind)
    ahead, behind = shift_span(ahead, 1), shift_span(behind, -1)
    target_sum = ring_total(target_out, ahead, behind)
    returned = swap_buckets(target_sum)
    ahead, behind = ring_payload(source_out, reach)
    for away in range(reach - 1, 0, -1):
        ahead, behind = shift_span(ahead, 1), shift_span(behind, -1)
        ahead, behind = ring_payload(source_out, away, ahead, behind)
    ahead, behind = shift_span(ahead, 1), shift_span(behind, -1)
    source_sum = ring_total(source_out, ahead, behind)
    returned = after(returned, source_sum)
    sorted_out = pl.pallas_call(
        functools.partial(place_kernel, block),
        out_shape=bundle_shape,
        in_specs=[SMEM_SPEC, VMEM_SPEC],
        out_specs=VMEM_SPEC,
        compiler_params=params(8),
    )(plan, returned)
    target_home = swap_buckets(sorted_out)
    source_parts = gather_span(source_sum)
    target_home = after(target_home, source_parts)
    home_parts = gather_span(target_home)
    (new_source,) = update(lanes, meta, source_cols, source_state.reshape(1, rows), source_parts)
    target_update = (lanes, meta, target_cols, target_state.reshape(1, rows), home_parts)
    if packed:
        relation_update = (relation, relation_state.reshape(kinds, 1))
        new_target, new_relation = update(*target_update, *relation_update)
    else:
        (new_target,) = update(*target_update)
        rel_total = sum_all(rel_part).T
        mean = jnp.mean(rel_total * rel_total, axis=1)
        new_relation = relation - LEARN_RATE * rel_total / jnp.sqrt(relation_state + mean)[:, None]
    return (new_source.T, new_target.T, new_relation)


def solution(mesh):
    placed = (
        P("bucket", None),
        P("bucket", None),
        P("bucket"),
        P("bucket"),
        P(),
        P(),
        P(),
        P("bucket", "span"),
        P("bucket", "span"),
        P("bucket", "span"),
        P("bucket"),
    )
    return jax.shard_map(
        per_device,
        mesh=mesh,
        in_specs=placed,
        out_specs=(P("bucket", None), P("bucket", None), P()),
        check_vma=False,
    )
```

```python
import functools

import jax
import jax.numpy as jnp
from jax import lax
from jax.experimental import pallas as pl
from jax.experimental.pallas import tpu as pltpu
from jax.sharding import PartitionSpec as P

E_CH = 640
LEARN_RATE = 0.25
NEG_WEIGHT = 0.03125

F32 = jnp.float32
BF16 = jnp.bfloat16
MIB = 1024 * 1024
SMEM_SPEC = pl.BlockSpec(memory_space=pltpu.SMEM)


ANY_SPEC = pl.BlockSpec(memory_space=pl.ANY)
VMEM_SPEC = pl.BlockSpec(memory_space=pltpu.VMEM)


def params(mib):
    return pltpu.CompilerParams(vmem_limit_bytes=mib * MIB)


def cost(flops, nbytes):
    return pl.CostEstimate(flops=int(flops), bytes_accessed=int(nbytes), transcendentals=0)


def dot_nn(a, b):
    return lax.dot_general(a, b, (((1,), (0,)), ((), ())), preferred_element_type=F32)


def dot_nt(a, b):
    return lax.dot_general(a, b, (((1,), (1,)), ((), ())), preferred_element_type=F32)


def dot_tn(a, b):
    return lax.dot_general(a, b, (((0,), (0,)), ((), ())), preferred_element_type=F32)


def live_ids(ids, meta_ref, step, steps):
    width = ids.shape[1]
    start = (meta_ref[1] * steps + step) * width
    slots = start + lax.broadcasted_iota(jnp.int32, ids.shape, 1)
    return jnp.where(slots < meta_ref[0], ids, -1)


def is_live(meta_ref, step, steps, width):
    return (meta_ref[1] * steps + step) * width < meta_ref[0]


def one_hot(ids, rows):
    match = lax.broadcasted_iota(jnp.int32, (rows, ids.shape[1]), 0) == ids
    return jnp.where(match, 1.0, 0.0).astype(BF16)


def relation_columns(rel_ref, kind):
    rel = rel_ref[...]
    high = rel.astype(BF16)
    rest = rel - high.astype(F32)
    middle = rest.astype(BF16)
    low = (rest - middle.astype(F32)).astype(BF16)
    parts = jnp.concatenate([high.astype(F32), middle.astype(F32), low.astype(F32)], axis=0)
    hot = jnp.concatenate([kind, kind, kind], axis=0)
    return dot_tn(parts.astype(BF16), hot.astype(BF16))


def kind_hot(ids, count):
    match = lax.broadcasted_iota(jnp.int32, (count, ids.shape[1]), 0) == ids
    return jnp.where(match, 1.0, 0.0)


def prep_kernel(steps, meta_ref, hid_ref, rid_ref, src_ref, rel_ref, out_ref, low_ref):
    step = pl.program_id(0)

    @pl.when(step == 0)
    def _():
        low_ref[...] = src_ref[...].astype(BF16)

    @pl.when(is_live(meta_ref, step, steps, hid_ref.shape[2]))
    def _():
        ids = live_ids(hid_ref[0], meta_ref, step, steps)
        kinds = live_ids(rid_ref[0], meta_ref, step, steps)
        head = dot_nn(low_ref[...], one_hot(ids, low_ref.shape[1]))
        rel = relation_columns(rel_ref, kind_hot(kinds, rel_ref.shape[0]))
        half = head.shape[0] // 2
        h_re, h_im, r_re, r_im = head[:half], head[half:], rel[:half], rel[half:]
        query = jnp.concatenate([h_re * r_re - h_im * r_im, h_re * r_im + h_im * r_re], axis=0)
        out_ref[0, 0] = query.astype(BF16)
        out_ref[0, 1] = head.astype(BF16)


def ring_plan(lanes, pieces):
    plan = [(0, 0, pieces)]
    for k in range(1, (lanes + 1) // 2):
        plan += [(k, 0, pieces), (-k, 0, pieces)]
    if lanes % 2 == 0:
        half = pieces // 2
        plan += [(lanes // 2, 0, half), (-(lanes // 2), half, pieces - half)]
    return plan


def add_pieces(total, part, first):
    last, part = first + part.shape[0], part.astype(F32)
    if part.shape == total.shape:
        return total + part
    return jnp.concatenate([total[:first], total[first:last] + part, total[last:]], axis=0)


def ring_payload(parts, away, ahead=None, behind=None):
    plan = ring_plan(lax.axis_size("span"), parts[0].shape[0])
    blocks = {far: part for part, (far, _, _) in zip(parts, plan)}
    if ahead is None:
        return blocks[away].astype(BF16), blocks[-away].astype(BF16)
    ahead = add_pieces(blocks[away], ahead, 0)
    return ahead.astype(BF16), add_pieces(blocks[-away], behind, plan[-1][1]).astype(BF16)


def ring_total(parts, ahead, behind):
    plan = ring_plan(lax.axis_size("span"), parts[0].shape[0])
    return add_pieces(add_pieces(parts[0], ahead, 0), behind, plan[-1][1]).astype(BF16)


def shift_two(x, y, by):
    both = shift_span(jnp.concatenate([x, y], axis=0), by)
    return both[: x.shape[0]], both[x.shape[0] :]


def ring_shapes(shape, lanes):
    return [
        jax.ShapeDtypeStruct((count,) + tuple(shape[1:]), F32 if abs(away) < (lanes + 1) // 2 else BF16)
        for away, first, count in ring_plan(lanes, shape[0])
    ]


def one_way_plan(lanes, pieces):
    plan = [entry for entry in ring_plan(lanes, pieces) if entry[2] == pieces]
    return plan + [(lanes // 2, 0, pieces)] * (lanes % 2 == 0)


def gather_span(x, halves):
    lanes = lax.axis_size("span")
    parts, ahead, behind = [x], x, x
    for _ in range(1, (lanes + 1) // 2):
        ahead, behind = shift_span(ahead, 1), shift_span(behind, -1)
        parts += [ahead, behind]
    if lanes % 2 == 0 and halves:
        half = x.shape[0] // 2
        parts += [shift_span(ahead[:half], 1), shift_span(behind[half:], -1)]
    elif lanes % 2 == 0:
        parts.append(shift_span(ahead, 1))
    return parts


def assemble(lanes, plan, lane, parts, out_ref):
    width = parts[0].shape[2]
    block = out_ref.shape[0] // lanes
    for at in range(lanes):

        @pl.when(lane == at)
        def _():
            for part, (behind, first, count) in zip(parts, plan):
                row = ((at - behind) % lanes) * block
                for b in range(count):
                    col = (first + b) * width
                    out_ref[row : row + block, col : col + width] = part[b, :block].astype(F32)


def emit(lanes, lane, acc_ref, outs):
    width = outs[0].shape[2]
    block = acc_ref.shape[0] // lanes
    plan = ring_plan(lanes, outs[0].shape[0])
    for at in range(lanes):

        @pl.when(lane == at)
        def _():
            for out, (away, first, count) in zip(outs, plan):
                row = ((at + away) % lanes) * block
                for b in range(count):
                    col = (first + b) * width
                    out[b, :block] = acc_ref[row : row + block, col : col + width].astype(out.dtype)


def main_kernel(
    steps, lanes, packed, meta_ref, tid_ref, rid_ref, rel_ref, edge_ref, parts_ref, *refs
):
    grad_ref, rel_out_ref = refs[:2]
    outs = refs[2:-4]
    table_ref, acc_ref, hot_ref, coef_ref = refs[-4:]
    step = pl.program_id(0)

    @pl.when(step == 0)
    def _():
        pieces, _, width = parts_ref.shape
        for b in range(pieces):
            table_ref[:, b * width : (b + 1) * width] = parts_ref[b]
        acc_ref[...] = jnp.zeros_like(acc_ref)
        rel_out_ref[...] = jnp.zeros_like(rel_out_ref)

    live = is_live(meta_ref, step, steps, tid_ref.shape[2])

    @pl.when(jnp.logical_not(live))
    def _():
        grad_ref[...] = jnp.zeros_like(grad_ref)

    @pl.when(live)
    def _():
        ids = live_ids(tid_ref[0], meta_ref, step, steps)
        hot_ref[...] = one_hot(ids, table_ref.shape[1])
        tail = dot_nn(table_ref[...], hot_ref[...]).astype(BF16)
        scores = dot_tn(edge_ref[0, 0], tail)
        sig = 0.5 * jnp.tanh(0.5 * scores) + 0.5
        diagonal = lax.broadcasted_iota(jnp.int32, scores.shape, 0) == lax.broadcasted_iota(
            jnp.int32, scores.shape, 1
        )
        coef_ref[...] = jnp.where(diagonal, sig - 1.0, NEG_WEIGHT * sig).astype(BF16)
        grad_tail = dot_nn(edge_ref[0, 0], coef_ref[...])
        acc_ref[...] += dot_nt(grad_tail.astype(BF16), hot_ref[...])

        kinds = live_ids(rid_ref[0], meta_ref, step, steps)
        kind = kind_hot(kinds, rel_ref.shape[0])
        rel = relation_columns(rel_ref, kind)
        head = edge_ref[0, 1].astype(F32)
        half = head.shape[0] // 2
        h_re, h_im, r_re, r_im = head[:half], head[half:], rel[:half], rel[half:]
        grad_query = dot_nt(tail, coef_ref[...])
        g_re, g_im = grad_query[:half], grad_query[half:]
        grad_head = jnp.concatenate([g_re * r_re + g_im * r_im, g_im * r_re - g_re * r_im], axis=0)
        grad_ref[0] = grad_head.astype(BF16)
        grad_rel = jnp.concatenate([g_re * h_re + g_im * h_im, g_im * h_re - g_re * h_im], axis=0)
        rel_out_ref[...] += dot_nt(grad_rel.astype(BF16), kind.astype(BF16))

    @pl.when(step == steps - 1)
    def _():
        emit(lanes, meta_ref[1], acc_ref, outs)
        if packed:
            rel_rows = rel_out_ref[...].T
            block = rel_rows.shape[1] // lanes
            each = rel_rows.shape[0] // outs[0].shape[0]
            plan = ring_plan(lanes, outs[0].shape[0])
            for at in range(lanes):

                @pl.when(meta_ref[1] == at)
                def _():
                    for out, (away, first, count) in zip(outs, plan):
                        col = ((at + away) % lanes) * block
                        for b in range(count):
                            row = (first + b) * each
                            out[b, block:, :block] = rel_rows[
                                row : row + each, col : col + block
                            ].astype(out.dtype)


def source_kernel(lanes, meta_ref, hid_ref, grad_ref, *refs):
    outs, acc_ref = refs[:-1], refs[-1]
    steps, rows = grad_ref.shape[0], acc_ref.shape[1]
    part = 256 if rows % 256 == 0 else rows
    ids = [live_ids(hid_ref[step], meta_ref, step, steps) for step in range(steps)]
    for first in range(0, rows, part):
        total = 0.0
        for step in range(steps):
            total += dot_nt(grad_ref[step], one_hot(ids[step] - first, part))
        acc_ref[:, first : first + part] = total
    emit(lanes, meta_ref[1], acc_ref, outs)
    block = acc_ref.shape[0] // lanes
    for out in outs:
        if out.shape[1] > block:
            out[:, block:] = jnp.zeros((out.shape[0], out.shape[1] - block, out.shape[2]), out.dtype)


def pick_kernel(plan_ref, in_ref, out_ref):
    for b in range(in_ref.shape[0]):
        out_ref[b] = in_ref[plan_ref[b]]


def place_kernel(block, plan_ref, in_ref, out_ref):
    for b in range(in_ref.shape[0]):
        out_ref[plan_ref[b]] = in_ref[b]
    if in_ref.shape[1] > block:
        total = jnp.sum(in_ref[:, block:].astype(F32), axis=0).astype(BF16)
        for b in range(in_ref.shape[0]):
            out_ref[b, block:] = total


def adagrad(table, state, grad, axis):
    mean = jnp.sum(grad * grad, axis=axis, keepdims=True) / grad.shape[axis]
    return table - grad * (LEARN_RATE / jnp.sqrt(state + mean))


def update_kernel(lanes, joined, meta_ref, *refs):
    plan_of = one_way_plan if joined else ring_plan
    count = len(plan_of(lanes, 2))
    if joined:
        table_ref, state_ref, rel_ref, rel_state_ref = refs[:4]
        parts, refs = refs[4 : 4 + count], refs[4 + count :]
        out_any, rel_out_ref, rel_grad_ref = refs[:3]
        refs = refs[3:]
    else:
        table_ref, state_ref = refs[:2]
        parts, out_any, refs = refs[2 : 2 + count], refs[2 + count], refs[3 + count :]
    new_ref, grad_ref, store_sems = refs
    features, rows = table_ref.shape
    chunk = 256 if rows % 256 == 0 else rows
    spots = [pl.ds(first, chunk) for first in range(0, rows, chunk)]
    stores = [
        pltpu.make_async_copy(new_ref.at[:, spot], out_any.at[:, spot], store_sems.at[k])
        for k, spot in enumerate(spots)
    ]
    plan = plan_of(lanes, parts[0].shape[0])
    assemble(lanes, plan, meta_ref[1], parts, grad_ref)
    for spot, store in zip(spots, stores):
        new_ref[:, spot] = adagrad(table_ref[:, spot], state_ref[:, spot], grad_ref[:, spot], 0)
        store.start()
    if joined:
        block = features // lanes
        each = parts[0].shape[1] - block
        for at in range(lanes):

            @pl.when(meta_ref[1] == at)
            def _():
                for part, (behind, first, pieces) in zip(parts, plan):
                    col = ((at - behind) % lanes) * block
                    for b in range(pieces):
                        row = (first + b) * each
                        piece = part[b, block:, :block].astype(F32)
                        rel_grad_ref[row : row + each, col : col + block] = piece

        rel_out_ref[...] = adagrad(rel_ref[...], rel_state_ref[...], rel_grad_ref[...], 1)
    for store in stores:
        store.wait()


def whole(shape):
    zeros = (0,) * len(shape)
    return pl.BlockSpec(tuple(shape), lambda i: zeros)


def per_span(shape):
    rest = (0,) * (len(shape) - 1)
    return pl.BlockSpec((1,) + tuple(shape[1:]), lambda i: (i,) + rest)


def shift_span(x, by):
    count = lax.axis_size("span")
    return lax.ppermute(x, "span", [(i, (i + by) % count) for i in range(count)])


def swap_buckets(x):
    return lax.all_to_all(x, "bucket", split_axis=0, concat_axis=0, tiled=True)


def after(x, y):
    return lax.optimization_barrier((x, y))[0]


def update(lanes, meta, table, state, parts, relation=None, relation_state=None):
    joined = relation is not None
    vmem = pl.BlockSpec(memory_space=pltpu.VMEM)
    dma = pltpu.SemaphoreType.DMA
    extra = (relation, relation_state) if joined else ()
    chunks = max(1, table.shape[1] // 256)
    return pl.pallas_call(
        functools.partial(update_kernel, lanes, joined),
        out_shape=[jax.ShapeDtypeStruct(t.shape, F32) for t in (table,) + extra[:1]],
        in_specs=[SMEM_SPEC] + [vmem] * (2 + len(extra) + len(parts)),
        out_specs=[ANY_SPEC] + [vmem] * joined,
        scratch_shapes=[pltpu.VMEM(t.shape, F32) for t in extra[:1]]
        + [pltpu.VMEM(table.shape, F32)] * 2
        + [dma((chunks,))],
        compiler_params=params(24),
    )(meta, table, state, *extra, *parts)


def sum_all(x):
    for axis in ("span", "bucket"):
        count = lax.axis_size(axis)
        if count & (count - 1):
            x = lax.psum(x, axis)
            continue
        bit = 1
        while bit < count:
            x = x + lax.ppermute(x, axis, [(i, i ^ bit) for i in range(count)])
            bit *= 2
    return x


def per_device(
    source_table,
    target_table,
    source_state,
    target_state,
    relation,
    relation_state,
    plan,
    source_index,
    target_index,
    relation_index,
    edge_counts,
):
    buckets = lax.axis_size("bucket")
    lanes = lax.axis_size("span")
    lane = lax.axis_index("span").astype(jnp.int32)
    rows, features = source_table.shape
    steps = source_index.shape[1] // E_CH
    kinds = relation.shape[0]
    block = features // lanes
    width = rows // buckets
    meta = jnp.stack([edge_counts[0], lane])
    hid = source_index.reshape(steps, 1, E_CH)
    tid = target_index.reshape(steps, 1, E_CH)
    rid = relation_index.reshape(steps, 1, E_CH)
    source_cols, target_cols = source_table.T, target_table.T

    owned = target_cols.astype(BF16).reshape(features, buckets, width).transpose(1, 0, 2)
    spread = swap_buckets(owned)
    dma = pltpu.SemaphoreType.DMA
    chosen = pl.pallas_call(
        pick_kernel,
        out_shape=jax.ShapeDtypeStruct(owned.shape, BF16),
        in_specs=[SMEM_SPEC, VMEM_SPEC],
        out_specs=VMEM_SPEC,
        compiler_params=params(8),
    )(plan, spread)
    fetched = swap_buckets(chosen)
    packed = kinds % buckets == 0 and width >= block
    pieces = (buckets, block, width)
    bundles = (buckets, block + kinds // buckets, width) if packed else pieces
    bundle_shape = jax.ShapeDtypeStruct(bundles, BF16)

    edge_shape = (steps, features, E_CH)
    both_shape = (steps, 2) + edge_shape[1:]
    edges = pl.pallas_call(
        functools.partial(prep_kernel, steps),
        grid=(steps,),
        out_shape=jax.ShapeDtypeStruct(both_shape, BF16),
        in_specs=[
            SMEM_SPEC,
            per_span(hid.shape),
            per_span(rid.shape),
            whole(source_cols.shape),
            whole(relation.shape),
        ],
        out_specs=per_span(both_shape),
        scratch_shapes=[pltpu.VMEM((features, rows), BF16)],
        compiler_params=params(56),
        cost_estimate=cost(4 * steps * features * rows * E_CH, 8 * features * steps * E_CH),
    )(meta, hid, rid, source_cols, relation)

    bundle_outs = ring_shapes(bundles, lanes)
    grad_head, rel_part, *target_out = pl.pallas_call(
        functools.partial(main_kernel, steps, lanes, packed),
        grid=(steps,),
        out_shape=[
            jax.ShapeDtypeStruct(edge_shape, BF16),
            jax.ShapeDtypeStruct((features, kinds), F32),
        ]
        + bundle_outs,
        in_specs=[
            SMEM_SPEC,
            per_span(tid.shape),
            per_span(rid.shape),
            whole(relation.shape),
            per_span(both_shape),
            VMEM_SPEC,
        ],
        out_specs=[per_span(edge_shape), whole((features, kinds))]
        + [whole(out.shape) for out in bundle_outs],
        scratch_shapes=[
            pltpu.VMEM((features, rows), BF16),
            pltpu.VMEM((features, rows), F32),
            pltpu.VMEM((rows, E_CH), BF16),
            pltpu.VMEM((E_CH, E_CH), BF16),
        ],
        compiler_params=params(48),
        cost_estimate=cost(12 * steps * features * rows * E_CH, 8 * features * steps * E_CH),
    )(meta, tid, rid, relation, edges, fetched)

    source_out = pl.pallas_call(
        functools.partial(source_kernel, lanes),
        out_shape=bundle_outs,
        in_specs=[SMEM_SPEC, VMEM_SPEC, VMEM_SPEC],
        out_specs=[VMEM_SPEC] * len(bundle_outs),
        scratch_shapes=[pltpu.VMEM((features, rows), F32)],
        compiler_params=params(24),
        cost_estimate=cost(4 * steps * features * rows * E_CH, 8 * features * steps * E_CH),
    )(meta, hid, grad_head)

    reach = lanes // 2
    ahead, behind = ring_payload(target_out, reach)
    for away in range(reach - 1, 0, -1):
        ahead, behind = shift_span(ahead, 1), shift_span(behind, -1)
        ahead, behind = after((ahead, behind), source_out)
        ahead, behind = ring_payload(target_out, away, ahead, behind)
    ahead, behind = shift_span(ahead, 1), shift_span(behind, -1)
    target_sum = ring_total(target_out, ahead, behind)
    returned = swap_buckets(target_sum)
    ahead, behind = ring_payload(source_out, reach)
    for away in range(reach - 1, 0, -1):
        ahead, behind = shift_span(ahead, 1), shift_span(behind, -1)
        ahead, behind = ring_payload(source_out, away, ahead, behind)
    ahead, behind = shift_span(ahead, 1), shift_span(behind, -1)
    source_sum = ring_total(source_out, ahead, behind)
    returned = after(returned, source_sum)
    sorted_out = pl.pallas_call(
        functools.partial(place_kernel, block),
        out_shape=bundle_shape,
        in_specs=[SMEM_SPEC, VMEM_SPEC],
        out_specs=VMEM_SPEC,
        compiler_params=params(8),
    )(plan, returned)
    target_home = swap_buckets(sorted_out)
    source_parts = gather_span(source_sum, True)
    target_home = after(target_home, source_parts[:-1])
    home_parts = gather_span(target_home, not packed)
    (new_source,) = update(lanes, meta, source_cols, source_state.reshape(1, rows), source_parts)
    target_update = (lanes, meta, target_cols, target_state.reshape(1, rows), home_parts)
    if packed:
        relation_update = (relation, relation_state.reshape(kinds, 1))
        new_target, new_relation = update(*target_update, *relation_update)
    else:
        (new_target,) = update(*target_update)
        rel_total = sum_all(rel_part).T
        mean = jnp.mean(rel_total * rel_total, axis=1)
        new_relation = relation - LEARN_RATE * rel_total / jnp.sqrt(relation_state + mean)[:, None]
    return (new_source.T, new_target.T, new_relation)


def solution(mesh):
    placed = (
        P("bucket", None),
        P("bucket", None),
        P("bucket"),
        P("bucket"),
        P(),
        P(),
        P(),
        P("bucket", "span"),
        P("bucket", "span"),
        P("bucket", "span"),
        P("bucket"),
    )
    return jax.shard_map(
        per_device,
        mesh=mesh,
        in_specs=placed,
        out_specs=(P("bucket", None), P("bucket", None), P()),
        check_vma=False,
    )
```

```python
import functools

import jax
import jax.numpy as jnp
from jax import lax
from jax.experimental import pallas as pl
from jax.experimental.pallas import tpu as pltpu
from jax.sharding import PartitionSpec as P

E_CH = 640
LEARN_RATE = 0.25
NEG_WEIGHT = 0.03125

F32 = jnp.float32
BF16 = jnp.bfloat16
MIB = 1024 * 1024
SMEM_SPEC = pl.BlockSpec(memory_space=pltpu.SMEM)


ANY_SPEC = pl.BlockSpec(memory_space=pl.ANY)
VMEM_SPEC = pl.BlockSpec(memory_space=pltpu.VMEM)


def params(mib):
    return pltpu.CompilerParams(vmem_limit_bytes=mib * MIB)


def cost(flops, nbytes):
    return pl.CostEstimate(flops=int(flops), bytes_accessed=int(nbytes), transcendentals=0)


def dot_nn(a, b):
    return lax.dot_general(a, b, (((1,), (0,)), ((), ())), preferred_element_type=F32)


def dot_nt(a, b):
    return lax.dot_general(a, b, (((1,), (1,)), ((), ())), preferred_element_type=F32)


def dot_tn(a, b):
    return lax.dot_general(a, b, (((0,), (0,)), ((), ())), preferred_element_type=F32)


def live_ids(ids, meta_ref, step, steps):
    width = ids.shape[1]
    start = (meta_ref[1] * steps + step) * width
    slots = start + lax.broadcasted_iota(jnp.int32, ids.shape, 1)
    return jnp.where(slots < meta_ref[0], ids, -1)


def is_live(meta_ref, step, steps, width):
    return (meta_ref[1] * steps + step) * width < meta_ref[0]


def one_hot(ids, rows):
    match = lax.broadcasted_iota(jnp.int32, (rows, ids.shape[1]), 0) == ids
    return jnp.where(match, 1.0, 0.0).astype(BF16)


def relation_columns(rel_ref, kind):
    rel = rel_ref[...]
    high = rel.astype(BF16)
    rest = rel - high.astype(F32)
    middle = rest.astype(BF16)
    low = (rest - middle.astype(F32)).astype(BF16)
    parts = jnp.concatenate([high.astype(F32), middle.astype(F32), low.astype(F32)], axis=0)
    hot = jnp.concatenate([kind, kind, kind], axis=0)
    return dot_tn(parts.astype(BF16), hot.astype(BF16))


def kind_hot(ids, count):
    match = lax.broadcasted_iota(jnp.int32, (count, ids.shape[1]), 0) == ids
    return jnp.where(match, 1.0, 0.0)


def prep_kernel(steps, meta_ref, hid_ref, rid_ref, src_ref, rel_ref, out_ref, low_ref):
    step = pl.program_id(0)

    @pl.when(step == 0)
    def _():
        low_ref[...] = src_ref[...].astype(BF16)

    @pl.when(is_live(meta_ref, step, steps, hid_ref.shape[2]))
    def _():
        ids = live_ids(hid_ref[0], meta_ref, step, steps)
        kinds = live_ids(rid_ref[0], meta_ref, step, steps)
        head = dot_nn(low_ref[...], one_hot(ids, low_ref.shape[1]))
        rel = relation_columns(rel_ref, kind_hot(kinds, rel_ref.shape[0]))
        half = head.shape[0] // 2
        h_re, h_im, r_re, r_im = head[:half], head[half:], rel[:half], rel[half:]
        query = jnp.concatenate([h_re * r_re - h_im * r_im, h_re * r_im + h_im * r_re], axis=0)
        out_ref[0, 0] = query.astype(BF16)
        out_ref[0, 1] = head.astype(BF16)


def ring_plan(lanes, pieces):
    plan = [(0, 0, pieces)]
    for k in range(1, (lanes + 1) // 2):
        plan += [(k, 0, pieces), (-k, 0, pieces)]
    if lanes % 2 == 0:
        half = pieces // 2
        plan += [(lanes // 2, 0, half), (-(lanes // 2), half, pieces - half)]
    return plan


def add_pieces(total, part, first):
    last, part = first + part.shape[0], part.astype(F32)
    if part.shape == total.shape:
        return total + part
    return jnp.concatenate([total[:first], total[first:last] + part, total[last:]], axis=0)


def ring_payload(parts, away, ahead=None, behind=None):
    plan = ring_plan(lax.axis_size("span"), parts[0].shape[0])
    blocks = {far: part for part, (far, _, _) in zip(parts, plan)}
    if ahead is None:
        return blocks[away].astype(BF16), blocks[-away].astype(BF16)
    ahead = add_pieces(blocks[away], ahead, 0)
    return ahead.astype(BF16), add_pieces(blocks[-away], behind, plan[-1][1]).astype(BF16)


def ring_total(parts, ahead, behind):
    plan = ring_plan(lax.axis_size("span"), parts[0].shape[0])
    return add_pieces(add_pieces(parts[0], ahead, 0), behind, plan[-1][1]).astype(BF16)


def shift_two(x, y, by):
    both = shift_span(jnp.concatenate([x, y], axis=0), by)
    return both[: x.shape[0]], both[x.shape[0] :]


def ring_shapes(shape, lanes):
    return [
        jax.ShapeDtypeStruct((count,) + tuple(shape[1:]), F32 if abs(away) < (lanes + 1) // 2 else BF16)
        for away, first, count in ring_plan(lanes, shape[0])
    ]


def one_way_plan(lanes, pieces):
    plan = [entry for entry in ring_plan(lanes, pieces) if entry[2] == pieces]
    return plan + [(lanes // 2, 0, pieces)] * (lanes % 2 == 0)


def gather_span(x, halves):
    lanes = lax.axis_size("span")
    parts, ahead, behind = [x], x, x
    for _ in range(1, (lanes + 1) // 2):
        ahead, behind = shift_span(ahead, 1), shift_span(behind, -1)
        parts += [ahead, behind]
    if lanes % 2 == 0 and halves:
        half = x.shape[0] // 2
        parts += [shift_span(ahead[:half], 1), shift_span(behind[half:], -1)]
    elif lanes % 2 == 0:
        parts.append(shift_span(ahead, 1))
    return parts


def assemble(lanes, plan, lane, parts, out_ref):
    width = parts[0].shape[2]
    block = out_ref.shape[0] // lanes
    for at in range(lanes):

        @pl.when(lane == at)
        def _():
            for part, (behind, first, count) in zip(parts, plan):
                row = ((at - behind) % lanes) * block
                for b in range(count):
                    col = (first + b) * width
                    out_ref[row : row + block, col : col + width] = part[b, :block].astype(F32)


def emit(lanes, lane, acc_ref, outs):
    width = outs[0].shape[2]
    block = acc_ref.shape[0] // lanes
    plan = ring_plan(lanes, outs[0].shape[0])
    for at in range(lanes):

        @pl.when(lane == at)
        def _():
            for out, (away, first, count) in zip(outs, plan):
                row = ((at + away) % lanes) * block
                for b in range(count):
                    col = (first + b) * width
                    out[b, :block] = acc_ref[row : row + block, col : col + width].astype(out.dtype)


def main_kernel(
    steps, lanes, packed, meta_ref, tid_ref, rid_ref, rel_ref, edge_ref, parts_ref, *refs
):
    grad_ref, rel_out_ref = refs[:2]
    outs = refs[2:-4]
    table_ref, acc_ref, hot_ref, coef_ref = refs[-4:]
    step = pl.program_id(0)

    @pl.when(step == 0)
    def _():
        pieces, _, width = parts_ref.shape
        for b in range(pieces):
            table_ref[:, b * width : (b + 1) * width] = parts_ref[b]
        acc_ref[...] = jnp.zeros_like(acc_ref)
        rel_out_ref[...] = jnp.zeros_like(rel_out_ref)

    group = tid_ref.shape[0]
    first = step * group
    last_live = is_live(meta_ref, first + group - 1, steps, tid_ref.shape[2])

    def spans(some):
        for j in some:
            ids = live_ids(tid_ref[j], meta_ref, first + j, steps)
            hot_ref[j] = one_hot(ids, table_ref.shape[1])
        tails = [dot_nn(table_ref[...], hot_ref[j]).astype(BF16) for j in some]
        for j, tail in zip(some, tails):
            scores = dot_tn(edge_ref[j, 0], tail)
            sig = 0.5 * jnp.tanh(0.5 * scores) + 0.5
            diagonal = lax.broadcasted_iota(jnp.int32, scores.shape, 0) == lax.broadcasted_iota(
                jnp.int32, scores.shape, 1
            )
            coef_ref[j] = jnp.where(diagonal, sig - 1.0, NEG_WEIGHT * sig).astype(BF16)
        for j, tail in zip(some, tails):
            kinds = live_ids(rid_ref[j], meta_ref, first + j, steps)
            kind = kind_hot(kinds, rel_ref.shape[0])
            rel = relation_columns(rel_ref, kind)
            head = edge_ref[j, 1].astype(F32)
            half = head.shape[0] // 2
            h_re, h_im, r_re, r_im = head[:half], head[half:], rel[:half], rel[half:]
            grad_query = dot_nt(tail, coef_ref[j])
            g_re, g_im = grad_query[:half], grad_query[half:]
            grad_head = [g_re * r_re + g_im * r_im, g_im * r_re - g_re * r_im]
            grad_ref[j] = jnp.concatenate(grad_head, axis=0).astype(BF16)
            grad_rel = [g_re * h_re + g_im * h_im, g_im * h_re - g_re * h_im]
            grad_rel = jnp.concatenate(grad_rel, axis=0).astype(BF16)
            rel_out_ref[...] += dot_nt(grad_rel, kind.astype(BF16))
        total = acc_ref[...]
        for j in some:
            grad_tail = dot_nn(edge_ref[j, 0], coef_ref[j])
            total += dot_nt(grad_tail.astype(BF16), hot_ref[j])
        acc_ref[...] = total

    @pl.when(last_live)
    def _():
        spans(range(group))

    for j in range(group - 1):

        @pl.when(jnp.logical_not(last_live))
        def _():
            live = is_live(meta_ref, first + j, steps, tid_ref.shape[2])

            @pl.when(live)
            def _():
                spans([j])

            @pl.when(jnp.logical_not(live))
            def _():
                grad_ref[j] = jnp.zeros(grad_ref.shape[1:], BF16)

    @pl.when(jnp.logical_not(last_live))
    def _():
        grad_ref[group - 1] = jnp.zeros(grad_ref.shape[1:], BF16)

    @pl.when(step == pl.num_programs(0) - 1)
    def _():
        emit(lanes, meta_ref[1], acc_ref, outs)
        if packed:
            rel_rows = rel_out_ref[...].T
            block = rel_rows.shape[1] // lanes
            each = rel_rows.shape[0] // outs[0].shape[0]
            plan = ring_plan(lanes, outs[0].shape[0])
            for at in range(lanes):

                @pl.when(meta_ref[1] == at)
                def _():
                    for out, (away, first, count) in zip(outs, plan):
                        col = ((at + away) % lanes) * block
                        for b in range(count):
                            row = (first + b) * each
                            out[b, block:, :block] = rel_rows[
                                row : row + each, col : col + block
                            ].astype(out.dtype)


def source_kernel(lanes, meta_ref, hid_ref, grad_ref, *refs):
    outs, acc_ref = refs[:-1], refs[-1]
    steps, rows = grad_ref.shape[0], acc_ref.shape[1]
    part = 256 if rows % 256 == 0 else rows
    ids = [live_ids(hid_ref[step], meta_ref, step, steps) for step in range(steps)]
    for first in range(0, rows, part):
        total = 0.0
        for step in range(steps):
            total += dot_nt(grad_ref[step], one_hot(ids[step] - first, part))
        acc_ref[:, first : first + part] = total
    emit(lanes, meta_ref[1], acc_ref, outs)
    block = acc_ref.shape[0] // lanes
    for out in outs:
        if out.shape[1] > block:
            out[:, block:] = jnp.zeros((out.shape[0], out.shape[1] - block, out.shape[2]), out.dtype)


def pick_kernel(plan_ref, in_ref, out_ref):
    for b in range(in_ref.shape[0]):
        out_ref[b] = in_ref[plan_ref[b]]


def place_kernel(block, plan_ref, in_ref, out_ref):
    for b in range(in_ref.shape[0]):
        out_ref[plan_ref[b]] = in_ref[b]
    if in_ref.shape[1] > block:
        total = jnp.sum(in_ref[:, block:].astype(F32), axis=0).astype(BF16)
        for b in range(in_ref.shape[0]):
            out_ref[b, block:] = total


def adagrad(table, state, grad, axis):
    mean = jnp.sum(grad * grad, axis=axis, keepdims=True) / grad.shape[axis]
    return table - grad * (LEARN_RATE / jnp.sqrt(state + mean))


def update_kernel(lanes, joined, meta_ref, *refs):
    plan_of = one_way_plan if joined else ring_plan
    count = len(plan_of(lanes, 2))
    if joined:
        table_ref, state_ref, rel_ref, rel_state_ref = refs[:4]
        parts, refs = refs[4 : 4 + count], refs[4 + count :]
        out_any, rel_out_ref, rel_grad_ref = refs[:3]
        refs = refs[3:]
    else:
        table_ref, state_ref = refs[:2]
        parts, out_any, refs = refs[2 : 2 + count], refs[2 + count], refs[3 + count :]
    new_ref, grad_ref, store_sems = refs
    features, rows = table_ref.shape
    chunk = 256 if rows % 256 == 0 else rows
    spots = [pl.ds(first, chunk) for first in range(0, rows, chunk)]
    stores = [
        pltpu.make_async_copy(new_ref.at[:, spot], out_any.at[:, spot], store_sems.at[k])
        for k, spot in enumerate(spots)
    ]
    plan = plan_of(lanes, parts[0].shape[0])
    assemble(lanes, plan, meta_ref[1], parts, grad_ref)
    for spot, store in zip(spots, stores):
        new_ref[:, spot] = adagrad(table_ref[:, spot], state_ref[:, spot], grad_ref[:, spot], 0)
        store.start()
    if joined:
        block = features // lanes
        each = parts[0].shape[1] - block
        for at in range(lanes):

            @pl.when(meta_ref[1] == at)
            def _():
                for part, (behind, first, pieces) in zip(parts, plan):
                    col = ((at - behind) % lanes) * block
                    for b in range(pieces):
                        row = (first + b) * each
                        piece = part[b, block:, :block].astype(F32)
                        rel_grad_ref[row : row + each, col : col + block] = piece

        rel_out_ref[...] = adagrad(rel_ref[...], rel_state_ref[...], rel_grad_ref[...], 1)
    for store in stores:
        store.wait()


def whole(shape):
    zeros = (0,) * len(shape)
    return pl.BlockSpec(tuple(shape), lambda i: zeros)


def per_span(shape, group=1):
    rest = (0,) * (len(shape) - 1)
    return pl.BlockSpec((group,) + tuple(shape[1:]), lambda i: (i,) + rest)


def shift_span(x, by):
    count = lax.axis_size("span")
    return lax.ppermute(x, "span", [(i, (i + by) % count) for i in range(count)])


def swap_buckets(x):
    return lax.all_to_all(x, "bucket", split_axis=0, concat_axis=0, tiled=True)


def after(x, y):
    return lax.optimization_barrier((x, y))[0]


def update(lanes, meta, table, state, parts, relation=None, relation_state=None):
    joined = relation is not None
    vmem = pl.BlockSpec(memory_space=pltpu.VMEM)
    dma = pltpu.SemaphoreType.DMA
    extra = (relation, relation_state) if joined else ()
    chunks = max(1, table.shape[1] // 256)
    return pl.pallas_call(
        functools.partial(update_kernel, lanes, joined),
        out_shape=[jax.ShapeDtypeStruct(t.shape, F32) for t in (table,) + extra[:1]],
        in_specs=[SMEM_SPEC] + [vmem] * (2 + len(extra) + len(parts)),
        out_specs=[ANY_SPEC] + [vmem] * joined,
        scratch_shapes=[pltpu.VMEM(t.shape, F32) for t in extra[:1]]
        + [pltpu.VMEM(table.shape, F32)] * 2
        + [dma((chunks,))],
        compiler_params=params(24),
    )(meta, table, state, *extra, *parts)


def sum_all(x):
    for axis in ("span", "bucket"):
        count = lax.axis_size(axis)
        if count & (count - 1):
            x = lax.psum(x, axis)
            continue
        bit = 1
        while bit < count:
            x = x + lax.ppermute(x, axis, [(i, i ^ bit) for i in range(count)])
            bit *= 2
    return x


def per_device(
    source_table,
    target_table,
    source_state,
    target_state,
    relation,
    relation_state,
    plan,
    source_index,
    target_index,
    relation_index,
    edge_counts,
):
    buckets = lax.axis_size("bucket")
    lanes = lax.axis_size("span")
    lane = lax.axis_index("span").astype(jnp.int32)
    rows, features = source_table.shape
    steps = source_index.shape[1] // E_CH
    kinds = relation.shape[0]
    block = features // lanes
    width = rows // buckets
    meta = jnp.stack([edge_counts[0], lane])
    hid = source_index.reshape(steps, 1, E_CH)
    tid = target_index.reshape(steps, 1, E_CH)
    rid = relation_index.reshape(steps, 1, E_CH)
    source_cols, target_cols = source_table.T, target_table.T

    owned = target_cols.astype(BF16).reshape(features, buckets, width).transpose(1, 0, 2)
    spread = swap_buckets(owned)
    dma = pltpu.SemaphoreType.DMA
    chosen = pl.pallas_call(
        pick_kernel,
        out_shape=jax.ShapeDtypeStruct(owned.shape, BF16),
        in_specs=[SMEM_SPEC, VMEM_SPEC],
        out_specs=VMEM_SPEC,
        compiler_params=params(8),
    )(plan, spread)
    fetched = swap_buckets(chosen)
    packed = kinds % buckets == 0 and width >= block
    pieces = (buckets, block, width)
    bundles = (buckets, block + kinds // buckets, width) if packed else pieces
    bundle_shape = jax.ShapeDtypeStruct(bundles, BF16)

    edge_shape = (steps, features, E_CH)
    both_shape = (steps, 2) + edge_shape[1:]
    edges = pl.pallas_call(
        functools.partial(prep_kernel, steps),
        grid=(steps,),
        out_shape=jax.ShapeDtypeStruct(both_shape, BF16),
        in_specs=[
            SMEM_SPEC,
            per_span(hid.shape),
            per_span(rid.shape),
            whole(source_cols.shape),
            whole(relation.shape),
        ],
        out_specs=per_span(both_shape),
        scratch_shapes=[pltpu.VMEM((features, rows), BF16)],
        compiler_params=params(56),
        cost_estimate=cost(4 * steps * features * rows * E_CH, 8 * features * steps * E_CH),
    )(meta, hid, rid, source_cols, relation)

    bundle_outs = ring_shapes(bundles, lanes)
    group = 2 if steps % 2 == 0 else 1
    grad_head, rel_part, *target_out = pl.pallas_call(
        functools.partial(main_kernel, steps, lanes, packed),
        grid=(steps // group,),
        out_shape=[
            jax.ShapeDtypeStruct(edge_shape, BF16),
            jax.ShapeDtypeStruct((features, kinds), F32),
        ]
        + bundle_outs,
        in_specs=[
            SMEM_SPEC,
            per_span(tid.shape, group),
            per_span(rid.shape, group),
            whole(relation.shape),
            per_span(both_shape, group),
            VMEM_SPEC,
        ],
        out_specs=[per_span(edge_shape, group), whole((features, kinds))]
        + [whole(out.shape) for out in bundle_outs],
        scratch_shapes=[
            pltpu.VMEM((features, rows), BF16),
            pltpu.VMEM((features, rows), F32),
            pltpu.VMEM((group, rows, E_CH), BF16),
            pltpu.VMEM((group, E_CH, E_CH), BF16),
        ],
        compiler_params=params(48),
        cost_estimate=cost(12 * steps * features * rows * E_CH, 8 * features * steps * E_CH),
    )(meta, tid, rid, relation, edges, fetched)

    source_out = pl.pallas_call(
        functools.partial(source_kernel, lanes),
        out_shape=bundle_outs,
        in_specs=[SMEM_SPEC, VMEM_SPEC, VMEM_SPEC],
        out_specs=[VMEM_SPEC] * len(bundle_outs),
        scratch_shapes=[pltpu.VMEM((features, rows), F32)],
        compiler_params=params(24),
        cost_estimate=cost(4 * steps * features * rows * E_CH, 8 * features * steps * E_CH),
    )(meta, hid, grad_head)

    reach = lanes // 2
    ahead, behind = ring_payload(target_out, reach)
    for away in range(reach - 1, 0, -1):
        ahead, behind = shift_span(ahead, 1), shift_span(behind, -1)
        ahead, behind = after((ahead, behind), source_out)
        ahead, behind = ring_payload(target_out, away, ahead, behind)
    ahead, behind = shift_span(ahead, 1), shift_span(behind, -1)
    target_sum = ring_total(target_out, ahead, behind)
    returned = swap_buckets(target_sum)
    ahead, behind = ring_payload(source_out, reach)
    for away in range(reach - 1, 0, -1):
        ahead, behind = shift_span(ahead, 1), shift_span(behind, -1)
        ahead, behind = ring_payload(source_out, away, ahead, behind)
    ahead, behind = shift_span(ahead, 1), shift_span(behind, -1)
    source_sum = ring_total(source_out, ahead, behind)
    returned = after(returned, source_sum)
    sorted_out = pl.pallas_call(
        functools.partial(place_kernel, block),
        out_shape=bundle_shape,
        in_specs=[SMEM_SPEC, VMEM_SPEC],
        out_specs=VMEM_SPEC,
        compiler_params=params(8),
    )(plan, returned)
    target_home = swap_buckets(sorted_out)
    source_parts = gather_span(source_sum, True)
    target_home = after(target_home, source_parts[:-1])
    home_parts = gather_span(target_home, not packed)
    (new_source,) = update(lanes, meta, source_cols, source_state.reshape(1, rows), source_parts)
    target_update = (lanes, meta, target_cols, target_state.reshape(1, rows), home_parts)
    if packed:
        relation_update = (relation, relation_state.reshape(kinds, 1))
        new_target, new_relation = update(*target_update, *relation_update)
    else:
        (new_target,) = update(*target_update)
        rel_total = sum_all(rel_part).T
        mean = jnp.mean(rel_total * rel_total, axis=1)
        new_relation = relation - LEARN_RATE * rel_total / jnp.sqrt(relation_state + mean)[:, None]
    return (new_source.T, new_target.T, new_relation)


def solution(mesh):
    placed = (
        P("bucket", None),
        P("bucket", None),
        P("bucket"),
        P("bucket"),
        P(),
        P(),
        P(),
        P("bucket", "span"),
        P("bucket", "span"),
        P("bucket", "span"),
        P("bucket"),
    )
    return jax.shard_map(
        per_device,
        mesh=mesh,
        in_specs=placed,
        out_specs=(P("bucket", None), P("bucket", None), P()),
        check_vma=False,
    )
```

```python
import functools

import jax
import jax.numpy as jnp
from jax import lax
from jax.experimental import pallas as pl
from jax.experimental.pallas import tpu as pltpu
from jax.sharding import PartitionSpec as P

E_CH = 640
LEARN_RATE = 0.25
NEG_WEIGHT = 0.03125

F32 = jnp.float32
BF16 = jnp.bfloat16
MIB = 1024 * 1024
SMEM_SPEC = pl.BlockSpec(memory_space=pltpu.SMEM)


ANY_SPEC = pl.BlockSpec(memory_space=pl.ANY)
VMEM_SPEC = pl.BlockSpec(memory_space=pltpu.VMEM)


def params(mib):
    return pltpu.CompilerParams(vmem_limit_bytes=mib * MIB)


def cost(flops, nbytes):
    return pl.CostEstimate(flops=int(flops), bytes_accessed=int(nbytes), transcendentals=0)


def dot_nn(a, b):
    return lax.dot_general(a, b, (((1,), (0,)), ((), ())), preferred_element_type=F32)


def dot_nt(a, b):
    return lax.dot_general(a, b, (((1,), (1,)), ((), ())), preferred_element_type=F32)


def dot_tn(a, b):
    return lax.dot_general(a, b, (((0,), (0,)), ((), ())), preferred_element_type=F32)


def live_ids(ids, meta_ref, step, steps):
    width = ids.shape[1]
    start = (meta_ref[1] * steps + step) * width
    slots = start + lax.broadcasted_iota(jnp.int32, ids.shape, 1)
    return jnp.where(slots < meta_ref[0], ids, -1)


def is_live(meta_ref, step, steps, width):
    return (meta_ref[1] * steps + step) * width < meta_ref[0]


def one_hot(ids, rows):
    match = lax.broadcasted_iota(jnp.int32, (rows, ids.shape[1]), 0) == ids
    return jnp.where(match, 1.0, 0.0).astype(BF16)


def relation_columns(rel_ref, kind):
    rel = rel_ref[...]
    high = rel.astype(BF16)
    rest = rel - high.astype(F32)
    middle = rest.astype(BF16)
    low = (rest - middle.astype(F32)).astype(BF16)
    parts = jnp.concatenate([high.astype(F32), middle.astype(F32), low.astype(F32)], axis=0)
    hot = jnp.concatenate([kind, kind, kind], axis=0)
    return dot_tn(parts.astype(BF16), hot.astype(BF16))


def kind_hot(ids, count):
    match = lax.broadcasted_iota(jnp.int32, (count, ids.shape[1]), 0) == ids
    return jnp.where(match, 1.0, 0.0)


def prep_kernel(steps, meta_ref, hid_ref, rid_ref, src_ref, rel_ref, out_ref, low_ref):
    step = pl.program_id(0)

    @pl.when(step == 0)
    def _():
        low_ref[...] = src_ref[...].astype(BF16)

    @pl.when(is_live(meta_ref, step, steps, hid_ref.shape[2]))
    def _():
        ids = live_ids(hid_ref[0], meta_ref, step, steps)
        kinds = live_ids(rid_ref[0], meta_ref, step, steps)
        head = dot_nn(low_ref[...], one_hot(ids, low_ref.shape[1]))
        rel = relation_columns(rel_ref, kind_hot(kinds, rel_ref.shape[0]))
        half = head.shape[0] // 2
        h_re, h_im, r_re, r_im = head[:half], head[half:], rel[:half], rel[half:]
        query = jnp.concatenate([h_re * r_re - h_im * r_im, h_re * r_im + h_im * r_re], axis=0)
        out_ref[0, 0] = query.astype(BF16)
        out_ref[0, 1] = head.astype(BF16)


def ring_plan(lanes, pieces):
    plan = [(0, 0, pieces)]
    for k in range(1, (lanes + 1) // 2):
        plan += [(k, 0, pieces), (-k, 0, pieces)]
    if lanes % 2 == 0:
        half = pieces // 2
        plan += [(lanes // 2, 0, half), (-(lanes // 2), half, pieces - half)]
    return plan


def add_pieces(total, part, first):
    last, part = first + part.shape[0], part.astype(F32)
    if part.shape == total.shape:
        return total + part
    return jnp.concatenate([total[:first], total[first:last] + part, total[last:]], axis=0)


def ring_payload(parts, away, ahead=None, behind=None):
    plan = ring_plan(lax.axis_size("span"), parts[0].shape[0])
    blocks = {far: part for part, (far, _, _) in zip(parts, plan)}
    if ahead is None:
        return blocks[away].astype(BF16), blocks[-away].astype(BF16)
    ahead = add_pieces(blocks[away], ahead, 0)
    return ahead.astype(BF16), add_pieces(blocks[-away], behind, plan[-1][1]).astype(BF16)


def ring_total(parts, ahead, behind):
    plan = ring_plan(lax.axis_size("span"), parts[0].shape[0])
    return add_pieces(add_pieces(parts[0], ahead, 0), behind, plan[-1][1]).astype(BF16)


def shift_two(x, y, by):
    both = shift_span(jnp.concatenate([x, y], axis=0), by)
    return both[: x.shape[0]], both[x.shape[0] :]


def ring_shapes(shape, lanes):
    return [
        jax.ShapeDtypeStruct((count,) + tuple(shape[1:]), F32 if abs(away) < (lanes + 1) // 2 else BF16)
        for away, first, count in ring_plan(lanes, shape[0])
    ]


def one_way_plan(lanes, pieces):
    plan = [entry for entry in ring_plan(lanes, pieces) if entry[2] == pieces]
    return plan + [(lanes // 2, 0, pieces)] * (lanes % 2 == 0)


def gather_span(x, halves):
    lanes = lax.axis_size("span")
    parts, ahead, behind = [x], x, x
    for _ in range(1, (lanes + 1) // 2):
        ahead, behind = shift_span(ahead, 1), shift_span(behind, -1)
        parts += [ahead, behind]
    if lanes % 2 == 0 and halves:
        half = x.shape[0] // 2
        parts += [shift_span(ahead[:half], 1), shift_span(behind[half:], -1)]
    elif lanes % 2 == 0:
        parts.append(shift_span(ahead, 1))
    return parts


def assemble(lanes, plan, lane, parts, out_ref):
    width = parts[0].shape[2]
    block = out_ref.shape[0] // lanes
    for at in range(lanes):

        @pl.when(lane == at)
        def _():
            for part, (behind, first, count) in zip(parts, plan):
                row = ((at - behind) % lanes) * block
                for b in range(count):
                    col = (first + b) * width
                    out_ref[row : row + block, col : col + width] = part[b, :block].astype(F32)


def emit(lanes, lane, acc_ref, outs):
    width = outs[0].shape[2]
    block = acc_ref.shape[0] // lanes
    plan = ring_plan(lanes, outs[0].shape[0])
    for at in range(lanes):

        @pl.when(lane == at)
        def _():
            for out, (away, first, count) in zip(outs, plan):
                row = ((at + away) % lanes) * block
                for b in range(count):
                    col = (first + b) * width
                    out[b, :block] = acc_ref[row : row + block, col : col + width].astype(out.dtype)


def main_kernel(
    steps, lanes, packed, meta_ref, tid_ref, rid_ref, rel_ref, edge_ref, parts_ref, *refs
):
    grad_ref, rel_out_ref = refs[:2]
    outs = refs[2:-4]
    table_ref, acc_ref, hot_ref, coef_ref = refs[-4:]
    step = pl.program_id(0)

    @pl.when(step == 0)
    def _():
        pieces, _, width = parts_ref.shape
        for b in range(pieces):
            table_ref[:, b * width : (b + 1) * width] = parts_ref[b]
        acc_ref[...] = jnp.zeros_like(acc_ref)
        rel_out_ref[...] = jnp.zeros_like(rel_out_ref)

    group = tid_ref.shape[0]
    first = step * group
    last_live = is_live(meta_ref, first + group - 1, steps, tid_ref.shape[2])

    def spans(some):
        for j in some:
            ids = live_ids(tid_ref[j], meta_ref, first + j, steps)
            hot_ref[:, j * E_CH : (j + 1) * E_CH] = one_hot(ids, table_ref.shape[1])
        here = slice(some[0] * E_CH, (some[-1] + 1) * E_CH)
        gathered = dot_nn(table_ref[...], hot_ref[:, here]).astype(BF16)
        tails = [gathered[:, k * E_CH : (k + 1) * E_CH] for k in range(len(some))]
        for j, tail in zip(some, tails):
            scores = dot_tn(edge_ref[j, 0], tail)
            sig = 0.5 * jnp.tanh(0.5 * scores) + 0.5
            diagonal = lax.broadcasted_iota(jnp.int32, scores.shape, 0) == lax.broadcasted_iota(
                jnp.int32, scores.shape, 1
            )
            coef_ref[j] = jnp.where(diagonal, sig - 1.0, NEG_WEIGHT * sig).astype(BF16)
        for j, tail in zip(some, tails):
            kinds = live_ids(rid_ref[j], meta_ref, first + j, steps)
            kind = kind_hot(kinds, rel_ref.shape[0])
            rel = relation_columns(rel_ref, kind)
            head = edge_ref[j, 1].astype(F32)
            half = head.shape[0] // 2
            h_re, h_im, r_re, r_im = head[:half], head[half:], rel[:half], rel[half:]
            grad_query = dot_nt(tail, coef_ref[j])
            g_re, g_im = grad_query[:half], grad_query[half:]
            grad_head = [g_re * r_re + g_im * r_im, g_im * r_re - g_re * r_im]
            grad_ref[j] = jnp.concatenate(grad_head, axis=0).astype(BF16)
            grad_rel = [g_re * h_re + g_im * h_im, g_im * h_re - g_re * h_im]
            grad_rel = jnp.concatenate(grad_rel, axis=0).astype(BF16)
            rel_out_ref[...] += dot_nt(grad_rel, kind.astype(BF16))
        grad_tails = [dot_nn(edge_ref[j, 0], coef_ref[j]).astype(BF16) for j in some]
        acc_ref[...] += dot_nt(jnp.concatenate(grad_tails, axis=1), hot_ref[:, here])

    @pl.when(last_live)
    def _():
        spans(range(group))

    for j in range(group - 1):

        @pl.when(jnp.logical_not(last_live))
        def _():
            live = is_live(meta_ref, first + j, steps, tid_ref.shape[2])

            @pl.when(live)
            def _():
                spans([j])

            @pl.when(jnp.logical_not(live))
            def _():
                grad_ref[j] = jnp.zeros(grad_ref.shape[1:], BF16)

    @pl.when(jnp.logical_not(last_live))
    def _():
        grad_ref[group - 1] = jnp.zeros(grad_ref.shape[1:], BF16)

    @pl.when(step == pl.num_programs(0) - 1)
    def _():
        emit(lanes, meta_ref[1], acc_ref, outs)
        if packed:
            rel_rows = rel_out_ref[...].T
            block = rel_rows.shape[1] // lanes
            each = rel_rows.shape[0] // outs[0].shape[0]
            plan = ring_plan(lanes, outs[0].shape[0])
            for at in range(lanes):

                @pl.when(meta_ref[1] == at)
                def _():
                    for out, (away, first, count) in zip(outs, plan):
                        col = ((at + away) % lanes) * block
                        for b in range(count):
                            row = (first + b) * each
                            out[b, block:, :block] = rel_rows[
                                row : row + each, col : col + block
                            ].astype(out.dtype)


def source_kernel(lanes, meta_ref, hid_ref, grad_ref, *refs):
    outs, acc_ref = refs[:-1], refs[-1]
    steps, rows = grad_ref.shape[0], acc_ref.shape[1]
    part = 256 if rows % 256 == 0 else rows
    ids = [live_ids(hid_ref[step], meta_ref, step, steps) for step in range(steps)]
    for first in range(0, rows, part):
        total = 0.0
        for step in range(steps):
            total += dot_nt(grad_ref[step], one_hot(ids[step] - first, part))
        acc_ref[:, first : first + part] = total
    emit(lanes, meta_ref[1], acc_ref, outs)
    block = acc_ref.shape[0] // lanes
    for out in outs:
        if out.shape[1] > block:
            out[:, block:] = jnp.zeros((out.shape[0], out.shape[1] - block, out.shape[2]), out.dtype)


def pick_kernel(plan_ref, in_ref, out_ref):
    for b in range(in_ref.shape[0]):
        out_ref[b] = in_ref[plan_ref[b]]


def place_kernel(block, plan_ref, in_ref, out_ref):
    for b in range(in_ref.shape[0]):
        out_ref[plan_ref[b]] = in_ref[b]
    if in_ref.shape[1] > block:
        total = jnp.sum(in_ref[:, block:].astype(F32), axis=0).astype(BF16)
        for b in range(in_ref.shape[0]):
            out_ref[b, block:] = total


def adagrad(table, state, grad, axis):
    mean = jnp.sum(grad * grad, axis=axis, keepdims=True) / grad.shape[axis]
    return table - grad * (LEARN_RATE / jnp.sqrt(state + mean))


def update_kernel(lanes, joined, meta_ref, *refs):
    plan_of = one_way_plan if joined else ring_plan
    count = len(plan_of(lanes, 2))
    if joined:
        table_ref, state_ref, rel_ref, rel_state_ref = refs[:4]
        parts, refs = refs[4 : 4 + count], refs[4 + count :]
        out_any, rel_out_ref, rel_grad_ref = refs[:3]
        refs = refs[3:]
    else:
        table_ref, state_ref = refs[:2]
        parts, out_any, refs = refs[2 : 2 + count], refs[2 + count], refs[3 + count :]
    new_ref, grad_ref, store_sems = refs
    features, rows = table_ref.shape
    chunk = 256 if rows % 256 == 0 else rows
    spots = [pl.ds(first, chunk) for first in range(0, rows, chunk)]
    stores = [
        pltpu.make_async_copy(new_ref.at[:, spot], out_any.at[:, spot], store_sems.at[k])
        for k, spot in enumerate(spots)
    ]
    plan = plan_of(lanes, parts[0].shape[0])
    assemble(lanes, plan, meta_ref[1], parts, grad_ref)
    for spot, store in zip(spots, stores):
        new_ref[:, spot] = adagrad(table_ref[:, spot], state_ref[:, spot], grad_ref[:, spot], 0)
        store.start()
    if joined:
        block = features // lanes
        each = parts[0].shape[1] - block
        for at in range(lanes):

            @pl.when(meta_ref[1] == at)
            def _():
                for part, (behind, first, pieces) in zip(parts, plan):
                    col = ((at - behind) % lanes) * block
                    for b in range(pieces):
                        row = (first + b) * each
                        piece = part[b, block:, :block].astype(F32)
                        rel_grad_ref[row : row + each, col : col + block] = piece

        rel_out_ref[...] = adagrad(rel_ref[...], rel_state_ref[...], rel_grad_ref[...], 1)
    for store in stores:
        store.wait()


def whole(shape):
    zeros = (0,) * len(shape)
    return pl.BlockSpec(tuple(shape), lambda i: zeros)


def per_span(shape, group=1):
    rest = (0,) * (len(shape) - 1)
    return pl.BlockSpec((group,) + tuple(shape[1:]), lambda i: (i,) + rest)


def shift_span(x, by):
    count = lax.axis_size("span")
    return lax.ppermute(x, "span", [(i, (i + by) % count) for i in range(count)])


def swap_buckets(x):
    return lax.all_to_all(x, "bucket", split_axis=0, concat_axis=0, tiled=True)


def after(x, y):
    return lax.optimization_barrier((x, y))[0]


def update(lanes, meta, table, state, parts, relation=None, relation_state=None):
    joined = relation is not None
    vmem = pl.BlockSpec(memory_space=pltpu.VMEM)
    dma = pltpu.SemaphoreType.DMA
    extra = (relation, relation_state) if joined else ()
    chunks = max(1, table.shape[1] // 256)
    return pl.pallas_call(
        functools.partial(update_kernel, lanes, joined),
        out_shape=[jax.ShapeDtypeStruct(t.shape, F32) for t in (table,) + extra[:1]],
        in_specs=[SMEM_SPEC] + [vmem] * (2 + len(extra) + len(parts)),
        out_specs=[ANY_SPEC] + [vmem] * joined,
        scratch_shapes=[pltpu.VMEM(t.shape, F32) for t in extra[:1]]
        + [pltpu.VMEM(table.shape, F32)] * 2
        + [dma((chunks,))],
        compiler_params=params(24),
    )(meta, table, state, *extra, *parts)


def sum_all(x):
    for axis in ("span", "bucket"):
        count = lax.axis_size(axis)
        if count & (count - 1):
            x = lax.psum(x, axis)
            continue
        bit = 1
        while bit < count:
            x = x + lax.ppermute(x, axis, [(i, i ^ bit) for i in range(count)])
            bit *= 2
    return x


def per_device(
    source_table,
    target_table,
    source_state,
    target_state,
    relation,
    relation_state,
    plan,
    source_index,
    target_index,
    relation_index,
    edge_counts,
):
    buckets = lax.axis_size("bucket")
    lanes = lax.axis_size("span")
    lane = lax.axis_index("span").astype(jnp.int32)
    rows, features = source_table.shape
    steps = source_index.shape[1] // E_CH
    kinds = relation.shape[0]
    block = features // lanes
    width = rows // buckets
    meta = jnp.stack([edge_counts[0], lane])
    hid = source_index.reshape(steps, 1, E_CH)
    tid = target_index.reshape(steps, 1, E_CH)
    rid = relation_index.reshape(steps, 1, E_CH)
    source_cols, target_cols = source_table.T, target_table.T

    owned = target_cols.astype(BF16).reshape(features, buckets, width).transpose(1, 0, 2)
    spread = swap_buckets(owned)
    dma = pltpu.SemaphoreType.DMA
    chosen = pl.pallas_call(
        pick_kernel,
        out_shape=jax.ShapeDtypeStruct(owned.shape, BF16),
        in_specs=[SMEM_SPEC, VMEM_SPEC],
        out_specs=VMEM_SPEC,
        compiler_params=params(8),
    )(plan, spread)
    fetched = swap_buckets(chosen)
    packed = kinds % buckets == 0 and width >= block
    pieces = (buckets, block, width)
    bundles = (buckets, block + kinds // buckets, width) if packed else pieces
    bundle_shape = jax.ShapeDtypeStruct(bundles, BF16)

    edge_shape = (steps, features, E_CH)
    both_shape = (steps, 2) + edge_shape[1:]
    edges = pl.pallas_call(
        functools.partial(prep_kernel, steps),
        grid=(steps,),
        out_shape=jax.ShapeDtypeStruct(both_shape, BF16),
        in_specs=[
            SMEM_SPEC,
            per_span(hid.shape),
            per_span(rid.shape),
            whole(source_cols.shape),
            whole(relation.shape),
        ],
        out_specs=per_span(both_shape),
        scratch_shapes=[pltpu.VMEM((features, rows), BF16)],
        compiler_params=params(56),
        cost_estimate=cost(4 * steps * features * rows * E_CH, 8 * features * steps * E_CH),
    )(meta, hid, rid, source_cols, relation)

    bundle_outs = ring_shapes(bundles, lanes)
    group = 2 if steps % 2 == 0 else 1
    grad_head, rel_part, *target_out = pl.pallas_call(
        functools.partial(main_kernel, steps, lanes, packed),
        grid=(steps // group,),
        out_shape=[
            jax.ShapeDtypeStruct(edge_shape, BF16),
            jax.ShapeDtypeStruct((features, kinds), F32),
        ]
        + bundle_outs,
        in_specs=[
            SMEM_SPEC,
            per_span(tid.shape, group),
            per_span(rid.shape, group),
            whole(relation.shape),
            per_span(both_shape, group),
            VMEM_SPEC,
        ],
        out_specs=[per_span(edge_shape, group), whole((features, kinds))]
        + [whole(out.shape) for out in bundle_outs],
        scratch_shapes=[
            pltpu.VMEM((features, rows), BF16),
            pltpu.VMEM((features, rows), F32),
            pltpu.VMEM((rows, group * E_CH), BF16),
            pltpu.VMEM((group, E_CH, E_CH), BF16),
        ],
        compiler_params=params(48),
        cost_estimate=cost(12 * steps * features * rows * E_CH, 8 * features * steps * E_CH),
    )(meta, tid, rid, relation, edges, fetched)

    source_out = pl.pallas_call(
        functools.partial(source_kernel, lanes),
        out_shape=bundle_outs,
        in_specs=[SMEM_SPEC, VMEM_SPEC, VMEM_SPEC],
        out_specs=[VMEM_SPEC] * len(bundle_outs),
        scratch_shapes=[pltpu.VMEM((features, rows), F32)],
        compiler_params=params(24),
        cost_estimate=cost(4 * steps * features * rows * E_CH, 8 * features * steps * E_CH),
    )(meta, hid, grad_head)

    reach = lanes // 2
    ahead, behind = ring_payload(target_out, reach)
    for away in range(reach - 1, 0, -1):
        ahead, behind = shift_span(ahead, 1), shift_span(behind, -1)
        ahead, behind = after((ahead, behind), source_out)
        ahead, behind = ring_payload(target_out, away, ahead, behind)
    ahead, behind = shift_span(ahead, 1), shift_span(behind, -1)
    target_sum = ring_total(target_out, ahead, behind)
    returned = swap_buckets(target_sum)
    ahead, behind = ring_payload(source_out, reach)
    for away in range(reach - 1, 0, -1):
        ahead, behind = shift_span(ahead, 1), shift_span(behind, -1)
        ahead, behind = ring_payload(source_out, away, ahead, behind)
    ahead, behind = shift_span(ahead, 1), shift_span(behind, -1)
    source_sum = ring_total(source_out, ahead, behind)
    returned = after(returned, source_sum)
    sorted_out = pl.pallas_call(
        functools.partial(place_kernel, block),
        out_shape=bundle_shape,
        in_specs=[SMEM_SPEC, VMEM_SPEC],
        out_specs=VMEM_SPEC,
        compiler_params=params(8),
    )(plan, returned)
    target_home = swap_buckets(sorted_out)
    source_parts = gather_span(source_sum, True)
    target_home = after(target_home, source_parts[:-1])
    home_parts = gather_span(target_home, not packed)
    (new_source,) = update(lanes, meta, source_cols, source_state.reshape(1, rows), source_parts)
    target_update = (lanes, meta, target_cols, target_state.reshape(1, rows), home_parts)
    if packed:
        relation_update = (relation, relation_state.reshape(kinds, 1))
        new_target, new_relation = update(*target_update, *relation_update)
    else:
        (new_target,) = update(*target_update)
        rel_total = sum_all(rel_part).T
        mean = jnp.mean(rel_total * rel_total, axis=1)
        new_relation = relation - LEARN_RATE * rel_total / jnp.sqrt(relation_state + mean)[:, None]
    return (new_source.T, new_target.T, new_relation)


def solution(mesh):
    placed = (
        P("bucket", None),
        P("bucket", None),
        P("bucket"),
        P("bucket"),
        P(),
        P(),
        P(),
        P("bucket", "span"),
        P("bucket", "span"),
        P("bucket", "span"),
        P("bucket"),
    )
    return jax.shard_map(
        per_device,
        mesh=mesh,
        in_specs=placed,
        out_specs=(P("bucket", None), P("bucket", None), P()),
        check_vma=False,
    )
```
